32 devices in a mesh: dp: 8 (over y, x, core), tensor: 4 (over z).
Axes of the slice: x: 2, y: 2, z: 4, core: 2. Of those that a mesh axis runs over, the one named last changes fastest.
Arguments:
- image_in: bfloat16 [16, 1024, 1536], P('dp', 'tensor'), may hold values from -10 to 10
- text_in: bfloat16 [16, 128, 1536], P('dp', 'tensor'), may hold values from -10 to 10
- condition: bfloat16 [16, 1536], P('dp'), may hold values from -6 to 6
- mod_weight: bfloat16 [2, 1536, 6, 1536], P(None, 'dp', None, 'tensor'), may hold values from -0.15625 to 0.15625
- qkv_weight: bfloat16 [2, 1536, 3, 1536], P(None, 'dp', None, 'tensor'), may hold values from -0.15625 to 0.15625
- proj_weight: bfloat16 [2, 1536, 1536], P(None, 'tensor', 'dp'), may hold values from -1.25 to 1.25
- up_weight: bfloat16 [2, 1536, 6144], P(None, 'dp', 'tensor'), may hold values from -0.15625 to 0.15625
- down_weight: bfloat16 [2, 6144, 1536], P(None, 'tensor', 'dp'), may hold values from -0.078125 to 0.078125
- mod_bias: bfloat16 [2, 6, 1536], replicated, may hold values from -1.796875 to 1.796875
- qkv_bias: bfloat16 [2, 3, 1536], replicated, may hold values from -0.29882812 to 0.29882812
- proj_bias: bfloat16 [2, 1536], replicated, may hold values from -1.1953125 to 1.1953125
- up_bias: bfloat16 [2, 6144], replicated, may hold values from -1.1953125 to 1.1953125
- down_bias: bfloat16 [2, 1536], replicated, may hold values from -1.1953125 to 1.1953125
- image_cot: bfloat16 [16, 1024, 1536], P('dp', 'tensor'), may hold values from -6 to 6
- text_cot: bfloat16 [16, 128, 1536], P('dp', 'tensor'), may hold values from -6 to 6
Outputs:
- image_out: bfloat16 [16, 1024, 1536], P('dp', 'tensor')
- text_out: bfloat16 [16, 128, 1536], P('dp', 'tensor')
- image_grad: float32 [16, 1024, 1536], P('dp', 'tensor')
- text_grad: float32 [16, 128, 1536], P('dp', 'tensor')
- condition_grad: float32 [16, 1536], P('dp')
- mod_weight_grad: float32 [2, 1536, 6, 1536], P(None, 'dp', None, 'tensor')
- qkv_weight_grad: float32 [2, 1536, 3, 1536], P(None, 'dp', None, 'tensor')
- proj_weight_grad: float32 [2, 1536, 1536], P(None, 'tensor', 'dp')
- up_weight_grad: float32 [2, 1536, 6144], P(None, 'dp', 'tensor')
- down_weight_grad: float32 [2, 6144, 1536], P(None, 'tensor', 'dp')
- mod_bias_grad: float32 [2, 6, 1536], replicated
- qkv_bias_grad: float32 [2, 3, 1536], replicated
- proj_bias_grad: float32 [2, 1536], replicated
- up_bias_grad: float32 [2, 6144], replicated
- down_bias_grad: float32 [2, 1536], replicated
- rms_stats: float32 [16, 2, 3], P('dp')
The draws below stay inside these ranges and needn't reach their ends.
All inputs are finite; a program needn't handle non-finite values.
Results may differ from the reference program's by a relative error of at most 0.012.
The reference program's roundings to bfloat16 on the way count: a program that leaves them out, or rounds other values in their place, can miss the bound.
Values may be sent and summed in bfloat16 or wider, within the bound.
A program may use at most 384 MiB of HBM per device.

```python
import jax
import jax.numpy as jnp
from jax import lax

D = 1536
H = 24
HD = 64
FF = 6144
IMG = 1024
TXT = 128
SEQS = 16


def rising_rows(key, sequences, rows, width, low_scale, high_scale):
    place = jnp.arange(rows, dtype=jnp.float32) / max(rows - 1, 1)
    scale_rows = low_scale * jnp.exp(jnp.log(high_scale / low_scale) * place)
    entries = jnp.clip(jax.random.normal(key, (sequences, rows, width), jnp.float32), -4.0, 4.0)
    return entries * scale_rows[None, :, None]


def draw_image_in(key, part):
    key = jax.random.fold_in(key, 11)
    return rising_rows(key, SEQS, IMG, D, 0.5, 2.5).astype(jnp.bfloat16)


def draw_text_in(key, part):
    key = jax.random.fold_in(key, 23)
    return rising_rows(key, SEQS, TXT, D, 0.5, 2.5).astype(jnp.bfloat16)


def steps_of(rng, extent, cuts, smallest, top_value):
    def one(position, parts):
        draws = jax.random.uniform(jax.random.fold_in(jax.random.fold_in(rng, 6), position), (parts,), jnp.float32, smallest / len(cuts), top_value / len(cuts))
        return jnp.repeat(jnp.exp(draws), extent[position] // parts).reshape((-1,) + (1,) * (len(extent) - position - 1))

    gain = one(*cuts[0])
    for cut in cuts[1:]:
        gain = gain * one(*cut)
    return gain


def gaussian(key, dims, scale, bound, split=(), kind=jnp.bfloat16):
    level = steps_of(key, dims, split, -0.22, 0.18) if split else 1.0
    drawn = jax.random.normal(key, dims, jnp.float32) * scale * level
    return jnp.minimum(jnp.maximum(drawn, -bound), bound).astype(kind)


def setup_inputs(seed: int = 0) -> dict:
    keys = jax.random.split(jax.random.key(seed), 16)
    image_in = draw_image_in(jax.random.fold_in(keys[15], 71), 0)
    text_in = draw_text_in(jax.random.fold_in(keys[15], 71), 0)
    condition = gaussian(keys[2], (SEQS, D), 1.0, 6.0, ((0, 8),))
    mod_weight = gaussian(keys[3], (2, D, 6, D), D ** -0.5, 0.15625, ((1, 8), (3, 4)))
    qkv_weight = gaussian(keys[4], (2, D, 3, D), D ** -0.5, 0.15625, ((1, 8), (3, 4)))
    proj_weight = gaussian(keys[5], (2, D, D), (max(D // 64, 1)) ** -0.5, 1.25, ((1, 4), (2, 8)))
    up_weight = gaussian(keys[6], (2, D, FF), D ** -0.5, 0.15625, ((1, 8), (2, 4)))
    down_weight = gaussian(keys[7], (2, FF, D), FF ** -0.5, 0.078125, ((1, 4), (2, 8)))
    mod_bias = gaussian(keys[8], (2, 6, D), 0.3, 1.796875)
    qkv_bias = gaussian(keys[9], (2, 3, D), 0.05, 0.29882812)
    proj_bias = gaussian(keys[10], (2, D), 0.2, 1.1953125)
    up_bias = gaussian(keys[11], (2, FF), 0.2, 1.1953125)
    down_bias = gaussian(keys[12], (2, D), 0.2, 1.1953125)
    image_cot = gaussian(keys[13], (SEQS, IMG, D), 1.0, 6.0, ((0, 8), (1, 4)))
    text_cot = gaussian(keys[14], (SEQS, TXT, D), 1.0, 6.0, ((0, 8), (1, 4)))
    return {"image_in": image_in, "text_in": text_in, "condition": condition, "mod_weight": mod_weight, "qkv_weight": qkv_weight, "proj_weight": proj_weight, "up_weight": up_weight, "down_weight": down_weight, "mod_bias": mod_bias, "qkv_bias": qkv_bias, "proj_bias": proj_bias, "up_bias": up_bias, "down_bias": down_bias, "image_cot": image_cot, "text_cot": text_cot}


@jax.custom_vjp
def low(v):
    return lax.optimization_barrier(v.astype(jnp.bfloat16)).astype(jnp.float32)

@jax.custom_vjp
def low_back(v):
    return v

def low_keep(v):
    return (low(v), None)

def low_pass(kept, grad):
    return (grad,)

def back_keep(v):
    return (v, None)

def back_low(kept, grad):
    return (low(grad),)
low.defvjp(low_keep, low_pass)
low_back.defvjp(back_keep, back_low)
EPSILON = 1e-06
HIGHEST = lax.Precision.HIGHEST

def rounded_both(operand):
    return low_back(low(operand))

def normalize(operand):
    center = operand - lax.optimization_barrier(jnp.mean(operand, axis=-1, keepdims=True))
    return center * lax.rsqrt(lax.optimization_barrier(jnp.mean(center * center, axis=-1, keepdims=True)) + EPSILON)

def root_mean(operand):
    return jnp.sqrt(jnp.mean(operand * operand))

def attention_rows(qkv):
    length = qkv.shape[0]
    queries = qkv[:, 0].reshape(length, H, HD)
    key_rows = qkv[:, 1].reshape(length, H, HD)
    values = qkv[:, 2].reshape(length, H, HD)
    scores = low_back(HD ** (-0.5) * jnp.einsum('qhe,khe->hqk', queries, key_rows, precision=HIGHEST))
    soft_scores = low(jax.nn.softmax(scores, axis=-1))
    attended = jnp.einsum('hqk,khe->qhe', soft_scores, values, precision=HIGHEST)
    return rounded_both(attended.reshape(length, H * HD))

def forward(image_seq, text_seq, cond_seq, mod_weight, qkv_weight, proj_weight, up_weight, down_weight, mod_bias, qkv_bias, proj_bias, up_bias, down_bias):
    silu_cond = low(jax.nn.silu(cond_seq))
    modulation = rounded_both(jnp.einsum('d,sdkf->skf', silu_cond, mod_weight, precision=HIGHEST) + mod_bias)
    residuals = (image_seq, text_seq)
    qkv_parts = []
    for stream in range(2):
        first_hidden = low(normalize(residuals[stream]) * (1.0 + modulation[stream, 1]) + modulation[stream, 0])
        qkv_parts.append(rounded_both(jnp.einsum('td,dkf->tkf', first_hidden, qkv_weight[stream], precision=HIGHEST) + qkv_bias[stream]))
    attended = jax.checkpoint(attention_rows)(jnp.concatenate(qkv_parts, axis=0))
    pieces = (attended[:IMG], attended[IMG:])
    outputs = []
    statistics = []
    for stream in range(2):
        residual = residuals[stream]
        attn_branch = low_back(jnp.dot(pieces[stream], proj_weight[stream], precision=HIGHEST) + proj_bias[stream])
        gated_attn = modulation[stream, 2] * attn_branch
        middle = residual + gated_attn
        second_hidden = low(normalize(middle) * (1.0 + modulation[stream, 4]) + modulation[stream, 3])
        preact = low_back(jnp.dot(second_hidden, up_weight[stream], precision=HIGHEST) + up_bias[stream])
        activated = low(jax.nn.gelu(preact, approximate=True))
        mlp_branch = low_back(jnp.dot(activated, down_weight[stream], precision=HIGHEST) + down_bias[stream])
        gated_mlp = modulation[stream, 5] * mlp_branch
        outputs.append(middle + gated_mlp)
        statistics.append(jnp.stack([root_mean(residual), root_mean(gated_attn), root_mean(gated_mlp)]))
    return ((outputs[0], outputs[1]), jnp.stack(statistics))

def reference(image_in, text_in, condition, mod_weight, qkv_weight, proj_weight, up_weight, down_weight, mod_bias, qkv_bias, proj_bias, up_bias, down_bias, image_cot, text_cot):
    weights = tuple((member.astype(jnp.float32) for member in (mod_weight, qkv_weight, proj_weight, up_weight, down_weight, mod_bias, qkv_bias, proj_bias, up_bias, down_bias)))
    zero_init = tuple((jnp.zeros(member.shape, jnp.float32) for member in weights))

    def one_sequence(running, sequence_items):
        image_seq, text_seq, cond_seq, image_back, text_back = sequence_items
        outputs, pullback, statistics = jax.vjp(forward, image_seq.astype(jnp.float32), text_seq.astype(jnp.float32), cond_seq.astype(jnp.float32), *weights, has_aux=True)
        gradients = pullback((image_back.astype(jnp.float32), text_back.astype(jnp.float32)))
        running = tuple((before + added for before, added in zip(running, gradients[3:])))
        return (running, (outputs[0].astype(jnp.bfloat16), outputs[1].astype(jnp.bfloat16), gradients[0], gradients[1], gradients[2], statistics))
    running, stacked = lax.scan(one_sequence, zero_init, (image_in, text_in, condition, image_cot, text_cot))
    return (stacked[0], stacked[1], stacked[2], stacked[3], stacked[4], running[0], running[1], running[2], running[3], running[4], running[5], running[6], running[7], running[8], running[9], stacked[5])
```

```python
import functools

import jax
import jax.numpy as jnp
from jax import lax
from jax.experimental import pallas as pl
from jax.experimental.pallas import tpu as pltpu
from jax.sharding import PartitionSpec as P

HD = 64
EPSILON = 1e-06
LOG2E = 1.4426950408889634
SCORE = HD ** (-0.5)
VMEM_LIMIT = 56 * 1024 * 1024
BF = jnp.bfloat16
F32 = jnp.float32


def nn(a, b):
    return lax.dot_general(a, b, (((1,), (0,)), ((), ())), preferred_element_type=F32)


def nt(a, b):
    return lax.dot_general(a, b, (((1,), (1,)), ((), ())), preferred_element_type=F32)


def params():
    return pltpu.CompilerParams(vmem_limit_bytes=VMEM_LIMIT)


def resident(shape):
    zeros = (0,) * len(shape)
    return pl.BlockSpec(shape, lambda *_: zeros, pipeline_mode=pl.Buffered(1))


def tile_of(width, most=512):
    for tile in (512, 384, 256, 128):
        if tile <= most and width % tile == 0:
            return tile
    return width


def chunk_of(blocks, rows):
    count = 1
    while count * rows < 512 and blocks % (2 * count) == 0:
        count *= 2
    return count


def up_kernel(image_rows, product, finish, x_ref, w_ref, extra_refs, out_refs):
    blocks, rows, depth = x_ref.shape
    width = out_refs[0].shape[-1]
    step = chunk_of(blocks, image_rows)

    def image(i, carry):
        part = pl.ds(i * step, step)
        x = x_ref[part, :image_rows, :].reshape(step * image_rows, depth)
        results = finish(0, product(x, w_ref[0]), (part, slice(0, image_rows)), extra_refs)
        for ref, value in zip(out_refs, results):
            ref[part, :image_rows, :] = value.reshape(step, image_rows, width).astype(ref.dtype)
        return carry

    lax.fori_loop(0, blocks // step, image, 0)
    text_rows = rows - image_rows
    x = x_ref[:, image_rows:, :].reshape(blocks * text_rows, depth)
    results = finish(1, product(x, w_ref[1]), (slice(None), slice(image_rows, rows)), extra_refs)
    for ref, value in zip(out_refs, results):
        ref[:, image_rows:, :] = value.reshape(blocks, text_rows, width).astype(ref.dtype)


def cost(blocks, rows, depth, width, groups=1):
    return pl.CostEstimate(
        flops=2 * blocks * rows * depth * width * groups,
        bytes_accessed=2 * (blocks * rows * (depth + groups * width) + 2 * groups * depth * width),
        transcendentals=0,
    )


def project_in(x, weight, bias, image_rows):
    blocks, rows, depth = x.shape
    groups, width = weight.shape[0], weight.shape[3]
    tile = tile_of(width)

    def finish(stream, value, place, extra):
        return (value + extra[0][stream],)

    def body(x_ref, w_ref, b_ref, o_ref):
        up_kernel(image_rows, nn, finish, x_ref, w_ref, (b_ref,), (o_ref,))

    return pl.pallas_call(
        body,
        grid=(groups, width // tile),
        in_specs=[
            resident((blocks, rows, depth)),
            pl.BlockSpec((None, 2, depth, tile), lambda g, n: (g, 0, 0, n)),
            pl.BlockSpec((None, 2, 1, tile), lambda g, n: (g, 0, 0, n)),
        ],
        out_specs=pl.BlockSpec((None, blocks, rows, tile), lambda g, n: (g, 0, 0, n)),
        out_shape=jax.ShapeDtypeStruct((groups, blocks, rows, width), BF),
        compiler_params=params(),
        cost_estimate=cost(blocks, rows, depth, width, groups),
        name="project_in",
    )(x, weight, bias)


def mlp_in(x, weight, bias, image_rows):
    blocks, rows, depth = x.shape
    width = weight.shape[2]
    tile = tile_of(width)
    root = 0.7978845608028654

    def finish(stream, value, place, extra):
        v = value + extra[0][stream]
        square = v * v
        t = jnp.tanh(v * (root + (root * 0.044715) * square))
        half = 0.5 + 0.5 * t
        slope = half + v * (0.5 - 0.5 * t * t) * (root + (root * 3.0 * 0.044715) * square)
        return (v * half, slope)

    def body(x_ref, w_ref, b_ref, a_ref, s_ref):
        up_kernel(image_rows, nn, finish, x_ref, w_ref, (b_ref,), (a_ref, s_ref))

    spec = pl.BlockSpec((blocks, rows, tile), lambda n: (0, 0, n))
    shape = jax.ShapeDtypeStruct((blocks, rows, width), BF)
    return pl.pallas_call(
        body,
        grid=(width // tile,),
        in_specs=[
            resident((blocks, rows, depth)),
            pl.BlockSpec((2, depth, tile), lambda n: (0, 0, n)),
            pl.BlockSpec((2, 1, tile), lambda n: (0, 0, n)),
        ],
        out_specs=[spec, spec],
        out_shape=[shape, shape],
        compiler_params=params(),
        cost_estimate=cost(blocks, rows, depth, width),
        name="mlp_in",
    )(x, weight, bias)


def mlp_back(x, weight, slope, image_rows):
    blocks, rows, depth = x.shape
    width = weight.shape[2]
    tile = tile_of(width)

    def finish(stream, value, place, extra):
        factor = extra[0][place[0], place[1], :].astype(F32)
        return (value * factor.reshape(value.shape),)

    def body(x_ref, w_ref, s_ref, o_ref):
        up_kernel(image_rows, nn, finish, x_ref, w_ref, (s_ref,), (o_ref,))

    spec = pl.BlockSpec((blocks, rows, tile), lambda n: (0, 0, n))
    return pl.pallas_call(
        body,
        grid=(width // tile,),
        in_specs=[
            resident((blocks, rows, depth)),
            pl.BlockSpec((2, depth, tile), lambda n: (0, 0, n)),
            spec,
        ],
        out_specs=spec,
        out_shape=jax.ShapeDtypeStruct((blocks, rows, width), BF),
        compiler_params=params(),
        cost_estimate=cost(blocks, rows, depth, width),
        name="mlp_back",
    )(x, weight, slope)


def plain_in(x, weight, image_rows):
    blocks, rows, depth = x.shape
    width = weight.shape[2]
    tile = tile_of(width)

    def finish(stream, value, place, extra):
        return (value,)

    def body(x_ref, w_ref, o_ref):
        up_kernel(image_rows, nn, finish, x_ref, w_ref, (), (o_ref,))

    return pl.pallas_call(
        body,
        grid=(width // tile,),
        in_specs=[
            resident((blocks, rows, depth)),
            pl.BlockSpec((2, depth, tile), lambda n: (0, 0, n)),
        ],
        out_specs=pl.BlockSpec((blocks, rows, tile), lambda n: (0, 0, n)),
        out_shape=jax.ShapeDtypeStruct((blocks, rows, width), BF),
        compiler_params=params(),
        cost_estimate=cost(blocks, rows, depth, width),
        name="plain_in",
    )(x, weight)


def project_out(y, weight, image_rows):
    groups, blocks, rows, width = y.shape
    depth = weight.shape[2]
    tile = tile_of(depth)

    def body(y_ref, w_ref, o_ref):
        step = chunk_of(blocks, image_rows)

        def image(i, carry):
            part = pl.ds(i * step, step)
            total = None
            for g in range(groups):
                y_part = y_ref[g, part, :image_rows, :].reshape(step * image_rows, width)
                term = nt(y_part, w_ref[g, 0])
                total = term if total is None else total + term
            o_ref[part, :image_rows, :] = total.reshape(step, image_rows, tile).astype(BF)
            return carry

        lax.fori_loop(0, blocks // step, image, 0)
        text_rows = rows - image_rows
        total = None
        for g in range(groups):
            y_part = y_ref[g, :, image_rows:, :].reshape(blocks * text_rows, width)
            term = nt(y_part, w_ref[g, 1])
            total = term if total is None else total + term
        o_ref[:, image_rows:, :] = total.reshape(blocks, text_rows, tile).astype(BF)

    return pl.pallas_call(
        body,
        grid=(depth // tile,),
        in_specs=[
            resident((groups, blocks, rows, width)),
            pl.BlockSpec((groups, 2, tile, width), lambda n: (0, 0, n, 0)),
        ],
        out_specs=pl.BlockSpec((blocks, rows, tile), lambda n: (0, 0, n)),
        out_shape=jax.ShapeDtypeStruct((blocks, rows, depth), BF),
        compiler_params=params(),
        cost_estimate=cost(blocks, rows, depth, width, groups),
        name="project_out",
    )(y, weight)


def weight_grad(x, y, image_rows):
    blocks, rows, depth = x.shape
    groups, width = y.shape[0], y.shape[3]
    tile = tile_of(depth, 256)
    text_rows = rows - image_rows
    columns = tile_of(width)

    def body(x_ref, y_ref, o_ref, s_ref):
        for stream, (low, high) in enumerate(((0, image_rows), (image_rows, rows))):
            count = blocks * (high - low)
            turned = x_ref[:, low:high, :].reshape(count, tile).T

            for n in range(width // columns):
                part = slice(n * columns, (n + 1) * columns)
                y_part = y_ref[:, low:high, part].reshape(count, columns)
                o_ref[stream, :, part] = nn(turned, y_part).astype(BF)

        @pl.when(pl.program_id(1) == 0)
        def _():
            for stream, (low, high) in enumerate(((0, image_rows), (image_rows, rows))):
                total = jnp.zeros((high - low, width), F32)
                total = lax.fori_loop(
                    0, blocks, lambda i, t: t + y_ref[i, low:high, :].astype(F32), total
                )
                s_ref[stream] = jnp.sum(total, axis=0, keepdims=True)

    return pl.pallas_call(
        body,
        grid=(groups, depth // tile),
        in_specs=[
            pl.BlockSpec((blocks, rows, tile), lambda g, k: (0, 0, k)),
            pl.BlockSpec((None, blocks, rows, width), lambda g, k: (g, 0, 0, 0)),
        ],
        out_specs=[
            pl.BlockSpec((None, 2, tile, width), lambda g, k: (g, 0, k, 0)),
            pl.BlockSpec((None, 2, 1, width), lambda g, k: (g, 0, 0, 0)),
        ],
        out_shape=[
            jax.ShapeDtypeStruct((groups, 2, depth, width), BF),
            jax.ShapeDtypeStruct((groups, 2, 1, width), F32),
        ],
        compiler_params=params(),
        cost_estimate=cost(blocks, rows, depth, width, groups),
        name="weight_grad",
    )(x, y)


def head_block(width):
    return 128 if width % 128 == 0 else width


def query_tile(length):
    for tile in (384, 256, 128):
        if length % tile == 0:
            return tile
    return length


def attention(qkv, ranks):
    _, blocks, rows, width = qkv.shape
    sequences = blocks // ranks
    length = ranks * rows
    block = head_block(width)
    heads = block // HD
    tile = query_tile(length)
    view = qkv.reshape(3, ranks, sequences, rows, width)

    def body(q_ref, k_ref, v_ref, o_ref, m_ref):
        turned = []
        for h in range(heads):
            lanes = slice(h * HD, (h + 1) * HD)
            queries = q_ref[:, :, lanes].reshape(length, HD)
            keys = k_ref[:, :, lanes].reshape(length, HD)
            values = v_ref[:, :, lanes].reshape(length, HD).T
            pieces = []
            for c in range(length // tile):
                part = slice(c * tile, (c + 1) * tile)
                scores = nt(keys, queries[part])
                highest = jnp.max(scores, axis=0, keepdims=True)
                shifted = jnp.exp2((scores - highest) * (SCORE * LOG2E))
                total = jnp.sum(shifted, axis=0, keepdims=True)
                pieces.append(nn(values, shifted.astype(BF)) / total)
                m_ref[h : h + 1, part] = highest * (SCORE * LOG2E) + jnp.log2(total)
            turned.append(jnp.concatenate(pieces, axis=1))
        result = jnp.concatenate(turned, axis=0).T
        o_ref[...] = result.astype(BF).reshape(ranks, rows, block)

    def pick(j):
        return pl.BlockSpec((None, ranks, None, rows, block), lambda s, p: (j, 0, s, 0, p))

    attended, totals = pl.pallas_call(
        body,
        grid=(sequences, width // block),
        in_specs=[pick(0), pick(1), pick(2)],
        out_specs=[
            pl.BlockSpec((ranks, None, rows, block), lambda s, p: (0, s, 0, p)),
            pl.BlockSpec((None, None, heads, length), lambda s, p: (s, p, 0, 0)),
        ],
        out_shape=[
            jax.ShapeDtypeStruct((ranks, sequences, rows, width), BF),
            jax.ShapeDtypeStruct((sequences, width // block, heads, length), F32),
        ],
        compiler_params=params(),
        cost_estimate=pl.CostEstimate(
            flops=16 * sequences * length * length * width,
            bytes_accessed=8 * blocks * rows * width,
            transcendentals=sequences * length * length * width // HD,
        ),
        name="attention",
    )(view, view, view)
    return attended.reshape(blocks, rows, width), totals


def attention_back(qkv, totals, attended, grad, ranks):
    _, blocks, rows, width = qkv.shape
    sequences = blocks // ranks
    length = ranks * rows
    block = head_block(width)
    heads = block // HD
    tile = query_tile(length)
    view = qkv.reshape(3, ranks, sequences, rows, width)
    split = (ranks, sequences, rows, width)

    def body(q_ref, k_ref, v_ref, m_ref, a_ref, g_ref, o_ref):
        for h in range(heads):
            lanes = slice(h * HD, (h + 1) * HD)
            queries = q_ref[:, :, lanes].reshape(length, HD)
            keys = k_ref[:, :, lanes].reshape(length, HD)
            values = v_ref[:, :, lanes].reshape(length, HD)
            grads = g_ref[:, :, lanes].reshape(length, HD)
            attended_rows = a_ref[:, :, lanes].reshape(length, HD)
            cross = grads.astype(F32) * attended_rows.astype(F32)
            delta = jnp.sum(cross.T, axis=0, keepdims=True)
            keys_turned = keys.T
            grad_keys = jnp.zeros((length, HD), F32)
            grad_values = jnp.zeros((length, HD), F32)
            pieces = []
            for c in range(length // tile):
                part = slice(c * tile, (c + 1) * tile)
                scores = nt(keys, queries[part])
                probs = jnp.exp2(scores * (SCORE * LOG2E) - m_ref[h : h + 1, part])
                grad_probs = nt(values, grads[part])
                grad_scores = (probs * (grad_probs - delta[:, part])).astype(BF)
                grad_values = grad_values + nn(probs.astype(BF), grads[part])
                grad_keys = grad_keys + nn(grad_scores, queries[part])
                pieces.append(nn(keys_turned, grad_scores))
            grad_queries = jnp.concatenate(pieces, axis=1).T
            for j, value in enumerate((grad_queries * SCORE, grad_keys * SCORE, grad_values)):
                o_ref[j, :, :, lanes] = value.astype(BF).reshape(ranks, rows, HD)

    def pick(j):
        return pl.BlockSpec((None, ranks, None, rows, block), lambda s, p: (j, 0, s, 0, p))

    plain = pl.BlockSpec((ranks, None, rows, block), lambda s, p: (0, s, 0, p))
    out = pl.pallas_call(
        body,
        grid=(sequences, width // block),
        in_specs=[
            pick(0),
            pick(1),
            pick(2),
            pl.BlockSpec((None, None, heads, length), lambda s, p: (s, p, 0, 0)),
            plain,
            plain,
        ],
        out_specs=pl.BlockSpec((3, ranks, None, rows, block), lambda s, p: (0, 0, s, 0, p)),
        out_shape=jax.ShapeDtypeStruct((3, ranks, sequences, rows, width), BF),
        compiler_params=params(),
        cost_estimate=pl.CostEstimate(
            flops=40 * sequences * length * length * width,
            bytes_accessed=16 * blocks * rows * width,
            transcendentals=sequences * length * length * width // HD,
        ),
        name="attention_back",
    )(view, view, view, totals, attended.reshape(split), grad.reshape(split))
    return out.reshape(3, blocks, rows, width)


def normalize(operand):
    center = operand - jnp.mean(operand, axis=-1, keepdims=True)
    inverse = lax.rsqrt(jnp.mean(center * center, axis=-1, keepdims=True) + EPSILON)
    return (center * inverse, inverse)


def normalize_back(grad_normed, normed, inverse):
    mean_grad = jnp.mean(grad_normed, axis=-1, keepdims=True)
    mean_cross = jnp.mean(grad_normed * normed, axis=-1, keepdims=True)
    return inverse * (grad_normed - mean_grad - normed * mean_cross)


def modulate(residual, shift, scale_mod):
    normed, inverse = normalize(residual)
    lowered = (normed * (1.0 + scale_mod[:, None, :]) + shift[:, None, :]).astype(BF)
    return (normed, inverse, lowered)


def spread(image, text):
    full = lax.all_gather(jnp.concatenate([image, text], axis=1), "tensor", axis=0)
    return full.reshape((-1,) + full.shape[2:])


def collect(terms, ranks, image_rows):
    split = terms.reshape((ranks, -1) + terms.shape[1:])
    total = lax.psum_scatter(split, "tensor", scatter_dimension=0).astype(F32)
    return total[:, :image_rows], total[:, image_rows:]


def fetch(shard):
    return lax.all_gather(shard, "dp", axis=shard.ndim - 2, tiled=True)


def give(total):
    return lax.psum_scatter(total, "dp", scatter_dimension=total.ndim - 2, tiled=True).astype(F32)


def per_device(
    image_in,
    text_in,
    condition,
    mod_weight,
    qkv_weight,
    proj_weight,
    up_weight,
    down_weight,
    mod_bias,
    qkv_bias,
    proj_bias,
    up_bias,
    down_bias,
    image_cot,
    text_cot,
):
    ranks = lax.axis_size("tensor")
    column = lax.axis_index("tensor")
    row = lax.axis_index("dp")
    sequences, image_rows, model_width = image_in.shape
    text_rows = text_in.shape[1]
    local_width = model_width // ranks
    local_inner = up_weight.shape[2]
    depth_rows = up_weight.shape[1]
    start_col = column * local_width
    start_inner = column * local_inner
    start_depth = row * depth_rows

    qkv_full = fetch(qkv_weight.transpose(2, 0, 1, 3))
    proj_full = fetch(proj_weight.transpose(0, 2, 1))
    up_full = fetch(up_weight)
    down_full = fetch(down_weight.transpose(0, 2, 1))

    cond_float = condition.astype(F32)
    silu_cond = jax.nn.silu(cond_float).astype(BF)
    silu_all = lax.all_gather(silu_cond, "dp", axis=0, tiled=True)
    silu_mine = lax.dynamic_slice_in_dim(silu_all, start_depth, depth_rows, 1)
    mod_term = jnp.einsum("bd,sdkf->bskf", silu_mine, mod_weight, preferred_element_type=F32)
    mod_bias_cols = lax.dynamic_slice_in_dim(mod_bias, start_col, local_width, 2).astype(F32)
    mod_cols = lax.psum_scatter(mod_term, "dp", scatter_dimension=0, tiled=True) + mod_bias_cols
    modulation = lax.all_gather(mod_cols.astype(BF), "tensor", axis=3, tiled=True).astype(F32)

    qkv_bias_cols = (
        lax.dynamic_slice_in_dim(qkv_bias, start_col, local_width, 2)
        .astype(F32)
        .transpose(1, 0, 2)[:, :, None, :]
    )
    up_bias_cols = lax.dynamic_slice_in_dim(up_bias, start_inner, local_inner, 1).astype(F32)[
        :, None, :
    ]
    proj_bias_full = proj_bias.astype(F32)
    down_bias_full = down_bias.astype(F32)

    residuals = (image_in.astype(F32), text_in.astype(F32))
    cotangents = (image_cot.astype(F32), text_cot.astype(F32))
    first_norm, first_inv, first_low = [], [], []
    for stream in range(2):
        normed, inverse, lowered = modulate(
            residuals[stream], modulation[:, stream, 0], modulation[:, stream, 1]
        )
        first_norm.append(normed)
        first_inv.append(inverse)
        first_low.append(lowered)
    first_full = spread(*first_low)

    grad_mlp_low, down_bias_terms = [], []
    for stream in range(2):
        lowered = (modulation[:, stream, 5][:, None, :] * cotangents[stream]).astype(BF)
        grad_mlp_low.append(lowered)
        down_bias_terms.append(jnp.sum(lowered.astype(F32), axis=(0, 1)))
    grad_mlp_full = spread(*grad_mlp_low)

    qkv = project_in(first_full, qkv_full, qkv_bias_cols, image_rows)
    attended, log_totals = attention(qkv, ranks)
    proj_sums = collect(
        project_out(attended[None], proj_full[None], image_rows), ranks, image_rows
    )

    attn_branches, middles, second_norm, second_inv, second_low = [], [], [], [], []
    for stream in range(2):
        attn_branch = proj_sums[stream] + proj_bias_full[stream]
        middle = residuals[stream] + modulation[:, stream, 2][:, None, :] * attn_branch
        normed, inverse, lowered = modulate(
            middle, modulation[:, stream, 3], modulation[:, stream, 4]
        )
        attn_branches.append(attn_branch)
        middles.append(middle)
        second_norm.append(normed)
        second_inv.append(inverse)
        second_low.append(lowered)
    second_full = spread(*second_low)

    activated, slope = mlp_in(second_full, up_full, up_bias_cols, image_rows)
    down_sums = collect(
        project_out(activated[None], down_full[None], image_rows), ranks, image_rows
    )
    grad_pre = mlp_back(grad_mlp_full, down_full, slope, image_rows)
    second_sums = collect(project_out(grad_pre[None], up_full[None], image_rows), ranks, image_rows)

    grad_shift_two, grad_scale_two, grad_gate_one = [], [], []
    grad_middles, grad_attn_low, proj_bias_terms = [], [], []
    for stream in range(2):
        incoming = second_sums[stream]
        grad_shift_two.append(jnp.sum(incoming, axis=1))
        grad_scale_two.append(jnp.sum(incoming * second_norm[stream], axis=1))
        scaled = incoming * (1.0 + modulation[:, stream, 4][:, None, :])
        grad_middle = cotangents[stream] + normalize_back(
            scaled, second_norm[stream], second_inv[stream]
        )
        grad_middles.append(grad_middle)
        grad_gate_one.append(jnp.sum(grad_middle * attn_branches[stream], axis=1))
        lowered = (modulation[:, stream, 2][:, None, :] * grad_middle).astype(BF)
        grad_attn_low.append(lowered)
        proj_bias_terms.append(jnp.sum(lowered.astype(F32), axis=(0, 1)))
    grad_attn_full = spread(*grad_attn_low)

    grad_gate_two, outputs, stat_rows = [], [], []
    for stream in range(2):
        mlp_branch = down_sums[stream] + down_bias_full[stream]
        gated_attn = modulation[:, stream, 2][:, None, :] * attn_branches[stream]
        gated_mlp = modulation[:, stream, 5][:, None, :] * mlp_branch
        outputs.append((middles[stream] + gated_mlp).astype(BF))
        grad_gate_two.append(jnp.sum(cotangents[stream] * mlp_branch, axis=1))
        residual = residuals[stream]
        stat_rows.append(
            jnp.stack(
                [
                    jnp.sum(residual * residual, axis=(1, 2)),
                    jnp.sum(gated_attn * gated_attn, axis=(1, 2)),
                    jnp.sum(gated_mlp * gated_mlp, axis=(1, 2)),
                ],
                axis=1,
            )
        )
    stat_local = jnp.stack(stat_rows, axis=1)

    down_grad, _ = weight_grad(grad_mlp_full, activated[None], image_rows)
    up_grad, up_bias_term = weight_grad(second_full, grad_pre[None], image_rows)
    down_total = give(down_grad[0])
    up_total = give(up_grad[0])

    grad_attended = plain_in(grad_attn_full, proj_full, image_rows)
    grad_qkv = attention_back(qkv, log_totals, attended, grad_attended, ranks)
    first_sums = collect(project_out(grad_qkv, qkv_full, image_rows), ranks, image_rows)
    proj_grad, _ = weight_grad(grad_attn_full, attended[None], image_rows)
    qkv_grad, qkv_bias_term = weight_grad(first_full, grad_qkv, image_rows)
    proj_total = give(proj_grad[0])
    qkv_total = give(qkv_grad)

    input_grads, grad_mod_rows = [], []
    for stream in range(2):
        incoming = first_sums[stream]
        grad_shift_one = jnp.sum(incoming, axis=1)
        grad_scale_one = jnp.sum(incoming * first_norm[stream], axis=1)
        scaled = incoming * (1.0 + modulation[:, stream, 1][:, None, :])
        input_grads.append(
            grad_middles[stream] + normalize_back(scaled, first_norm[stream], first_inv[stream])
        )
        grad_mod_rows.append(
            jnp.stack(
                [
                    grad_shift_one,
                    grad_scale_one,
                    grad_gate_one[stream],
                    grad_shift_two[stream],
                    grad_scale_two[stream],
                    grad_gate_two[stream],
                ],
                axis=1,
            )
        )
    grad_mod = jnp.stack(grad_mod_rows, axis=1)
    grad_mod_cols = lax.psum_scatter(grad_mod, "tensor", scatter_dimension=3, tiled=True).astype(BF)
    grad_mod_all = lax.all_gather(grad_mod_cols, "dp", axis=0, tiled=True)
    mod_total = jnp.einsum("bd,bskf->sdkf", silu_mine, grad_mod_all, preferred_element_type=F32)
    cond_term = jnp.einsum("bskf,sdkf->bd", grad_mod_all, mod_weight, preferred_element_type=F32)
    cond_total = lax.all_gather(lax.psum(cond_term, "tensor"), "dp", axis=1, tiled=True)
    cond_mine = lax.dynamic_slice_in_dim(cond_total, row * sequences, sequences, 0)
    unused_silu, silu_pull = jax.vjp(jax.nn.silu, cond_float)
    condition_grad = silu_pull(cond_mine)[0]

    mod_bias_mine = jnp.sum(grad_mod_all.astype(F32), axis=0)
    wide = jnp.concatenate(
        [jnp.stack(proj_bias_terms).ravel(), jnp.stack(down_bias_terms).ravel()]
    )
    owned = jnp.concatenate([qkv_bias_term.ravel(), up_bias_term.ravel()])
    wide_all, stat_totals = lax.psum((wide, stat_local), "tensor")
    shared = lax.psum(jnp.concatenate([owned, wide_all]), "dp")
    owned_sum, wide_sum = shared[: owned.size], shared[owned.size :]
    columns = lax.all_gather(
        jnp.concatenate([owned_sum, mod_bias_mine.ravel()]), "tensor", axis=0
    )
    qkv_size, up_size = 6 * local_width, 2 * local_inner
    qkv_bias_grad = columns[:, :qkv_size].reshape(ranks, 3, 2, local_width)
    qkv_bias_grad = qkv_bias_grad.transpose(2, 1, 0, 3).reshape(2, 3, model_width)
    up_bias_grad = columns[:, qkv_size : qkv_size + up_size].reshape(ranks, 2, local_inner)
    up_bias_grad = up_bias_grad.transpose(1, 0, 2).reshape(2, ranks * local_inner)
    mod_bias_grad = columns[:, qkv_size + up_size :].reshape(ranks, 2, 6, local_width)
    mod_bias_grad = mod_bias_grad.transpose(1, 2, 0, 3).reshape(2, 6, model_width)
    wide_sum = wide_sum.reshape(2, 2, model_width)

    row_counts = jnp.array(
        [ranks * image_rows * model_width, ranks * text_rows * model_width], F32
    ).reshape(1, 2, 1)
    rms_stats = jnp.sqrt(stat_totals / row_counts)
    return (
        outputs[0],
        outputs[1],
        input_grads[0],
        input_grads[1],
        condition_grad,
        mod_total,
        qkv_total.transpose(1, 2, 0, 3),
        proj_total.transpose(0, 2, 1),
        up_total,
        down_total.transpose(0, 2, 1),
        mod_bias_grad,
        qkv_bias_grad,
        wide_sum[0],
        up_bias_grad,
        wide_sum[1],
        rms_stats,
    )


def solution(mesh):
    tokens = P("dp", "tensor", None)
    return jax.shard_map(
        per_device,
        mesh=mesh,
        in_specs=(
            tokens,
            tokens,
            P("dp", None),
            P(None, "dp", None, "tensor"),
            P(None, "dp", None, "tensor"),
            P(None, "tensor", "dp"),
            P(None, "dp", "tensor"),
            P(None, "tensor", "dp"),
            P(),
            P(),
            P(),
            P(),
            P(),
            tokens,
            tokens,
        ),
        out_specs=(
            tokens,
            tokens,
            tokens,
            tokens,
            P("dp", None),
            P(None, "dp", None, "tensor"),
            P(None, "dp", None, "tensor"),
            P(None, "tensor", "dp"),
            P(None, "dp", "tensor"),
            P(None, "tensor", "dp"),
            P(),
            P(),
            P(),
            P(),
            P(),
            P("dp", None, None),
        ),
        check_vma=False,
    )
```

```python
import functools

import jax
import jax.numpy as jnp
from jax import lax
from jax.experimental import pallas as pl
from jax.experimental.pallas import tpu as pltpu
from jax.sharding import PartitionSpec as P

HD = 64
EPSILON = 1e-06
LOG2E = 1.4426950408889634
SCORE = HD ** (-0.5)
VMEM_LIMIT = 56 * 1024 * 1024
BF = jnp.bfloat16
F32 = jnp.float32


def nn(a, b):
    return lax.dot_general(a, b, (((1,), (0,)), ((), ())), preferred_element_type=F32)


def nt(a, b):
    return lax.dot_general(a, b, (((1,), (1,)), ((), ())), preferred_element_type=F32)


def params():
    return pltpu.CompilerParams(vmem_limit_bytes=VMEM_LIMIT)


def resident(shape):
    zeros = (0,) * len(shape)
    return pl.BlockSpec(shape, lambda *_: zeros, pipeline_mode=pl.Buffered(1))


def tile_of(width, most=512):
    for tile in (512, 384, 256, 128):
        if tile <= most and width % tile == 0:
            return tile
    return width


def chunk_of(blocks, rows):
    count = 1
    while count * rows < 512 and blocks % (2 * count) == 0:
        count *= 2
    return count


def up_kernel(image_rows, product, finish, x_ref, w_ref, extra_refs, out_refs):
    blocks, rows, depth = x_ref.shape
    width = out_refs[0].shape[-1]
    step = chunk_of(blocks, image_rows)

    def image(i, carry):
        part = pl.ds(i * step, step)
        x = x_ref[part, :image_rows, :].reshape(step * image_rows, depth)
        results = finish(0, product(x, w_ref[0]), (part, slice(0, image_rows)), extra_refs)
        for ref, value in zip(out_refs, results):
            ref[part, :image_rows, :] = value.reshape(step, image_rows, width).astype(ref.dtype)
        return carry

    lax.fori_loop(0, blocks // step, image, 0)
    text_rows = rows - image_rows
    x = x_ref[:, image_rows:, :].reshape(blocks * text_rows, depth)
    results = finish(1, product(x, w_ref[1]), (slice(None), slice(image_rows, rows)), extra_refs)
    for ref, value in zip(out_refs, results):
        ref[:, image_rows:, :] = value.reshape(blocks, text_rows, width).astype(ref.dtype)


def project_in(x, weight, bias, image_rows):
    blocks, rows, depth = x.shape
    groups, width = weight.shape[0], weight.shape[3]
    tile = tile_of(width)

    extras = () if bias is None else (bias,)

    def finish(stream, value, place, extra):
        return (value + extra[0][stream] if extra else value,)

    def body(x_ref, w_ref, *refs):
        up_kernel(image_rows, nn, finish, x_ref, w_ref, refs[:-1], refs[-1:])

    return pl.pallas_call(
        body,
        grid=(groups, width // tile),
        in_specs=[
            resident((blocks, rows, depth)),
            pl.BlockSpec((None, 2, depth, tile), lambda g, n: (g, 0, 0, n)),
        ]
        + [pl.BlockSpec((None, 2, 1, tile), lambda g, n: (g, 0, 0, n)) for _ in extras],
        out_specs=pl.BlockSpec((None, blocks, rows, tile), lambda g, n: (g, 0, 0, n)),
        out_shape=jax.ShapeDtypeStruct((groups, blocks, rows, width), BF),
        compiler_params=params(),
        name="project_in",
    )(x, weight, *extras)


def mlp_in(x, weight, bias, image_rows):
    blocks, rows, depth = x.shape
    width = weight.shape[2]
    tile = tile_of(width)
    root = 0.7978845608028654

    def finish(stream, value, place, extra):
        v = value + extra[0][stream]
        square = v * v
        t = jnp.tanh(v * (root + (root * 0.044715) * square))
        half = 0.5 + 0.5 * t
        slope = half + v * (0.5 - 0.5 * t * t) * (root + (root * 3.0 * 0.044715) * square)
        return (v * half, slope)

    def body(x_ref, w_ref, b_ref, a_ref, s_ref):
        up_kernel(image_rows, nn, finish, x_ref, w_ref, (b_ref,), (a_ref, s_ref))

    spec = pl.BlockSpec((blocks, rows, tile), lambda n: (0, 0, n))
    shape = jax.ShapeDtypeStruct((blocks, rows, width), BF)
    return pl.pallas_call(
        body,
        grid=(width // tile,),
        in_specs=[
            resident((blocks, rows, depth)),
            pl.BlockSpec((2, depth, tile), lambda n: (0, 0, n)),
            pl.BlockSpec((2, 1, tile), lambda n: (0, 0, n)),
        ],
        out_specs=[spec, spec],
        out_shape=[shape, shape],
        compiler_params=params(),
        name="mlp_in",
    )(x, weight, bias)


def mlp_back(x, weight, slope, image_rows):
    blocks, rows, depth = x.shape
    width = weight.shape[2]
    tile = tile_of(width)

    def finish(stream, value, place, extra):
        factor = extra[0][place[0], place[1], :].astype(F32)
        return (value * factor.reshape(value.shape),)

    def body(x_ref, w_ref, s_ref, o_ref):
        up_kernel(image_rows, nn, finish, x_ref, w_ref, (s_ref,), (o_ref,))

    spec = pl.BlockSpec((blocks, rows, tile), lambda n: (0, 0, n))
    return pl.pallas_call(
        body,
        grid=(width // tile,),
        in_specs=[
            resident((blocks, rows, depth)),
            pl.BlockSpec((2, depth, tile), lambda n: (0, 0, n)),
            spec,
        ],
        out_specs=spec,
        out_shape=jax.ShapeDtypeStruct((blocks, rows, width), BF),
        compiler_params=params(),
        name="mlp_back",
    )(x, weight, slope)


def project_out(y, weight, image_rows, dtype=BF):
    groups, blocks, rows, width = y.shape
    depth = weight.shape[2]
    tile = tile_of(depth)

    def body(y_ref, w_ref, o_ref):
        step = chunk_of(blocks, image_rows)

        def image(i, carry):
            part = pl.ds(i * step, step)
            total = None
            for g in range(groups):
                y_part = y_ref[g, part, :image_rows, :].reshape(step * image_rows, width)
                term = nt(y_part, w_ref[g, 0])
                total = term if total is None else total + term
            o_ref[part, :image_rows, :] = total.reshape(step, image_rows, tile).astype(dtype)
            return carry

        lax.fori_loop(0, blocks // step, image, 0)
        text_rows = rows - image_rows
        total = None
        for g in range(groups):
            y_part = y_ref[g, :, image_rows:, :].reshape(blocks * text_rows, width)
            term = nt(y_part, w_ref[g, 1])
            total = term if total is None else total + term
        o_ref[:, image_rows:, :] = total.reshape(blocks, text_rows, tile).astype(dtype)

    return pl.pallas_call(
        body,
        grid=(depth // tile,),
        in_specs=[
            resident((groups, blocks, rows, width)),
            pl.BlockSpec((groups, 2, tile, width), lambda n: (0, 0, n, 0)),
        ],
        out_specs=pl.BlockSpec((blocks, rows, tile), lambda n: (0, 0, n)),
        out_shape=jax.ShapeDtypeStruct((blocks, rows, depth), dtype),
        compiler_params=params(),
        name="project_out",
    )(y, weight)


def weight_grad(x, y, image_rows):
    blocks, rows, depth = x.shape
    groups, width = y.shape[0], y.shape[3]
    tile = tile_of(depth, 256)
    text_rows = rows - image_rows
    columns = tile_of(width)

    def body(x_ref, y_ref, o_ref, s_ref):
        for stream, (low, high) in enumerate(((0, image_rows), (image_rows, rows))):
            count = blocks * (high - low)
            turned = x_ref[:, low:high, :].reshape(count, tile).T

            for n in range(width // columns):
                part = slice(n * columns, (n + 1) * columns)
                y_part = y_ref[:, low:high, part].reshape(count, columns)
                o_ref[stream, :, part] = nn(turned, y_part).astype(BF)

        @pl.when(pl.program_id(1) == 0)
        def _():
            for stream, (low, high) in enumerate(((0, image_rows), (image_rows, rows))):
                total = jnp.zeros((high - low, width), F32)
                total = lax.fori_loop(
                    0, blocks, lambda i, t: t + y_ref[i, low:high, :].astype(F32), total
                )
                s_ref[stream] = jnp.sum(total, axis=0, keepdims=True)

    return pl.pallas_call(
        body,
        grid=(groups, depth // tile),
        in_specs=[
            pl.BlockSpec((blocks, rows, tile), lambda g, k: (0, 0, k)),
            pl.BlockSpec((None, blocks, rows, width), lambda g, k: (g, 0, 0, 0)),
        ],
        out_specs=[
            pl.BlockSpec((None, 2, tile, width), lambda g, k: (g, 0, k, 0)),
            pl.BlockSpec((None, 2, 1, width), lambda g, k: (g, 0, 0, 0)),
        ],
        out_shape=[
            jax.ShapeDtypeStruct((groups, 2, depth, width), BF),
            jax.ShapeDtypeStruct((groups, 2, 1, width), F32),
        ],
        compiler_params=params(),
        name="weight_grad",
    )(x, y)


def modulate_all(x, mods, image_rows):
    ranks, sequences, rows, depth = x.shape
    step = 16

    def body(x_ref, m_ref, o_ref):
        def some(i, carry):
            part = pl.ds(pl.multiple_of(i * step, step), step)
            stream = lax.div(i * step, image_rows)
            value = x_ref[part, :].astype(F32)
            center = value - jnp.mean(value, axis=-1, keepdims=True)
            inverse = lax.rsqrt(jnp.mean(center * center, axis=-1, keepdims=True) + EPSILON)
            scale, shift = 1.0 + m_ref[stream, 1:2, :], m_ref[stream, 0:1, :]
            o_ref[part, :] = (center * inverse * scale + shift).astype(BF)
            return carry

        lax.fori_loop(0, rows // step, some, 0, unroll=3)

    spec = pl.BlockSpec((None, None, rows, depth), lambda t, q: (t, q, 0, 0))
    return pl.pallas_call(
        body,
        grid=(ranks, sequences),
        in_specs=[spec, pl.BlockSpec((None, 2, 2, depth), lambda t, q: (q, 0, 0, 0))],
        out_specs=spec,
        out_shape=jax.ShapeDtypeStruct(x.shape, BF),
        compiler_params=params(),
        name="modulate_all",
    )(x, mods)


def head_block(width):
    return 128 if width % 128 == 0 else width


def query_tile(length):
    for tile in (384, 256, 128):
        if length % tile == 0:
            return tile
    return length


def attention(qkv, ranks):
    _, blocks, rows, width = qkv.shape
    sequences = blocks // ranks
    length = ranks * rows
    block = head_block(width)
    heads = block // HD
    tile = query_tile(length)
    view = qkv.reshape(3, ranks, sequences, rows, width)

    def body(q_ref, k_ref, v_ref, o_ref, m_ref):
        turned = []
        for h in range(heads):
            lanes = slice(h * HD, (h + 1) * HD)
            queries = q_ref[:, :, lanes].reshape(length, HD)
            keys = k_ref[:, :, lanes].reshape(length, HD)
            values = v_ref[:, :, lanes].reshape(length, HD).T
            pieces = []
            for c in range(length // tile):
                part = slice(c * tile, (c + 1) * tile)
                scores = nt(keys, queries[part])
                highest = jnp.max(scores, axis=0, keepdims=True)
                shifted = jnp.exp2((scores - highest) * (SCORE * LOG2E))
                total = jnp.sum(shifted, axis=0, keepdims=True)
                pieces.append(nn(values, shifted.astype(BF)) / total)
                m_ref[h : h + 1, part] = highest * (SCORE * LOG2E) + jnp.log2(total)
            turned.append(jnp.concatenate(pieces, axis=1))
        result = jnp.concatenate(turned, axis=0).T
        o_ref[...] = result.astype(BF).reshape(ranks, rows, block)

    def pick(j):
        return pl.BlockSpec((None, ranks, None, rows, block), lambda s, p: (j, 0, s, 0, p))

    attended, totals = pl.pallas_call(
        body,
        grid=(sequences, width // block),
        in_specs=[pick(0), pick(1), pick(2)],
        out_specs=[
            pl.BlockSpec((ranks, None, rows, block), lambda s, p: (0, s, 0, p)),
            pl.BlockSpec((None, None, heads, length), lambda s, p: (s, p, 0, 0)),
        ],
        out_shape=[
            jax.ShapeDtypeStruct((ranks, sequences, rows, width), BF),
            jax.ShapeDtypeStruct((sequences, width // block, heads, length), F32),
        ],
        compiler_params=params(),
        name="attention",
    )(view, view, view)
    return attended.reshape(blocks, rows, width), totals


def attention_back(qkv, totals, attended, grad, ranks):
    _, blocks, rows, width = qkv.shape
    sequences = blocks // ranks
    length = ranks * rows
    block = head_block(width)
    heads = block // HD
    tile = query_tile(length)
    view = qkv.reshape(3, ranks, sequences, rows, width)
    split = (ranks, sequences, rows, width)

    def body(q_ref, k_ref, v_ref, m_ref, a_ref, g_ref, o_ref):
        for h in range(heads):
            lanes = slice(h * HD, (h + 1) * HD)
            queries = q_ref[:, :, lanes].reshape(length, HD)
            keys = k_ref[:, :, lanes].reshape(length, HD)
            values = v_ref[:, :, lanes].reshape(length, HD)
            grads = g_ref[:, :, lanes].reshape(length, HD)
            attended_rows = a_ref[:, :, lanes].reshape(length, HD)
            cross = grads.astype(F32) * attended_rows.astype(F32)
            delta = jnp.sum(cross.T, axis=0, keepdims=True)
            keys_turned = keys.T
            grad_keys = jnp.zeros((length, HD), F32)
            grad_values = jnp.zeros((length, HD), F32)
            pieces = []
            for c in range(length // tile):
                part = slice(c * tile, (c + 1) * tile)
                scores = nt(keys, queries[part])
                probs = jnp.exp2(scores * (SCORE * LOG2E) - m_ref[h : h + 1, part])
                grad_probs = nt(values, grads[part])
                grad_scores = (probs * (grad_probs - delta[:, part])).astype(BF)
                grad_values = grad_values + nn(probs.astype(BF), grads[part])
                grad_keys = grad_keys + nn(grad_scores, queries[part])
                pieces.append(nn(keys_turned, grad_scores))
            grad_queries = jnp.concatenate(pieces, axis=1).T
            for j, value in enumerate((grad_queries * SCORE, grad_keys * SCORE, grad_values)):
                o_ref[j, :, :, lanes] = value.astype(BF).reshape(ranks, rows, HD)

    def pick(j):
        return pl.BlockSpec((None, ranks, None, rows, block), lambda s, p: (j, 0, s, 0, p))

    plain = pl.BlockSpec((ranks, None, rows, block), lambda s, p: (0, s, 0, p))
    out = pl.pallas_call(
        body,
        grid=(sequences, width // block),
        in_specs=[
            pick(0),
            pick(1),
            pick(2),
            pl.BlockSpec((None, None, heads, length), lambda s, p: (s, p, 0, 0)),
            plain,
            plain,
        ],
        out_specs=pl.BlockSpec((3, ranks, None, rows, block), lambda s, p: (0, 0, s, 0, p)),
        out_shape=jax.ShapeDtypeStruct((3, ranks, sequences, rows, width), BF),
        compiler_params=params(),
        name="attention_back",
    )(view, view, view, totals, attended.reshape(split), grad.reshape(split))
    return out.reshape(3, blocks, rows, width)


MESH = pl.DeviceIdType.MESH


def comm_params(collective_id):
    return pltpu.CompilerParams(
        vmem_limit_bytes=VMEM_LIMIT, collective_id=collective_id, has_side_effects=True
    )


def in_memory(shapes):
    return [pl.BlockSpec(memory_space=pltpu.VMEM) for _ in shapes]


def meet(peers):
    barrier = pltpu.get_barrier_semaphore()
    for peer in peers:
        pl.semaphore_signal(barrier, inc=1, device_id=peer, device_id_type=MESH)
    pl.semaphore_wait(barrier, len(peers))


def bit_steps(place, bits):
    core = lax.rem(place, 2)

    def flip(bit):
        return bit * (1 - 2 * lax.rem(lax.div(place, bit), 2))

    outer = bits - 1
    deltas = []
    for j in range(outer):
        low, high = flip(1 << (1 + j)), flip(1 << (outer - j))
        deltas.append(low + core * (high - low))
    return core, deltas, 1 - 2 * core


def gather_rows(arrays, size, collective_id):
    count = len(arrays)
    bits = size.bit_length() - 1
    outer = bits - 1

    def body(*refs):
        sources, targets = refs[:count], refs[count : 2 * count]
        send_sems, recv_sems, local_sems = refs[2 * count :]
        place = lax.axis_index("dp")
        core, deltas, core_delta = bit_steps(place, bits)
        steps = deltas + [core_delta]
        meet([{"dp": place + delta} for delta in steps])

        def piece(a, mask):
            index = place
            for j in range(outer):
                if mask >> j & 1:
                    index = index + deltas[j]
            rows = sources[a].shape[-2]
            lead = (slice(None),) * (len(sources[a].shape) - 2)
            start = pl.multiple_of(index * rows, rows)
            return targets[a].at[lead + (pl.ds(start, rows), slice(None))]

        def hop(a, mask, j):
            target = piece(a, mask)
            source = sources[a] if mask == 0 else target
            arrival = mask + (1 << j)
            return pltpu.make_async_remote_copy(
                src_ref=source,
                dst_ref=target,
                send_sem=send_sems.at[a, arrival],
                recv_sem=recv_sems.at[a, arrival],
                device_id={"dp": place + steps[j]},
                device_id_type=MESH,
            )

        hops = {}

        def start(a, mask, j):
            hops[a, mask + (1 << j)] = hop(a, mask, j)
            hops[a, mask + (1 << j)].start()

        locals_ = [
            pltpu.make_async_copy(sources[a], piece(a, 0), local_sems.at[a]) for a in range(count)
        ]
        for a in range(count):
            for j in range(bits):
                start(a, 0, j)
            locals_[a].start()
        for mask in range(1, 1 << outer):
            for a in range(count):
                hops[a, mask].wait_recv()
                for j in range(mask.bit_length(), bits):
                    start(a, mask, j)
        for a in range(count):
            locals_[a].wait()
            for mask in range(1, 1 << bits):
                if mask >> outer:
                    hops[a, mask].wait_recv()
                hops[a, mask].wait_send()

    shapes = [
        jax.ShapeDtypeStruct(a.shape[:-2] + (size * a.shape[-2], a.shape[-1]), a.dtype)
        for a in arrays
    ]
    return pl.pallas_call(
        body,
        in_specs=[pl.BlockSpec(memory_space=pl.ANY)] * count,
        out_specs=[pl.BlockSpec(memory_space=pl.ANY)] * count,
        out_shape=shapes,
        scratch_shapes=[
            pltpu.SemaphoreType.DMA((count, size)),
            pltpu.SemaphoreType.DMA((count, size)),
            pltpu.SemaphoreType.DMA((count,)),
        ],
        compiler_params=comm_params(collective_id),
        name="gather_rows",
    )(*arrays)


def scatter_rows(arrays, size, collective_id):
    count = len(arrays)
    bits = size.bit_length() - 1
    outer = bits - 1
    half = size // 2
    dims = [(a.shape[0], a.shape[1] // size, a.shape[2]) for a in arrays]
    views = [a.reshape(g, half, 2, r, f) for a, (g, r, f) in zip(arrays, dims)]
    chunks = [(a, g) for a in range(count) for g in range(dims[a][0])]

    def body(*refs):
        sources, targets = refs[:count], refs[count : 2 * count]
        rest = list(refs[2 * count :])
        mine, met = rest[:count], rest[count : 2 * count]
        slots = [rest[(2 + j) * count : (3 + j) * count] for j in range(outer)]
        load_sems, send0, recv0, send_sems, recv_sems = rest[(2 + outer) * count :]
        place = lax.axis_index("dp")
        core, deltas, core_delta = bit_steps(place, bits)
        meet([{"dp": place + delta} for delta in deltas + [core_delta]])
        position = lax.div(place, 2)

        def shard(mask):
            index = position
            for j in range(outer):
                if mask >> j & 1:
                    index = index + lax.div(deltas[j], 2)
            return index

        loads, swaps, hops = {}, {}, {}
        for n, (a, g) in enumerate(chunks):
            swaps[n] = pltpu.make_async_remote_copy(
                src_ref=sources[a].at[g, :, 1 - core],
                dst_ref=met[a].at[g],
                send_sem=send0.at[n],
                recv_sem=recv0.at[n],
                device_id={"dp": place + core_delta},
                device_id_type=MESH,
            )
            loads[n] = pltpu.make_async_copy(
                sources[a].at[g, :, core], mine[a].at[g], load_sems.at[n]
            )
            swaps[n].start()
            loads[n].start()

        def total(n, mask, below, target):
            a, g = chunks[n]
            rows = dims[a][1]
            step = 32 if rows % 32 == 0 else 16
            k = shard(mask)

            def add(i, carry):
                part = pl.ds(pl.multiple_of(i * step, step), step)
                value = mine[a][g, k, part, :].astype(F32) + met[a][g, k, part, :].astype(F32)
                for j in range(below):
                    value = value + slots[j][a][g, mask >> (j + 1), part, :].astype(F32)
                target(a, g, k, part, value)
                return carry

            lax.fori_loop(0, rows // step, add, 0)

        def keep(a, g, k, part, value):
            met[a][g, k, part, :] = value.astype(BF)

        def finish(a, g, k, part, value):
            targets[a][g, part, :] = value

        for j in range(outer):
            for n, (a, g) in enumerate(chunks):
                if j == 0:
                    swaps[n].wait_recv()
                    loads[n].wait()
                for mask in range(1, 1 << outer):
                    if mask & ((1 << (j + 1)) - 1) != 1 << j:
                        continue
                    for i in range(j):
                        hops[n, mask | 1 << i].wait_recv()
                    total(n, mask, j, keep)
                    hops[n, mask] = pltpu.make_async_remote_copy(
                        src_ref=met[a].at[g, shard(mask)],
                        dst_ref=slots[j][a].at[g, mask >> (j + 1)],
                        send_sem=send_sems.at[n, mask],
                        recv_sem=recv_sems.at[n, mask],
                        device_id={"dp": place + deltas[j]},
                        device_id_type=MESH,
                    )
                    hops[n, mask].start()
        for n in range(len(chunks)):
            for j in range(outer):
                hops[n, 1 << j].wait_recv()
            total(n, 0, outer, finish)
        for n in range(len(chunks)):
            swaps[n].wait_send()
            for mask in range(1, 1 << outer):
                hops[n, mask].wait_send()

    scratch = []
    for repeat in range(2):
        scratch += [pltpu.VMEM((g, half, r, f), BF) for g, r, f in dims]
    for j in range(outer):
        scratch += [pltpu.VMEM((g, 1 << (outer - 1 - j), r, f), BF) for g, r, f in dims]
    total_chunks = len(chunks)
    return pl.pallas_call(
        body,
        in_specs=[pl.BlockSpec(memory_space=pl.ANY)] * count,
        out_specs=in_memory(arrays),
        out_shape=[jax.ShapeDtypeStruct(d, F32) for d in dims],
        scratch_shapes=scratch
        + [
            pltpu.SemaphoreType.DMA((total_chunks,)),
            pltpu.SemaphoreType.DMA((total_chunks,)),
            pltpu.SemaphoreType.DMA((total_chunks,)),
            pltpu.SemaphoreType.DMA((total_chunks, half)),
            pltpu.SemaphoreType.DMA((total_chunks, half)),
        ],
        compiler_params=comm_params(collective_id),
        name="scatter_rows",
    )(*views)


def peers_of(axis, size):
    place = lax.axis_index(axis)
    return [lax.rem(place + i, size) for i in range(1, size)]


def exchange(axis, size, source, target, send_sems, recv_sems):
    place = lax.axis_index(axis)
    copies = []
    for i, peer in enumerate(peers_of(axis, size)):
        copy = pltpu.make_async_remote_copy(
            src_ref=source(peer),
            dst_ref=target(place),
            send_sem=send_sems.at[i],
            recv_sem=recv_sems.at[i],
            device_id={axis: peer},
            device_id_type=MESH,
        )
        copy.start()
        copies.append(copy)
    return copies


def wait_all(copies):
    for copy in copies:
        copy.wait_recv()
    for copy in copies:
        copy.wait_send()


def modulation_of(silu_parts, weight, bias, proj, ranks, collective_id):
    size, sequences, rows = silu_parts.shape
    width = weight.shape[2]

    def body(s_ref, w_ref, b_ref, p_ref, m_ref, all_ref, proj_ref, tall, terms, got, *sems):
        place, column = lax.axis_index("dp"), lax.axis_index("tensor")
        meet(
            [{"dp": p} for p in peers_of("dp", size)]
            + [{"tensor": p} for p in peers_of("tensor", ranks)]
        )
        copies = exchange(
            "dp", size, lambda p: s_ref.at[p], lambda p: all_ref.at[p], sems[0], sems[1]
        )
        spreads = exchange(
            "tensor", ranks, lambda p: p_ref, lambda p: proj_ref.at[p], sems[6], sems[7]
        )
        all_ref[place] = s_ref[place]
        proj_ref[column] = p_ref[...]
        tall[...] = jnp.zeros_like(tall)
        wait_all(copies)
        for j in range(size):
            tall[j, :sequences, :] = all_ref[j]
        left = tall[...].reshape(size * 8, rows).astype(BF)
        for stream in range(2):
            product = nn(left, w_ref[stream])
            for j in range(size):
                terms[j, :, stream * width : (stream + 1) * width] = product[
                    j * 8 : j * 8 + sequences
                ]
        copies = exchange(
            "dp", size, lambda p: terms.at[p], lambda p: got.at[p], sems[2], sems[3]
        )
        got[place] = terms[place]
        wait_all(copies)
        total = b_ref[...]
        for j in range(size):
            total = total + got[j]
        m_ref[column] = total.astype(BF).astype(F32)
        copies = exchange(
            "tensor",
            ranks,
            lambda p: m_ref.at[column],
            lambda p: m_ref.at[p],
            sems[4],
            sems[5],
        )
        wait_all(copies + spreads)

    dp_sems = pltpu.SemaphoreType.DMA((size,))
    tensor_sems = pltpu.SemaphoreType.DMA((ranks,))
    return pl.pallas_call(
        body,
        in_specs=in_memory(range(4)),
        out_specs=in_memory(range(3)),
        out_shape=[
            jax.ShapeDtypeStruct((ranks, sequences, 2 * width), F32),
            jax.ShapeDtypeStruct(silu_parts.shape, F32),
            jax.ShapeDtypeStruct((ranks,) + proj.shape, BF),
        ],
        scratch_shapes=[
            pltpu.VMEM((size, 8, rows), F32),
            pltpu.VMEM((size, sequences, 2 * width), F32),
            pltpu.VMEM((size, sequences, 2 * width), F32),
            dp_sems,
            dp_sems,
            dp_sems,
            dp_sems,
            tensor_sems,
            tensor_sems,
            tensor_sems,
            tensor_sems,
        ],
        compiler_params=comm_params(collective_id),
        name="modulation_of",
    )(silu_parts, weight, bias, proj)


def last_sums(grad_mod, wide, owned, weight, silu_all, collective_id):
    ranks, sequences, both = grad_mod.shape
    size, _, rows = silu_all.shape
    width = both // 2
    wide_size, owned_size = wide.shape[1], owned.shape[1]
    line = owned_size + wide_size

    def body(
        g_ref,
        wide_ref,
        owned_ref,
        w_ref,
        silu_ref,
        mod_ref,
        cond_ref,
        sum_ref,
        own_ref,
        got_g,
        got_wide,
        all_g,
        all_line,
        tall_g,
        tall_s,
        terms,
        got_terms,
        summed,
        *sems,
    ):
        place, column = lax.axis_index("dp"), lax.axis_index("tensor")
        meet(
            [{"dp": p} for p in peers_of("dp", size)]
            + [{"tensor": p} for p in peers_of("tensor", ranks)]
        )
        copies = exchange(
            "tensor", ranks, lambda p: g_ref.at[p], lambda p: got_g.at[p], sems[0], sems[1]
        )
        copies += exchange(
            "tensor", ranks, lambda p: wide_ref, lambda p: got_wide.at[p], sems[2], sems[3]
        )
        got_g[column] = g_ref[column]
        got_wide[column] = wide_ref[...]
        tall_g[...] = jnp.zeros_like(tall_g)
        tall_s[...] = jnp.zeros_like(tall_s)
        for j in range(size):
            tall_s[j, :sequences, :] = silu_ref[j]
        wait_all(copies)
        total, wide_total = got_g[0], got_wide[0]
        for t in range(1, ranks):
            total = total + got_g[t]
            wide_total = wide_total + got_wide[t]
        all_g[place] = total.astype(BF).astype(F32)
        all_line[place, :, :owned_size] = owned_ref[...]
        all_line[place, :, owned_size:] = wide_total
        copies = exchange(
            "dp", size, lambda p: all_g.at[place], lambda p: all_g.at[p], sems[4], sems[5]
        )
        copies += exchange(
            "dp", size, lambda p: all_line.at[place], lambda p: all_line.at[p], sems[6], sems[7]
        )
        wait_all(copies)
        line_total = all_line[0]
        bias_rows = all_g[0]
        for j in range(1, size):
            line_total = line_total + all_line[j]
            bias_rows = bias_rows + all_g[j]
        sum_ref[...] = line_total[:, owned_size:]
        sum_ref[:, wide_size - 128 :] = wide_total[:, wide_size - 128 :]
        own_ref[column, :, :owned_size] = line_total[:, :owned_size]
        own_ref[column, :, owned_size:] = jnp.sum(bias_rows, axis=0, keepdims=True)
        copies = exchange(
            "tensor",
            ranks,
            lambda p: own_ref.at[column],
            lambda p: own_ref.at[p],
            sems[8],
            sems[9],
        )
        for j in range(size):
            tall_g[j, :sequences, :] = all_g[j]
        grads = tall_g[...].reshape(size * 8, both).astype(BF)
        product = nt(grads[:, :width], w_ref[0]) + nt(grads[:, width:], w_ref[1])
        for j in range(size):
            terms[j] = product[j * 8 : j * 8 + sequences]
        copies += exchange(
            "tensor", ranks, lambda p: terms, lambda p: got_terms.at[p], sems[10], sems[11]
        )
        got_terms[column] = terms[...]
        turned = tall_s[...].reshape(size * 8, rows).T.astype(BF)
        for stream in range(2):
            mod_ref[stream] = nn(turned, grads[:, stream * width : (stream + 1) * width])
        wait_all(copies)
        total = got_terms[0]
        for t in range(1, ranks):
            total = total + got_terms[t]
        summed[...] = total
        cond_ref[place] = summed[place]
        copies = exchange(
            "dp", size, lambda p: summed.at[p], lambda p: cond_ref.at[p], sems[12], sems[13]
        )
        wait_all(copies)

    dp_sems = pltpu.SemaphoreType.DMA((size,))
    tensor_sems = pltpu.SemaphoreType.DMA((ranks,))
    return pl.pallas_call(
        body,
        in_specs=in_memory(range(5)),
        out_specs=in_memory(range(4)),
        out_shape=[
            jax.ShapeDtypeStruct((2, rows, width), F32),
            jax.ShapeDtypeStruct((size, sequences, rows), F32),
            jax.ShapeDtypeStruct((1, wide_size), F32),
            jax.ShapeDtypeStruct((ranks, 1, owned_size + both), F32),
        ],
        scratch_shapes=[
            pltpu.VMEM((ranks, sequences, both), F32),
            pltpu.VMEM((ranks, 1, wide_size), F32),
            pltpu.VMEM((size, sequences, both), F32),
            pltpu.VMEM((size, 1, line), F32),
            pltpu.VMEM((size, 8, both), F32),
            pltpu.VMEM((size, 8, rows), F32),
            pltpu.VMEM((size, sequences, rows), F32),
            pltpu.VMEM((ranks, size, sequences, rows), F32),
            pltpu.VMEM((size, sequences, rows), F32),
        ]
        + [tensor_sems] * 4
        + [dp_sems] * 4
        + [tensor_sems] * 4
        + [dp_sems] * 2,
        compiler_params=comm_params(collective_id),
        name="last_sums",
    )(grad_mod, wide, owned, weight, silu_all)


def after(value, *others):
    return lax.optimization_barrier((value,) + others)[0]


def normalize(operand):
    center = operand - jnp.mean(operand, axis=-1, keepdims=True)
    inverse = lax.rsqrt(jnp.mean(center * center, axis=-1, keepdims=True) + EPSILON)
    return (center * inverse, inverse)


def normalize_back(grad_normed, normed, inverse):
    mean_grad = jnp.mean(grad_normed, axis=-1, keepdims=True)
    mean_cross = jnp.mean(grad_normed * normed, axis=-1, keepdims=True)
    return inverse * (grad_normed - mean_grad - normed * mean_cross)


def modulate(residual, shift, scale_mod):
    normed, inverse = normalize(residual)
    lowered = (normed * (1.0 + scale_mod[:, None, :]) + shift[:, None, :]).astype(BF)
    return (normed, inverse, lowered)


def spread(image, text):
    full = lax.all_gather(jnp.concatenate([image, text], axis=1), "tensor", axis=0)
    return full.reshape((-1,) + full.shape[2:])


def collect(terms, ranks, image_rows):
    split = terms.reshape((ranks, -1) + terms.shape[1:])
    total = lax.psum_scatter(split, "tensor", scatter_dimension=0).astype(F32)
    return total[:, :image_rows], total[:, image_rows:]


def per_device(
    image_in,
    text_in,
    condition,
    mod_weight,
    qkv_weight,
    proj_weight,
    up_weight,
    down_weight,
    mod_bias,
    qkv_bias,
    proj_bias,
    up_bias,
    down_bias,
    image_cot,
    text_cot,
):
    ranks = lax.axis_size("tensor")
    column = lax.axis_index("tensor")
    sequences, image_rows, model_width = image_in.shape
    text_rows = text_in.shape[1]
    local_width = model_width // ranks
    local_inner = up_weight.shape[2]
    depth_rows = up_weight.shape[1]
    start_col = column * local_width
    start_inner = column * local_inner

    size = lax.axis_size("dp")

    raw_full = lax.all_gather(jnp.concatenate([image_in, text_in], axis=1), "tensor", axis=0)

    cond_float = condition.astype(F32)
    silu_cond = jax.nn.silu(cond_float).astype(BF).astype(F32)
    silu_parts = silu_cond.reshape(sequences, size, depth_rows).transpose(1, 0, 2)
    mod_flat = mod_weight.reshape(2, depth_rows, 6 * local_width)
    mod_bias_cols = lax.dynamic_slice_in_dim(mod_bias, start_col, local_width, 2).astype(F32)
    mod_parts, silu_all, proj_ranks = modulation_of(
        silu_parts,
        mod_flat,
        mod_bias_cols.reshape(1, 12 * local_width),
        proj_weight.transpose(0, 2, 1),
        ranks,
        0,
    )
    modulation = (
        mod_parts.reshape(ranks, sequences, 2, 6, local_width)
        .transpose(1, 2, 3, 0, 4)
        .reshape(sequences, 2, 6, model_width)
    )

    qkv_bias_cols = (
        lax.dynamic_slice_in_dim(qkv_bias, start_col, local_width, 2)
        .astype(F32)
        .transpose(1, 0, 2)[:, :, None, :]
    )
    up_bias_cols = lax.dynamic_slice_in_dim(up_bias, start_inner, local_inner, 1).astype(F32)[
        :, None, :
    ]
    proj_bias_full = proj_bias.astype(F32)
    down_bias_full = down_bias.astype(F32)

    residuals = (image_in.astype(F32), text_in.astype(F32))
    cotangents = (image_cot.astype(F32), text_cot.astype(F32))
    first_norm, first_inv = [], []
    for stream in range(2):
        normed, inverse = normalize(residuals[stream])
        first_norm.append(normed)
        first_inv.append(inverse)

    qkv_full, proj_full = gather_rows((qkv_weight.transpose(2, 0, 1, 3), proj_ranks), size, 1)
    raw_full, qkv_full = lax.optimization_barrier((raw_full, qkv_full))
    first_full = modulate_all(raw_full, modulation[:, :, :2], image_rows)
    first_full = first_full.reshape((-1,) + first_full.shape[2:])

    grad_mlp_low, down_bias_terms = [], []
    for stream in range(2):
        lowered = (modulation[:, stream, 5][:, None, :] * cotangents[stream]).astype(BF)
        grad_mlp_low.append(after(lowered, raw_full))
        down_bias_terms.append(jnp.sum(lowered.astype(F32), axis=(0, 1)))
    grad_mlp_full = spread(*grad_mlp_low)

    qkv = project_in(first_full, qkv_full, qkv_bias_cols, image_rows)
    attended, log_totals = attention(qkv, ranks)
    split = (ranks, sequences, image_rows + text_rows, local_width)
    attended_mine = lax.all_to_all(attended.reshape(split), "tensor", 0, 0)
    proj_out = project_out(attended_mine, proj_full, image_rows, F32)
    proj_sums = (proj_out[:, :image_rows], proj_out[:, image_rows:])

    attn_branches, middles, second_norm, second_inv, second_low = [], [], [], [], []
    for stream in range(2):
        attn_branch = proj_sums[stream] + proj_bias_full[stream]
        middle = residuals[stream] + modulation[:, stream, 2][:, None, :] * attn_branch
        normed, inverse, lowered = modulate(
            middle, modulation[:, stream, 3], modulation[:, stream, 4]
        )
        attn_branches.append(attn_branch)
        middles.append(middle)
        second_norm.append(normed)
        second_inv.append(inverse)
        second_low.append(lowered)
    second_low[0] = after(second_low[0], grad_mlp_full)
    second_full = spread(*second_low)
    up_shards = (up_weight, down_weight.transpose(0, 2, 1))
    up_shards = lax.optimization_barrier(up_shards + tuple(second_low))[:2]
    up_full, down_full = gather_rows(up_shards, size, 5)

    activated, slope = mlp_in(second_full, up_full, up_bias_cols, image_rows)
    down_terms = project_out(activated[None], down_full[None], image_rows)
    grad_pre = mlp_back(grad_mlp_full, down_full, slope, image_rows)
    second_sums = collect(project_out(grad_pre[None], up_full[None], image_rows), ranks, image_rows)
    down_grad, _ = weight_grad(grad_mlp_full, activated[None], image_rows)
    up_grad, up_bias_term = weight_grad(second_full, grad_pre[None], image_rows)
    (down_total,) = scatter_rows((down_grad[0],), size, 2)
    second_sums = lax.optimization_barrier(second_sums + (down_total, up_grad))[:2]

    grad_shift_two, grad_scale_two, grad_gate_one = [], [], []
    grad_middles, grad_attn_low, proj_bias_terms = [], [], []
    for stream in range(2):
        incoming = second_sums[stream]
        grad_shift_two.append(jnp.sum(incoming, axis=1))
        grad_scale_two.append(jnp.sum(incoming * second_norm[stream], axis=1))
        scaled = incoming * (1.0 + modulation[:, stream, 4][:, None, :])
        grad_middle = cotangents[stream] + normalize_back(
            scaled, second_norm[stream], second_inv[stream]
        )
        grad_middles.append(grad_middle)
        grad_gate_one.append(jnp.sum(grad_middle * attn_branches[stream], axis=1))
        lowered = (modulation[:, stream, 2][:, None, :] * grad_middle).astype(BF)
        grad_attn_low.append(lowered)
        proj_bias_terms.append(jnp.sum(lowered.astype(F32), axis=(0, 1)))
    grad_attn = jnp.concatenate(grad_attn_low, axis=1)

    down_sums = collect(after(down_terms, *second_sums), ranks, image_rows)

    grad_attended = project_in(grad_attn, proj_full, None, image_rows)
    (up_total,) = scatter_rows((after(up_grad[0], grad_attended),), size, 6)
    grad_attended = lax.all_to_all(grad_attended, "tensor", 0, 0).reshape(attended.shape)
    grad_attended = after(grad_attended, up_total)
    grad_qkv = attention_back(qkv, log_totals, attended, grad_attended, ranks)
    down_sums = lax.optimization_barrier(down_sums + (grad_qkv,))[:2]
    first_terms = project_out(grad_qkv, qkv_full, image_rows)
    first_sums = collect(after(first_terms, *down_sums), ranks, image_rows)
    proj_grad, _ = weight_grad(after(grad_attn, first_terms), attended_mine, image_rows)
    qkv_grad, qkv_bias_term = weight_grad(first_full, after(grad_qkv, first_terms), image_rows)
    grad_gate_two, outputs, stat_rows = [], [], []
    for stream in range(2):
        mlp_branch = down_sums[stream] + down_bias_full[stream]
        gated_attn = modulation[:, stream, 2][:, None, :] * attn_branches[stream]
        gated_mlp = modulation[:, stream, 5][:, None, :] * mlp_branch
        outputs.append((middles[stream] + gated_mlp).astype(BF))
        grad_gate_two.append(jnp.sum(cotangents[stream] * mlp_branch, axis=1))
        residual = residuals[stream]
        stat_rows.append(
            jnp.stack(
                [
                    jnp.sum(residual * residual, axis=(1, 2)),
                    jnp.sum(gated_attn * gated_attn, axis=(1, 2)),
                    jnp.sum(gated_mlp * gated_mlp, axis=(1, 2)),
                ],
                axis=1,
            )
        )
    stat_local = jnp.stack(stat_rows, axis=1)
    proj_total, qkv_total = scatter_rows(
        (
            proj_grad.reshape((2 * ranks,) + proj_grad.shape[2:]),
            qkv_grad.reshape((6,) + qkv_grad.shape[2:]),
        ),
        size,
        3,
    )
    proj_total = proj_total.astype(BF).reshape(ranks, 2, depth_rows, local_width)
    first_sums = lax.optimization_barrier(first_sums + (qkv_total,))[:2]
    proj_total = lax.psum_scatter(
        after(proj_total, *first_sums), "tensor", scatter_dimension=0
    ).astype(F32)
    qkv_total = qkv_total.reshape(3, 2, depth_rows, local_width)

    input_grads, grad_mod_rows = [], []
    for stream in range(2):
        incoming = first_sums[stream]
        grad_shift_one = jnp.sum(incoming, axis=1)
        grad_scale_one = jnp.sum(incoming * first_norm[stream], axis=1)
        scaled = incoming * (1.0 + modulation[:, stream, 1][:, None, :])
        input_grads.append(
            grad_middles[stream] + normalize_back(scaled, first_norm[stream], first_inv[stream])
        )
        grad_mod_rows.append(
            jnp.stack(
                [
                    grad_shift_one,
                    grad_scale_one,
                    grad_gate_one[stream],
                    grad_shift_two[stream],
                    grad_scale_two[stream],
                    grad_gate_two[stream],
                ],
                axis=1,
            )
        )
    grad_mod = jnp.stack(grad_mod_rows, axis=1)
    grad_mod_parts = (
        grad_mod.reshape(sequences, 12, ranks, local_width)
        .transpose(2, 0, 1, 3)
        .reshape(ranks, sequences, 12 * local_width)
    )
    wide = jnp.concatenate(
        [
            jnp.stack(proj_bias_terms).ravel(),
            jnp.stack(down_bias_terms).ravel(),
            stat_local.ravel(),
            jnp.zeros((128 - stat_local.size,), F32),
        ]
    )[None]
    owned = jnp.concatenate([qkv_bias_term.ravel(), up_bias_term.ravel()])[None]
    mod_total, cond_parts, wide_sum, columns = last_sums(
        grad_mod_parts, wide, owned, mod_flat, silu_all, 4
    )
    cond_total = cond_parts.transpose(1, 0, 2).reshape(sequences, model_width)
    unused_silu, silu_pull = jax.vjp(jax.nn.silu, cond_float)
    condition_grad = silu_pull(cond_total)[0]
    columns = columns[:, 0]
    qkv_size, up_size = 6 * local_width, 2 * local_inner
    qkv_bias_grad = columns[:, :qkv_size].reshape(ranks, 3, 2, local_width)
    qkv_bias_grad = qkv_bias_grad.transpose(2, 1, 0, 3).reshape(2, 3, model_width)
    up_bias_grad = columns[:, qkv_size : qkv_size + up_size].reshape(ranks, 2, local_inner)
    up_bias_grad = up_bias_grad.transpose(1, 0, 2).reshape(2, ranks * local_inner)
    mod_bias_grad = columns[:, qkv_size + up_size :].reshape(ranks, 2, 6, local_width)
    mod_bias_grad = mod_bias_grad.transpose(1, 2, 0, 3).reshape(2, 6, model_width)
    stat_totals = wide_sum[0, 4 * model_width : 4 * model_width + stat_local.size]
    stat_totals = stat_totals.reshape(stat_local.shape)
    wide_sum = wide_sum[0, : 4 * model_width].reshape(2, 2, model_width)

    row_counts = jnp.array(
        [ranks * image_rows * model_width, ranks * text_rows * model_width], F32
    ).reshape(1, 2, 1)
    rms_stats = jnp.sqrt(stat_totals / row_counts)
    return (
        outputs[0],
        outputs[1],
        input_grads[0],
        input_grads[1],
        condition_grad,
        mod_total.reshape(mod_weight.shape),
        qkv_total.transpose(1, 2, 0, 3),
        proj_total.transpose(0, 2, 1),
        up_total,
        down_total.transpose(0, 2, 1),
        mod_bias_grad,
        qkv_bias_grad,
        wide_sum[0],
        up_bias_grad,
        wide_sum[1],
        rms_stats,
    )


def solution(mesh):
    tokens = P("dp", "tensor", None)
    return jax.shard_map(
        per_device,
        mesh=mesh,
        in_specs=(
            tokens,
            tokens,
            P("dp", None),
            P(None, "dp", None, "tensor"),
            P(None, "dp", None, "tensor"),
            P(None, "tensor", "dp"),
            P(None, "dp", "tensor"),
            P(None, "tensor", "dp"),
            P(),
            P(),
            P(),
            P(),
            P(),
            tokens,
            tokens,
        ),
        out_specs=(
            tokens,
            tokens,
            tokens,
            tokens,
            P("dp", None),
            P(None, "dp", None, "tensor"),
            P(None, "dp", None, "tensor"),
            P(None, "tensor", "dp"),
            P(None, "dp", "tensor"),
            P(None, "tensor", "dp"),
            P(),
            P(),
            P(),
            P(),
            P(),
            P("dp", None, None),
        ),
        check_vma=False,
    )
```

```python
import functools

import jax
import jax.numpy as jnp
from jax import lax
from jax.experimental import pallas as pl
from jax.experimental.pallas import tpu as pltpu
from jax.sharding import PartitionSpec as P

HD = 64
EPSILON = 1e-06
LOG2E = 1.4426950408889634
SCORE = HD ** (-0.5)
VMEM_LIMIT = 56 * 1024 * 1024
BF = jnp.bfloat16
F32 = jnp.float32


def nn(a, b):
    return lax.dot_general(a, b, (((1,), (0,)), ((), ())), preferred_element_type=F32)


def nt(a, b):
    return lax.dot_general(a, b, (((1,), (1,)), ((), ())), preferred_element_type=F32)


def params():
    return pltpu.CompilerParams(vmem_limit_bytes=VMEM_LIMIT)


def resident(shape):
    zeros = (0,) * len(shape)
    return pl.BlockSpec(shape, lambda *_: zeros, pipeline_mode=pl.Buffered(1))


def tile_of(width, most=512):
    for tile in (512, 384, 256, 128):
        if tile <= most and width % tile == 0:
            return tile
    return width


def chunk_of(blocks, rows):
    count = 1
    while count * rows < 512 and blocks % (2 * count) == 0:
        count *= 2
    return count


def up_kernel(image_rows, product, finish, x_ref, w_ref, extra_refs, out_refs):
    blocks, rows, depth = x_ref.shape
    width = out_refs[0].shape[-1]
    step = chunk_of(blocks, image_rows)

    def image(i, carry):
        part = pl.ds(i * step, step)
        x = x_ref[part, :image_rows, :].reshape(step * image_rows, depth)
        results = finish(0, product(x, w_ref[0]), (part, slice(0, image_rows)), extra_refs)
        for ref, value in zip(out_refs, results):
            ref[part, :image_rows, :] = value.reshape(step, image_rows, width).astype(ref.dtype)
        return carry

    lax.fori_loop(0, blocks // step, image, 0, unroll=blocks // step)
    text_rows = rows - image_rows
    x = x_ref[:, image_rows:, :].reshape(blocks * text_rows, depth)
    results = finish(1, product(x, w_ref[1]), (slice(None), slice(image_rows, rows)), extra_refs)
    for ref, value in zip(out_refs, results):
        ref[:, image_rows:, :] = value.reshape(blocks, text_rows, width).astype(ref.dtype)


def project_in(x, weight, bias, image_rows):
    blocks, rows, depth = x.shape
    groups, width = weight.shape[0], weight.shape[3]
    tile = tile_of(width)

    extras = () if bias is None else (bias,)

    def finish(stream, value, place, extra):
        return (value + extra[0][stream] if extra else value,)

    def body(x_ref, w_ref, *refs):
        up_kernel(image_rows, nn, finish, x_ref, w_ref, refs[:-1], refs[-1:])

    return pl.pallas_call(
        body,
        grid=(groups, width // tile),
        in_specs=[
            resident((blocks, rows, depth)),
            pl.BlockSpec((None, 2, depth, tile), lambda g, n: (g, 0, 0, n)),
        ]
        + [pl.BlockSpec((None, 2, 1, tile), lambda g, n: (g, 0, 0, n)) for _ in extras],
        out_specs=pl.BlockSpec((None, blocks, rows, tile), lambda g, n: (g, 0, 0, n)),
        out_shape=jax.ShapeDtypeStruct((groups, blocks, rows, width), BF),
        compiler_params=params(),
        name="project_in",
    )(x, weight, *extras)


def mlp_in(x, weight, bias, image_rows):
    blocks, rows, depth = x.shape
    width = weight.shape[2]
    tile = tile_of(width)
    root = 0.7978845608028654

    def finish(stream, value, place, extra):
        v = value + extra[0][stream]
        square = v * v
        t = jnp.tanh(v * (root + (root * 0.044715) * square))
        half = 0.5 + 0.5 * t
        slope = half + v * (0.5 - 0.5 * t * t) * (root + (root * 3.0 * 0.044715) * square)
        return (v * half, slope)

    def body(x_ref, w_ref, b_ref, a_ref, s_ref):
        up_kernel(image_rows, nn, finish, x_ref, w_ref, (b_ref,), (a_ref, s_ref))

    spec = pl.BlockSpec((blocks, rows, tile), lambda n: (0, 0, n))
    shape = jax.ShapeDtypeStruct((blocks, rows, width), BF)
    return pl.pallas_call(
        body,
        grid=(width // tile,),
        in_specs=[
            resident((blocks, rows, depth)),
            pl.BlockSpec((2, depth, tile), lambda n: (0, 0, n)),
            pl.BlockSpec((2, 1, tile), lambda n: (0, 0, n)),
        ],
        out_specs=[spec, spec],
        out_shape=[shape, shape],
        compiler_params=params(),
        name="mlp_in",
    )(x, weight, bias)


def mlp_back(x, weight, slope, sequence, image_rows):
    blocks, rows, depth = x.shape
    width = weight.shape[2]
    tile = tile_of(width)

    def finish(stream, value, place, extra):
        factor = extra[0][place[0], place[1], :].astype(F32)
        return (value * factor.reshape(value.shape),)

    def body(x_ref, w_ref, s_ref, o_ref):
        up_kernel(image_rows, nn, finish, x_ref, w_ref, (s_ref,), (o_ref,))

    return pl.pallas_call(
        body,
        grid=(width // tile,),
        in_specs=[
            resident((blocks, rows, depth)),
            pl.BlockSpec((2, depth, tile), lambda n: (0, 0, n)),
            pl.BlockSpec((blocks, None, rows, tile), lambda n: (0, sequence, 0, n)),
        ],
        out_specs=pl.BlockSpec((blocks, rows, tile), lambda n: (0, 0, n)),
        out_shape=jax.ShapeDtypeStruct((blocks, rows, width), BF),
        compiler_params=params(),
        name="mlp_back",
    )(x, weight, slope)


def project_out(y, weight, image_rows, dtype=BF):
    groups, blocks, rows, width = y.shape
    depth = weight.shape[2]
    tile = tile_of(depth)

    def body(y_ref, w_ref, o_ref):
        step = chunk_of(blocks, image_rows)

        def image(i, carry):
            part = pl.ds(i * step, step)
            total = None
            for g in range(groups):
                y_part = y_ref[g, part, :image_rows, :].reshape(step * image_rows, width)
                term = nt(y_part, w_ref[g, 0])
                total = term if total is None else total + term
            o_ref[part, :image_rows, :] = total.reshape(step, image_rows, tile).astype(dtype)
            return carry

        lax.fori_loop(0, blocks // step, image, 0, unroll=blocks // step)
        text_rows = rows - image_rows
        total = None
        for g in range(groups):
            y_part = y_ref[g, :, image_rows:, :].reshape(blocks * text_rows, width)
            term = nt(y_part, w_ref[g, 1])
            total = term if total is None else total + term
        o_ref[:, image_rows:, :] = total.reshape(blocks, text_rows, tile).astype(dtype)

    return pl.pallas_call(
        body,
        grid=(depth // tile,),
        in_specs=[
            resident((groups, blocks, rows, width)),
            pl.BlockSpec((groups, 2, tile, width), lambda n: (0, 0, n, 0)),
        ],
        out_specs=pl.BlockSpec((blocks, rows, tile), lambda n: (0, 0, n)),
        out_shape=jax.ShapeDtypeStruct((blocks, rows, depth), dtype),
        compiler_params=params(),
        name="project_out",
    )(y, weight)


def sequence_of(array, sequence):
    return (array, sequence)


def token_spec(entry, lead, tile, place):
    array, sequence = entry
    if sequence is None:
        return pl.BlockSpec(lead + array.shape[-3:-1] + (tile,), lambda *i: place(*i, ()))
    ranks, rows = array.shape[-4], array.shape[-2]
    return pl.BlockSpec(lead + (ranks, None, rows, tile), lambda *i: place(*i, (sequence,)))


def weight_grad(parts, image_rows):
    rows, depth = parts[0][0][0].shape[-2:]
    groups, width = parts[0][1][0].shape[0], parts[0][1][0].shape[-1]
    tile = tile_of(depth, 256)
    columns = tile_of(width)
    count = len(parts)
    streams = ((0, image_rows), (image_rows, rows))

    def body(*refs):
        x_refs, y_refs, (o_ref, s_ref) = refs[:count], refs[count : 2 * count], refs[2 * count :]
        for stream, (low, high) in enumerate(streams):
            turned = []
            for x_ref in x_refs:
                tokens = x_ref.shape[0] * (high - low)
                turned.append(x_ref[:, low:high, :].reshape(tokens, tile).T)
            for n in range(width // columns):
                part = slice(n * columns, (n + 1) * columns)
                total = None
                for x, y_ref in zip(turned, y_refs):
                    y = y_ref[:, low:high, part].reshape(x.shape[1], columns)
                    term = nn(x, y)
                    total = term if total is None else total + term
                o_ref[stream, :, part] = total.astype(BF)

        @pl.when(pl.program_id(1) == 0)
        def _():
            for stream, (low, high) in enumerate(streams):
                total = jnp.zeros((high - low, width), F32)
                for y_ref in y_refs:
                    total = lax.fori_loop(
                        0,
                        y_ref.shape[0],
                        lambda i, t, ref=y_ref: t + ref[i, low:high, :].astype(F32),
                        total,
                    )
                s_ref[stream] = jnp.sum(total, axis=0, keepdims=True)

    return pl.pallas_call(
        body,
        grid=(groups, depth // tile),
        in_specs=[
            token_spec(x, (), tile, lambda g, k, q: (0,) + q + (0, k)) for x, _ in parts
        ]
        + [token_spec(y, (None,), width, lambda g, k, q: (g, 0) + q + (0, 0)) for _, y in parts],
        out_specs=[
            pl.BlockSpec((None, 2, tile, width), lambda g, k: (g, 0, k, 0)),
            pl.BlockSpec((None, 2, 1, width), lambda g, k: (g, 0, 0, 0)),
        ],
        out_shape=[
            jax.ShapeDtypeStruct((groups, 2, depth, width), BF),
            jax.ShapeDtypeStruct((groups, 2, 1, width), F32),
        ],
        compiler_params=params(),
        name="weight_grad",
    )(*[x[0] for x, _ in parts], *[y[0] for _, y in parts])


def normalize(operand):
    center = operand - jnp.mean(operand, axis=-1, keepdims=True)
    inverse = lax.rsqrt(jnp.mean(center * center, axis=-1, keepdims=True) + EPSILON)
    return (center * inverse, inverse)


def normalize_back(grad_normed, normed, inverse):
    mean_grad = jnp.mean(grad_normed, axis=-1, keepdims=True)
    mean_cross = jnp.mean(grad_normed * normed, axis=-1, keepdims=True)
    return inverse * (grad_normed - mean_grad - normed * mean_cross)


def row_pass(name, work, inputs, mods, biases, image_rows, outs, sums):
    count, rows, depth = inputs[0].shape
    sequences = mods.shape[0]
    step = 16
    streams = ((0, image_rows), (image_rows, rows))

    def body(*refs):
        refs = list(refs)
        in_refs = [refs.pop(0) for _ in inputs]
        m_ref = refs.pop(0)
        bias_refs = [refs.pop(0) for _ in biases]
        out_refs = []
        for dtype, apart in outs:
            pair = [refs.pop(0), refs.pop(0)] if apart else [refs.pop(0)] * 2
            out_refs.append((dtype, apart, pair))
        if sums:
            s_ref, acc = refs
            acc[...] = jnp.zeros_like(acc)
        for stream, (low, high) in enumerate(streams):
            steps = (high - low) // step

            def some(i, carry, stream=stream, low=low):
                start = pl.multiple_of(i * step, step)
                part = pl.ds(low + start, step)
                values = [ref[part, :].astype(F32) for ref in in_refs]
                results, terms = work(
                    stream,
                    values,
                    lambda k: m_ref[stream, k : k + 1, :],
                    [ref[stream] for ref in bias_refs],
                )
                for (dtype, apart, pair), value in zip(out_refs, results):
                    place = pl.ds(start, step) if apart else part
                    pair[stream][place, :] = value.astype(dtype)
                for k, term in enumerate(terms):
                    acc[stream, k] += term[:8] + term[8:]
                return carry

            lax.fori_loop(0, steps, some, 0, unroll=min(8, steps))
        if sums:
            for stream in range(2):
                for k in range(sums):
                    s_ref[stream, k : k + 1, :] = jnp.sum(acc[stream, k], axis=0, keepdims=True)

    def rows_spec(size):
        return pl.BlockSpec((None, size, depth), lambda n: (n, 0, 0))

    out_specs, out_shapes = [], []
    for dtype, apart in outs:
        for size in (image_rows, rows - image_rows) if apart else (rows,):
            out_specs.append(rows_spec(size))
            out_shapes.append(jax.ShapeDtypeStruct((count, size, depth), dtype))
    scratch = []
    if sums:
        out_specs.append(pl.BlockSpec((None, 2, sums, depth), lambda n: (n, 0, 0, 0)))
        out_shapes.append(jax.ShapeDtypeStruct((count, 2, sums, depth), F32))
        scratch.append(pltpu.VMEM((2, sums, 8, depth), F32))
    return pl.pallas_call(
        body,
        grid=(count,),
        in_specs=[rows_spec(rows) for _ in inputs]
        + [pl.BlockSpec((None,) + mods.shape[1:], lambda n: (lax.rem(n, sequences), 0, 0, 0))]
        + [pl.BlockSpec((2, 1, depth), lambda n: (0, 0, 0)) for _ in biases],
        out_specs=out_specs,
        out_shape=out_shapes,
        scratch_shapes=scratch,
        compiler_params=params(),
        name=name,
    )(*inputs, mods, *biases)


def work_first(stream, values, mod, biases):
    normed, _ = normalize(values[0])
    return (normed * (1.0 + mod(1)) + mod(0),), ()


def work_grad_mlp(stream, values, mod, biases):
    lowered = (mod(5) * values[0]).astype(BF)
    return (lowered,), (lowered.astype(F32),)


def middle_of(values, mod, biases):
    attn_branch = values[0] + biases[0]
    return attn_branch, values[1] + mod(2) * attn_branch


def work_second(stream, values, mod, biases):
    _, middle = middle_of(values, mod, biases)
    normed, _ = normalize(middle)
    return (normed * (1.0 + mod(4)) + mod(3),), ()


def work_middle_back(stream, values, mod, biases):
    attn_branch, middle = middle_of(values, mod, biases)
    cotangent, incoming = values[2], values[3]
    normed, inverse = normalize(middle)
    scaled = incoming * (1.0 + mod(4))
    grad_middle = cotangent + normalize_back(scaled, normed, inverse)
    lowered = (mod(2) * grad_middle).astype(BF)
    terms = (incoming, incoming * normed, grad_middle * attn_branch, lowered.astype(F32))
    return (grad_middle, lowered), terms


def work_out(stream, values, mod, biases):
    attn_branch, middle = middle_of(values, mod, biases)
    residual, cotangent = values[1], values[2]
    mlp_branch = values[3] + biases[1]
    gated_attn = mod(2) * attn_branch
    gated_mlp = mod(5) * mlp_branch
    terms = (
        cotangent * mlp_branch,
        residual * residual,
        gated_attn * gated_attn,
        gated_mlp * gated_mlp,
    )
    return (middle + gated_mlp,), terms


def work_first_back(stream, values, mod, biases):
    residual, grad_middle, incoming = values
    normed, inverse = normalize(residual)
    scaled = incoming * (1.0 + mod(1))
    grad = grad_middle + normalize_back(scaled, normed, inverse)
    return (grad,), (incoming, incoming * normed)


def head_block(width):
    return 128 if width % 128 == 0 else width


def query_tile(length):
    for tile in (384, 256, 128):
        if length % tile == 0:
            return tile
    return length


def attention(qkv, ranks):
    _, blocks, rows, width = qkv.shape
    sequences = blocks // ranks
    length = ranks * rows
    block = head_block(width)
    heads = block // HD
    tile = query_tile(length)
    view = qkv.reshape(3, ranks, sequences, rows, width)

    def body(q_ref, k_ref, v_ref, o_ref, m_ref):
        turned = []
        for h in range(heads):
            lanes = slice(h * HD, (h + 1) * HD)
            queries = q_ref[:, :, lanes].reshape(length, HD)
            keys = k_ref[:, :, lanes].reshape(length, HD)
            values = v_ref[:, :, lanes].reshape(length, HD).T
            pieces = []
            for c in range(length // tile):
                part = slice(c * tile, (c + 1) * tile)
                scores = nt(keys, queries[part])
                highest = jnp.max(scores, axis=0, keepdims=True)
                shifted = jnp.exp2((scores - highest) * (SCORE * LOG2E))
                total = jnp.sum(shifted, axis=0, keepdims=True)
                pieces.append(nn(values, shifted.astype(BF)) / total)
                m_ref[h : h + 1, part] = highest * (SCORE * LOG2E) + jnp.log2(total)
            turned.append(jnp.concatenate(pieces, axis=1))
        result = jnp.concatenate(turned, axis=0).T
        o_ref[...] = result.astype(BF).reshape(ranks, rows, block)

    def pick(j):
        return pl.BlockSpec((None, ranks, None, rows, block), lambda s, p: (j, 0, s, 0, p))

    attended, totals = pl.pallas_call(
        body,
        grid=(sequences, width // block),
        in_specs=[pick(0), pick(1), pick(2)],
        out_specs=[
            pl.BlockSpec((ranks, None, rows, block), lambda s, p: (0, s, 0, p)),
            pl.BlockSpec((None, None, heads, length), lambda s, p: (s, p, 0, 0)),
        ],
        out_shape=[
            jax.ShapeDtypeStruct((ranks, sequences, rows, width), BF),
            jax.ShapeDtypeStruct((sequences, width // block, heads, length), F32),
        ],
        compiler_params=params(),
        name="attention",
    )(view, view, view)
    return attended.reshape(blocks, rows, width), totals


def attention_back(qkv, totals, attended, grad, ranks):
    _, blocks, rows, width = qkv.shape
    sequences = blocks // ranks
    length = ranks * rows
    block = head_block(width)
    heads = block // HD
    tile = query_tile(length)
    view = qkv.reshape(3, ranks, sequences, rows, width)
    split = (ranks, sequences, rows, width)

    def body(q_ref, k_ref, v_ref, m_ref, a_ref, g_ref, o_ref):
        for h in range(heads):
            lanes = slice(h * HD, (h + 1) * HD)
            queries = q_ref[:, :, lanes].reshape(length, HD)
            keys = k_ref[:, :, lanes].reshape(length, HD)
            values = v_ref[:, :, lanes].reshape(length, HD)
            grads = g_ref[:, :, lanes].reshape(length, HD)
            attended_rows = a_ref[:, :, lanes].reshape(length, HD)
            cross = grads.astype(F32) * attended_rows.astype(F32)
            delta = jnp.sum(cross.T, axis=0, keepdims=True)
            keys_turned = keys.T
            grad_keys = jnp.zeros((length, HD), F32)
            grad_values = jnp.zeros((length, HD), F32)
            pieces = []
            for c in range(length // tile):
                part = slice(c * tile, (c + 1) * tile)
                scores = nt(keys, queries[part])
                probs = jnp.exp2(scores * (SCORE * LOG2E) - m_ref[h : h + 1, part])
                grad_probs = nt(values, grads[part])
                grad_scores = (probs * (grad_probs - delta[:, part])).astype(BF)
                grad_values = grad_values + nn(probs.astype(BF), grads[part])
                grad_keys = grad_keys + nn(grad_scores, queries[part])
                pieces.append(nn(keys_turned, grad_scores))
            grad_queries = jnp.concatenate(pieces, axis=1).T
            for j, value in enumerate((grad_queries * SCORE, grad_keys * SCORE, grad_values)):
                o_ref[j, :, :, lanes] = value.astype(BF).reshape(ranks, rows, HD)

    def pick(j):
        return pl.BlockSpec((None, ranks, None, rows, block), lambda s, p: (j, 0, s, 0, p))

    plain = pl.BlockSpec((ranks, None, rows, block), lambda s, p: (0, s, 0, p))
    out = pl.pallas_call(
        body,
        grid=(sequences, width // block),
        in_specs=[
            pick(0),
            pick(1),
            pick(2),
            pl.BlockSpec((None, None, heads, length), lambda s, p: (s, p, 0, 0)),
            plain,
            plain,
        ],
        out_specs=pl.BlockSpec((3, ranks, None, rows, block), lambda s, p: (0, 0, s, 0, p)),
        out_shape=jax.ShapeDtypeStruct((3, ranks, sequences, rows, width), BF),
        compiler_params=params(),
        name="attention_back",
    )(view, view, view, totals, attended.reshape(split), grad.reshape(split))
    return out.reshape(3, blocks, rows, width)


MESH = pl.DeviceIdType.MESH


def comm_params(collective_id):
    return pltpu.CompilerParams(
        vmem_limit_bytes=VMEM_LIMIT, collective_id=collective_id, has_side_effects=True
    )


def in_memory(shapes):
    return [pl.BlockSpec(memory_space=pltpu.VMEM) for _ in shapes]


def meet(peers):
    barrier = pltpu.get_barrier_semaphore()
    for peer in peers:
        pl.semaphore_signal(barrier, inc=1, device_id=peer, device_id_type=MESH)
    pl.semaphore_wait(barrier, len(peers))


def bit_steps(place, bits):
    core = lax.rem(place, 2)

    def flip(bit):
        return bit * (1 - 2 * lax.rem(lax.div(place, bit), 2))

    outer = bits - 1
    deltas = []
    for j in range(outer):
        low, high = flip(1 << (1 + j)), flip(1 << (outer - j))
        deltas.append(low + core * (high - low))
    return core, deltas, 1 - 2 * core


def gather_rows(arrays, size, collective_id):
    count = len(arrays)
    bits = size.bit_length() - 1
    outer = bits - 1

    def body(*refs):
        sources, targets = refs[:count], refs[count : 2 * count]
        send_sems, recv_sems, local_sems = refs[2 * count :]
        place = lax.axis_index("dp")
        core, deltas, core_delta = bit_steps(place, bits)
        steps = deltas + [core_delta]
        meet([{"dp": place + delta} for delta in steps])

        def piece(a, mask):
            index = place
            for j in range(outer):
                if mask >> j & 1:
                    index = index + deltas[j]
            rows = sources[a].shape[-2]
            lead = (slice(None),) * (len(sources[a].shape) - 2)
            start = pl.multiple_of(index * rows, rows)
            return targets[a].at[lead + (pl.ds(start, rows), slice(None))]

        def hop(a, mask, j):
            target = piece(a, mask)
            source = sources[a] if mask == 0 else target
            arrival = mask + (1 << j)
            return pltpu.make_async_remote_copy(
                src_ref=source,
                dst_ref=target,
                send_sem=send_sems.at[a, arrival],
                recv_sem=recv_sems.at[a, arrival],
                device_id={"dp": place + steps[j]},
                device_id_type=MESH,
            )

        hops = {}

        def start(a, mask, j):
            hops[a, mask + (1 << j)] = hop(a, mask, j)
            hops[a, mask + (1 << j)].start()

        locals_ = [
            pltpu.make_async_copy(sources[a], piece(a, 0), local_sems.at[a]) for a in range(count)
        ]
        for a in range(count):
            for j in range(bits):
                start(a, 0, j)
            locals_[a].start()
        for mask in range(1, 1 << outer):
            for a in range(count):
                hops[a, mask].wait_recv()
                for j in range(mask.bit_length(), bits):
                    start(a, mask, j)
        for a in range(count):
            locals_[a].wait()
            for mask in range(1, 1 << bits):
                if mask >> outer:
                    hops[a, mask].wait_recv()
                hops[a, mask].wait_send()

    shapes = [
        jax.ShapeDtypeStruct(a.shape[:-2] + (size * a.shape[-2], a.shape[-1]), a.dtype)
        for a in arrays
    ]
    return pl.pallas_call(
        body,
        in_specs=[pl.BlockSpec(memory_space=pl.ANY)] * count,
        out_specs=[pl.BlockSpec(memory_space=pl.ANY)] * count,
        out_shape=shapes,
        scratch_shapes=[
            pltpu.SemaphoreType.DMA((count, size)),
            pltpu.SemaphoreType.DMA((count, size)),
            pltpu.SemaphoreType.DMA((count,)),
        ],
        compiler_params=comm_params(collective_id),
        name="gather_rows",
    )(*arrays)


def scatter_rows(arrays, size, collective_id, dtype=F32):
    count = len(arrays)
    bits = size.bit_length() - 1
    outer = bits - 1
    half = size // 2
    dims = [(a.shape[0], a.shape[1] // size, a.shape[2]) for a in arrays]
    views = [a.reshape(g, half, 2, r, f) for a, (g, r, f) in zip(arrays, dims)]
    chunks = [(a, g) for a in range(count) for g in range(dims[a][0])]

    def body(*refs):
        sources, targets = refs[:count], refs[count : 2 * count]
        rest = list(refs[2 * count :])
        mine, met = rest[:count], rest[count : 2 * count]
        slots = [rest[(2 + j) * count : (3 + j) * count] for j in range(outer)]
        load_sems, send0, recv0, send_sems, recv_sems = rest[(2 + outer) * count :]
        place = lax.axis_index("dp")
        core, deltas, core_delta = bit_steps(place, bits)
        meet([{"dp": place + delta} for delta in deltas + [core_delta]])
        position = lax.div(place, 2)

        def shard(mask):
            index = position
            for j in range(outer):
                if mask >> j & 1:
                    index = index + lax.div(deltas[j], 2)
            return index

        loads, swaps, hops = {}, {}, {}
        for n, (a, g) in enumerate(chunks):
            swaps[n] = pltpu.make_async_remote_copy(
                src_ref=sources[a].at[g, :, 1 - core],
                dst_ref=met[a].at[g],
                send_sem=send0.at[n],
                recv_sem=recv0.at[n],
                device_id={"dp": place + core_delta},
                device_id_type=MESH,
            )
            loads[n] = pltpu.make_async_copy(
                sources[a].at[g, :, core], mine[a].at[g], load_sems.at[n]
            )
            swaps[n].start()
            loads[n].start()

        def total(n, mask, below, target):
            a, g = chunks[n]
            rows = dims[a][1]
            step = 32 if rows % 32 == 0 else 16
            k = shard(mask)

            def add(i, carry):
                part = pl.ds(pl.multiple_of(i * step, step), step)
                value = mine[a][g, k, part, :].astype(F32) + met[a][g, k, part, :].astype(F32)
                for j in range(below):
                    value = value + slots[j][a][g, mask >> (j + 1), part, :].astype(F32)
                target(a, g, k, part, value)
                return carry

            lax.fori_loop(0, rows // step, add, 0)

        def keep(a, g, k, part, value):
            met[a][g, k, part, :] = value.astype(BF)

        def finish(a, g, k, part, value):
            targets[a][g, part, :] = value.astype(dtype)

        for j in range(outer):
            for n, (a, g) in enumerate(chunks):
                if j == 0:
                    swaps[n].wait_recv()
                    loads[n].wait()
                for mask in range(1, 1 << outer):
                    if mask & ((1 << (j + 1)) - 1) != 1 << j:
                        continue
                    for i in range(j):
                        hops[n, mask | 1 << i].wait_recv()
                    total(n, mask, j, keep)
                    hops[n, mask] = pltpu.make_async_remote_copy(
                        src_ref=met[a].at[g, shard(mask)],
                        dst_ref=slots[j][a].at[g, mask >> (j + 1)],
                        send_sem=send_sems.at[n, mask],
                        recv_sem=recv_sems.at[n, mask],
                        device_id={"dp": place + deltas[j]},
                        device_id_type=MESH,
                    )
                    hops[n, mask].start()
        for n in range(len(chunks)):
            for j in range(outer):
                hops[n, 1 << j].wait_recv()
            total(n, 0, outer, finish)
        for n in range(len(chunks)):
            swaps[n].wait_send()
            for mask in range(1, 1 << outer):
                hops[n, mask].wait_send()

    scratch = []
    for repeat in range(2):
        scratch += [pltpu.VMEM((g, half, r, f), BF) for g, r, f in dims]
    for j in range(outer):
        scratch += [pltpu.VMEM((g, 1 << (outer - 1 - j), r, f), BF) for g, r, f in dims]
    total_chunks = len(chunks)
    return pl.pallas_call(
        body,
        in_specs=[pl.BlockSpec(memory_space=pl.ANY)] * count,
        out_specs=in_memory(arrays),
        out_shape=[jax.ShapeDtypeStruct(d, dtype) for d in dims],
        scratch_shapes=scratch
        + [
            pltpu.SemaphoreType.DMA((total_chunks,)),
            pltpu.SemaphoreType.DMA((total_chunks,)),
            pltpu.SemaphoreType.DMA((total_chunks,)),
            pltpu.SemaphoreType.DMA((total_chunks, half)),
            pltpu.SemaphoreType.DMA((total_chunks, half)),
        ],
        compiler_params=comm_params(collective_id),
        name="scatter_rows",
    )(*views)


def peers_of(axis, size):
    place = lax.axis_index(axis)
    return [lax.rem(place + i, size) for i in range(1, size)]


def exchange(axis, size, source, target, send_sems, recv_sems):
    place = lax.axis_index(axis)
    copies = []
    for i, peer in enumerate(peers_of(axis, size)):
        copy = pltpu.make_async_remote_copy(
            src_ref=source(peer),
            dst_ref=target(place),
            send_sem=send_sems.at[i],
            recv_sem=recv_sems.at[i],
            device_id={axis: peer},
            device_id_type=MESH,
        )
        copy.start()
        copies.append(copy)
    return copies


def wait_all(copies):
    for copy in copies:
        copy.wait_recv()
    for copy in copies:
        copy.wait_send()


def modulation_of(silu_parts, weight, bias, proj, ranks, collective_id):
    size, sequences, rows = silu_parts.shape
    width = weight.shape[2]

    def body(s_ref, w_ref, b_ref, p_ref, m_ref, all_ref, proj_ref, tall, terms, got, *sems):
        place, column = lax.axis_index("dp"), lax.axis_index("tensor")
        meet(
            [{"dp": p} for p in peers_of("dp", size)]
            + [{"tensor": p} for p in peers_of("tensor", ranks)]
        )
        copies = exchange(
            "dp", size, lambda p: s_ref.at[p], lambda p: all_ref.at[p], sems[0], sems[1]
        )
        spreads = exchange(
            "tensor", ranks, lambda p: p_ref, lambda p: proj_ref.at[p], sems[6], sems[7]
        )
        all_ref[place] = s_ref[place]
        proj_ref[column] = p_ref[...]
        tall[...] = jnp.zeros_like(tall)
        wait_all(copies)
        for j in range(size):
            tall[j, :sequences, :] = all_ref[j]
        left = tall[...].reshape(size * 8, rows).astype(BF)
        for stream in range(2):
            product = nn(left, w_ref[stream])
            for j in range(size):
                terms[j, :, stream * width : (stream + 1) * width] = product[
                    j * 8 : j * 8 + sequences
                ]
        copies = exchange(
            "dp", size, lambda p: terms.at[p], lambda p: got.at[p], sems[2], sems[3]
        )
        got[place] = terms[place]
        wait_all(copies)
        total = b_ref[...]
        for j in range(size):
            total = total + got[j]
        m_ref[column] = total.astype(BF).astype(F32)
        copies = exchange(
            "tensor",
            ranks,
            lambda p: m_ref.at[column],
            lambda p: m_ref.at[p],
            sems[4],
            sems[5],
        )
        wait_all(copies + spreads)

    dp_sems = pltpu.SemaphoreType.DMA((size,))
    tensor_sems = pltpu.SemaphoreType.DMA((ranks,))
    return pl.pallas_call(
        body,
        in_specs=in_memory(range(4)),
        out_specs=in_memory(range(3)),
        out_shape=[
            jax.ShapeDtypeStruct((ranks, sequences, 2 * width), F32),
            jax.ShapeDtypeStruct(silu_parts.shape, F32),
            jax.ShapeDtypeStruct((ranks,) + proj.shape, BF),
        ],
        scratch_shapes=[
            pltpu.VMEM((size, 8, rows), F32),
            pltpu.VMEM((size, sequences, 2 * width), F32),
            pltpu.VMEM((size, sequences, 2 * width), F32),
            dp_sems,
            dp_sems,
            dp_sems,
            dp_sems,
            tensor_sems,
            tensor_sems,
            tensor_sems,
            tensor_sems,
        ],
        compiler_params=comm_params(collective_id),
        name="modulation_of",
    )(silu_parts, weight, bias, proj)


def last_sums(grad_mod, line, stats, weight, silu_all, collective_id):
    ranks, sequences, both = grad_mod.shape
    size, _, rows = silu_all.shape
    width = both // 2
    length = line.shape[1]

    def body(
        g_ref,
        line_ref,
        stat_ref,
        w_ref,
        silu_ref,
        mod_ref,
        cond_ref,
        own_ref,
        got_g,
        all_g,
        all_line,
        tall_g,
        tall_s,
        terms,
        got_terms,
        summed,
        *sems,
    ):
        place, column = lax.axis_index("dp"), lax.axis_index("tensor")
        meet(
            [{"dp": p} for p in peers_of("dp", size)]
            + [{"tensor": p} for p in peers_of("tensor", ranks)]
        )
        copies = exchange(
            "tensor", ranks, lambda p: g_ref.at[p], lambda p: got_g.at[p], sems[0], sems[1]
        )
        lines = exchange(
            "dp", size, lambda p: line_ref, lambda p: all_line.at[p], sems[2], sems[3]
        )
        got_g[column] = g_ref[column]
        all_line[place] = line_ref[...]
        own_ref[column, :, length + both :] = stat_ref[...]
        tall_g[...] = jnp.zeros_like(tall_g)
        tall_s[...] = jnp.zeros_like(tall_s)
        for j in range(size):
            tall_s[j, :sequences, :] = silu_ref[j]
        turned = tall_s[...].reshape(size * 8, rows).T.astype(BF)
        wait_all(copies)
        total = got_g[0]
        for t in range(1, ranks):
            total = total + got_g[t]
        all_g[place] = total.astype(BF).astype(F32)
        copies = exchange(
            "dp", size, lambda p: all_g.at[place], lambda p: all_g.at[p], sems[4], sems[5]
        )
        wait_all(lines)
        line_total = all_line[0]
        for j in range(1, size):
            line_total = line_total + all_line[j]
        own_ref[column, :, :length] = line_total
        wait_all(copies)
        bias_rows = all_g[0]
        for j in range(1, size):
            bias_rows = bias_rows + all_g[j]
        own_ref[column, :, length : length + both] = jnp.sum(bias_rows, axis=0, keepdims=True)
        copies = exchange(
            "tensor",
            ranks,
            lambda p: own_ref.at[column],
            lambda p: own_ref.at[p],
            sems[6],
            sems[7],
        )
        for j in range(size):
            tall_g[j, :sequences, :] = all_g[j]
        grads = tall_g[...].reshape(size * 8, both).astype(BF)
        product = nt(grads[:, :width], w_ref[0]) + nt(grads[:, width:], w_ref[1])
        for j in range(size):
            terms[j] = product[j * 8 : j * 8 + sequences]
        copies += exchange(
            "tensor", ranks, lambda p: terms, lambda p: got_terms.at[p], sems[8], sems[9]
        )
        got_terms[column] = terms[...]
        for stream in range(2):
            mod_ref[stream] = nn(turned, grads[:, stream * width : (stream + 1) * width])
        wait_all(copies)
        total = got_terms[0]
        for t in range(1, ranks):
            total = total + got_terms[t]
        summed[...] = total
        cond_ref[place] = summed[place]
        copies = exchange(
            "dp", size, lambda p: summed.at[p], lambda p: cond_ref.at[p], sems[10], sems[11]
        )
        wait_all(copies)

    dp_sems = pltpu.SemaphoreType.DMA((size,))
    tensor_sems = pltpu.SemaphoreType.DMA((ranks,))
    return pl.pallas_call(
        body,
        in_specs=in_memory(range(5)),
        out_specs=in_memory(range(3)),
        out_shape=[
            jax.ShapeDtypeStruct((2, rows, width), F32),
            jax.ShapeDtypeStruct((size, sequences, rows), F32),
            jax.ShapeDtypeStruct((ranks, 1, length + both + 128), F32),
        ],
        scratch_shapes=[
            pltpu.VMEM((ranks, sequences, both), F32),
            pltpu.VMEM((size, sequences, both), F32),
            pltpu.VMEM((size, 1, length), F32),
            pltpu.VMEM((size, 8, both), F32),
            pltpu.VMEM((size, 8, rows), F32),
            pltpu.VMEM((size, sequences, rows), F32),
            pltpu.VMEM((ranks, size, sequences, rows), F32),
            pltpu.VMEM((size, sequences, rows), F32),
        ]
        + [tensor_sems] * 2
        + [dp_sems] * 4
        + [tensor_sems] * 4
        + [dp_sems] * 2,
        compiler_params=comm_params(collective_id),
        name="last_sums",
    )(grad_mod, line, stats, weight, silu_all)


def after(value, *others):
    return lax.optimization_barrier((value,) + others)[0]


def reduce_tokens(terms):
    return lax.psum_scatter(terms, "tensor", scatter_dimension=0)


def per_device(
    image_in,
    text_in,
    condition,
    mod_weight,
    qkv_weight,
    proj_weight,
    up_weight,
    down_weight,
    mod_bias,
    qkv_bias,
    proj_bias,
    up_bias,
    down_bias,
    image_cot,
    text_cot,
):
    ranks = lax.axis_size("tensor")
    column = lax.axis_index("tensor")
    sequences, image_rows, model_width = image_in.shape
    text_rows = text_in.shape[1]
    local_width = model_width // ranks
    local_inner = up_weight.shape[2]
    depth_rows = up_weight.shape[1]
    start_col = column * local_width
    start_inner = column * local_inner

    size = lax.axis_size("dp")

    rows = image_rows + text_rows
    tokens = (ranks, sequences, rows, model_width)

    raw = jnp.concatenate([image_in, text_in], axis=1)
    raw_full = lax.all_gather(raw, "tensor", axis=0)
    cotangent = jnp.concatenate([image_cot, text_cot], axis=1)

    cond_float = condition.astype(F32)
    silu_cond = jax.nn.silu(cond_float).astype(BF).astype(F32)
    silu_parts = silu_cond.reshape(sequences, size, depth_rows).transpose(1, 0, 2)
    mod_flat = mod_weight.reshape(2, depth_rows, 6 * local_width)
    mod_bias_cols = lax.dynamic_slice_in_dim(mod_bias, start_col, local_width, 2).astype(F32)
    mod_parts, silu_all, proj_ranks = modulation_of(
        silu_parts,
        mod_flat,
        mod_bias_cols.reshape(1, 12 * local_width),
        proj_weight.transpose(0, 2, 1),
        ranks,
        0,
    )
    modulation = (
        mod_parts.reshape(ranks, sequences, 2, 6, local_width)
        .transpose(1, 2, 3, 0, 4)
        .reshape(sequences, 2, 6, model_width)
    )

    qkv_bias_cols = (
        lax.dynamic_slice_in_dim(qkv_bias, start_col, local_width, 2)
        .astype(F32)
        .transpose(1, 0, 2)[:, :, None, :]
    )
    up_bias_cols = lax.dynamic_slice_in_dim(up_bias, start_inner, local_inner, 1).astype(F32)[
        :, None, :
    ]
    proj_bias_rows = proj_bias.astype(F32)[:, None, :]
    down_bias_rows = down_bias.astype(F32)[:, None, :]

    grad_mlp, down_bias_sums = row_pass(
        "grad_mlp", work_grad_mlp, (cotangent,), modulation, (), image_rows, ((BF, False),), 1
    )

    qkv_full, proj_full = gather_rows((qkv_weight.transpose(2, 0, 1, 3), proj_ranks), size, 1)
    raw_full, qkv_full, grad_mlp = lax.optimization_barrier((raw_full, qkv_full, grad_mlp))
    joined = (ranks * sequences, rows, model_width)
    (first_full,) = row_pass(
        "modulate_all",
        work_first,
        (raw_full.reshape(joined),),
        modulation,
        (),
        image_rows,
        ((BF, False),),
        0,
    )

    qkv = project_in(first_full, qkv_full, qkv_bias_cols, image_rows)

    grad_mlp_full = [lax.all_gather(after(grad_mlp[0], raw_full), "tensor", axis=0)]

    attended, log_totals = attention(qkv, ranks)
    split = (ranks, sequences, rows, local_width)
    attended_mine = lax.all_to_all(attended.reshape(split), "tensor", 0, 0)
    proj_out = project_out(attended_mine, proj_full, image_rows, F32)
    (second_low,) = row_pass(
        "modulate_second",
        work_second,
        (proj_out, raw),
        modulation,
        (proj_bias_rows,),
        image_rows,
        ((BF, False),),
        0,
    )
    second_full = lax.all_gather(after(second_low, grad_mlp_full[0]), "tensor", axis=0)
    up_shards = (up_weight, down_weight.transpose(0, 2, 1))
    up_shards = lax.optimization_barrier(up_shards + (second_low,))[:2]
    up_full, down_full = gather_rows(up_shards, size, 5)
    for sequence in range(1, sequences):
        late = after(grad_mlp[sequence], second_full, up_full)
        grad_mlp_full.append(lax.all_gather(late, "tensor", axis=0))

    activated, slope = mlp_in(second_full.reshape(joined), up_full, up_bias_cols, image_rows)
    wide_split = (ranks, sequences, rows, local_inner)
    slope = slope.reshape(wide_split)
    grad_pre, second_sums = [], []
    down_terms = None
    for sequence in range(sequences):
        incoming = grad_mlp_full[sequence]
        if down_terms is not None:
            incoming = after(incoming, down_terms)
        grad_pre.append(mlp_back(incoming, down_full, slope, sequence, image_rows))
        terms = project_out(grad_pre[-1][None], up_full[None], image_rows)
        second_sums.append(reduce_tokens(terms))
        if down_terms is None:
            down_terms = project_out(after(activated, terms)[None], down_full[None], image_rows)
    activated = activated.reshape((1,) + wide_split)
    down_grad, _ = weight_grad(
        [
            ((after(grad_mlp_full[q], terms), None), sequence_of(activated, q))
            for q in range(sequences)
        ],
        image_rows,
    )
    up_grad, up_bias_term = weight_grad(
        [
            (sequence_of(second_full, q), (after(grad_pre[q], terms)[None], None))
            for q in range(sequences)
        ],
        image_rows,
    )
    (down_total,) = scatter_rows((down_grad[0],), size, 2)
    second_sums = lax.optimization_barrier(tuple(second_sums) + (down_total, up_grad))[:sequences]
    second_sums = jnp.stack(second_sums)

    down_terms = after(down_terms, second_sums).reshape(tokens)
    down_sums = reduce_tokens(down_terms)
    grad_middle, grad_attn, middle_terms = row_pass(
        "middle_back",
        work_middle_back,
        (proj_out, raw, cotangent, second_sums),
        modulation,
        (proj_bias_rows,),
        image_rows,
        ((F32, False), (BF, False)),
        4,
    )
    grad_attended = project_in(grad_attn, proj_full, None, image_rows)
    proj_grad, _ = weight_grad(
        [((after(grad_attn, grad_attended), None), (attended_mine, None))], image_rows
    )
    (proj_total,) = scatter_rows(
        (proj_grad.reshape((2 * ranks,) + proj_grad.shape[2:]),), size, 6, BF
    )
    grad_attended = lax.all_to_all(grad_attended, "tensor", 0, 0).reshape(attended.shape)
    grad_attended = after(grad_attended, proj_total)
    grad_qkv = attention_back(qkv, log_totals, attended, grad_attended, ranks)
    first_terms = project_out(grad_qkv, qkv_full, image_rows).reshape(tokens)
    down_sums = after(down_sums, grad_qkv)
    first_sums = reduce_tokens(after(first_terms, down_sums))
    qkv_grad, qkv_bias_term = weight_grad(
        [((first_full, None), (after(grad_qkv, first_terms), None))], image_rows
    )
    image_out, text_out, out_terms = row_pass(
        "outputs",
        work_out,
        (proj_out, raw, cotangent, down_sums),
        modulation,
        (proj_bias_rows, down_bias_rows),
        image_rows,
        ((BF, True),),
        4,
    )
    up_total, qkv_total = scatter_rows(
        (up_grad[0], qkv_grad.reshape((6,) + qkv_grad.shape[2:])), size, 3
    )
    first_sums = lax.optimization_barrier((first_sums, qkv_total, image_out))[0]
    proj_total = proj_total.reshape(ranks, 2, depth_rows, local_width)
    proj_total = reduce_tokens(after(proj_total, first_sums))
    qkv_total = qkv_total.reshape(3, 2, depth_rows, local_width)

    image_grad, text_grad, first_terms = row_pass(
        "first_back",
        work_first_back,
        (raw, grad_middle, first_sums),
        modulation,
        (),
        image_rows,
        ((F32, True),),
        2,
    )
    grad_mod = jnp.concatenate(
        [
            first_terms,
            middle_terms[:, :, 2:3],
            middle_terms[:, :, :2],
            out_terms[:, :, :1],
        ],
        axis=2,
    )
    stat_local = jnp.sum(out_terms[:, :, 1:], axis=3)
    grad_mod_parts = (
        grad_mod.reshape(sequences, 12, ranks, local_width)
        .transpose(2, 0, 1, 3)
        .reshape(ranks, sequences, 12 * local_width)
    )
    line = jnp.concatenate(
        [
            qkv_bias_term.ravel(),
            up_bias_term.ravel(),
            jnp.sum(middle_terms[:, :, 3], axis=0).ravel(),
            jnp.sum(down_bias_sums[:, :, 0], axis=0).ravel(),
        ]
    )[None]
    stat_line = jnp.pad(stat_local.reshape(1, -1), ((0, 0), (0, 128 - stat_local.size)))
    mod_total, cond_parts, columns = last_sums(
        grad_mod_parts, line, stat_line, mod_flat, silu_all, 4
    )
    cond_total = cond_parts.transpose(1, 0, 2).reshape(sequences, model_width)
    unused_silu, silu_pull = jax.vjp(jax.nn.silu, cond_float)
    condition_grad = silu_pull(cond_total)[0]
    columns = columns[:, 0]
    qkv_size, up_size = 6 * local_width, 2 * local_inner
    wide_start = qkv_size + up_size
    mod_start = wide_start + 4 * model_width
    stat_start = mod_start + 12 * local_width
    qkv_bias_grad = columns[:, :qkv_size].reshape(ranks, 3, 2, local_width)
    qkv_bias_grad = qkv_bias_grad.transpose(2, 1, 0, 3).reshape(2, 3, model_width)
    up_bias_grad = columns[:, qkv_size:wide_start].reshape(ranks, 2, local_inner)
    up_bias_grad = up_bias_grad.transpose(1, 0, 2).reshape(2, ranks * local_inner)
    wide_sum = jnp.sum(columns[:, wide_start:mod_start], axis=0).reshape(2, 2, model_width)
    mod_bias_grad = columns[:, mod_start:stat_start].reshape(ranks, 2, 6, local_width)
    mod_bias_grad = mod_bias_grad.transpose(1, 2, 0, 3).reshape(2, 6, model_width)
    stat_totals = jnp.sum(columns[:, stat_start : stat_start + stat_local.size], axis=0)
    stat_totals = stat_totals.reshape(stat_local.shape)

    row_counts = jnp.array(
        [ranks * image_rows * model_width, ranks * text_rows * model_width], F32
    ).reshape(1, 2, 1)
    rms_stats = jnp.sqrt(stat_totals / row_counts)
    return (
        image_out,
        text_out,
        image_grad,
        text_grad,
        condition_grad,
        mod_total.reshape(mod_weight.shape),
        qkv_total.transpose(1, 2, 0, 3),
        proj_total.astype(F32).transpose(0, 2, 1),
        up_total,
        down_total.transpose(0, 2, 1),
        mod_bias_grad,
        qkv_bias_grad,
        wide_sum[0],
        up_bias_grad,
        wide_sum[1],
        rms_stats,
    )


def solution(mesh):
    tokens = P("dp", "tensor", None)
    return jax.shard_map(
        per_device,
        mesh=mesh,
        in_specs=(
            tokens,
            tokens,
            P("dp", None),
            P(None, "dp", None, "tensor"),
            P(None, "dp", None, "tensor"),
            P(None, "tensor", "dp"),
            P(None, "dp", "tensor"),
            P(None, "tensor", "dp"),
            P(),
            P(),
            P(),
            P(),
            P(),
            tokens,
            tokens,
        ),
        out_specs=(
            tokens,
            tokens,
            tokens,
            tokens,
            P("dp", None),
            P(None, "dp", None, "tensor"),
            P(None, "dp", None, "tensor"),
            P(None, "tensor", "dp"),
            P(None, "dp", "tensor"),
            P(None, "tensor", "dp"),
            P(),
            P(),
            P(),
            P(),
            P(),
            P("dp", None, None),
        ),
        check_vma=False,
    )
```

```python
import functools

import jax
import jax.numpy as jnp
from jax import lax
from jax.experimental import pallas as pl
from jax.experimental.pallas import tpu as pltpu
from jax.sharding import PartitionSpec as P

HD = 64
EPSILON = 1e-06
LOG2E = 1.4426950408889634
SCORE = HD ** (-0.5)
VMEM_LIMIT = 56 * 1024 * 1024
BF = jnp.bfloat16
F32 = jnp.float32


def nn(a, b):
    return lax.dot_general(a, b, (((1,), (0,)), ((), ())), preferred_element_type=F32)


def nt(a, b):
    return lax.dot_general(a, b, (((1,), (1,)), ((), ())), preferred_element_type=F32)


def params():
    return pltpu.CompilerParams(vmem_limit_bytes=VMEM_LIMIT)


def resident(shape):
    zeros = (0,) * len(shape)
    return pl.BlockSpec(shape, lambda *_: zeros, pipeline_mode=pl.Buffered(1))


def tile_of(width, most=512):
    for tile in (512, 384, 256, 128):
        if tile <= most and width % tile == 0:
            return tile
    return width


def chunk_of(blocks, rows):
    count = 1
    while count * rows < 512 and blocks % (2 * count) == 0:
        count *= 2
    return count


def up_kernel(image_rows, product, finish, x_ref, w_ref, extra_refs, out_refs):
    blocks, rows, depth = x_ref.shape
    width = out_refs[0].shape[-1]
    step = chunk_of(blocks, image_rows)

    def image(i, carry):
        part = pl.ds(i * step, step)
        x = x_ref[part, :image_rows, :].reshape(step * image_rows, depth)
        results = finish(0, product(x, w_ref[0]), (part, slice(0, image_rows)), extra_refs)
        for ref, value in zip(out_refs, results):
            ref[part, :image_rows, :] = value.reshape(step, image_rows, width).astype(ref.dtype)
        return carry

    lax.fori_loop(0, blocks // step, image, 0, unroll=blocks // step)
    text_rows = rows - image_rows
    x = x_ref[:, image_rows:, :].reshape(blocks * text_rows, depth)
    results = finish(1, product(x, w_ref[1]), (slice(None), slice(image_rows, rows)), extra_refs)
    for ref, value in zip(out_refs, results):
        ref[:, image_rows:, :] = value.reshape(blocks, text_rows, width).astype(ref.dtype)


def project_in(x, weight, bias, image_rows):
    blocks, rows, depth = x.shape
    groups, width = weight.shape[0], weight.shape[3]
    tile = tile_of(width)

    extras = () if bias is None else (bias,)

    def finish(stream, value, place, extra):
        return (value + extra[0][stream] if extra else value,)

    def body(x_ref, w_ref, *refs):
        up_kernel(image_rows, nn, finish, x_ref, w_ref, refs[:-1], refs[-1:])

    return pl.pallas_call(
        body,
        grid=(groups, width // tile),
        in_specs=[
            resident((blocks, rows, depth)),
            pl.BlockSpec((None, 2, depth, tile), lambda g, n: (g, 0, 0, n)),
        ]
        + [pl.BlockSpec((None, 2, 1, tile), lambda g, n: (g, 0, 0, n)) for _ in extras],
        out_specs=pl.BlockSpec((None, blocks, rows, tile), lambda g, n: (g, 0, 0, n)),
        out_shape=jax.ShapeDtypeStruct((groups, blocks, rows, width), BF),
        compiler_params=params(),
        name="project_in",
    )(x, weight, *extras)


def mlp_in(x, weight, bias, image_rows):
    blocks, rows, depth = x.shape
    width = weight.shape[2]
    tile = tile_of(width)
    root = 0.7978845608028654

    def finish(stream, value, place, extra):
        v = value + extra[0][stream]
        square = v * v
        t = jnp.tanh(v * (root + (root * 0.044715) * square))
        half = 0.5 + 0.5 * t
        slope = half + v * (0.5 - 0.5 * t * t) * (root + (root * 3.0 * 0.044715) * square)
        return (v * half, slope)

    def body(x_ref, w_ref, b_ref, a_ref, s_ref):
        up_kernel(image_rows, nn, finish, x_ref, w_ref, (b_ref,), (a_ref, s_ref))

    spec = pl.BlockSpec((blocks, rows, tile), lambda n: (0, 0, n))
    shape = jax.ShapeDtypeStruct((blocks, rows, width), BF)
    return pl.pallas_call(
        body,
        grid=(width // tile,),
        in_specs=[
            resident((blocks, rows, depth)),
            pl.BlockSpec((2, depth, tile), lambda n: (0, 0, n)),
            pl.BlockSpec((2, 1, tile), lambda n: (0, 0, n)),
        ],
        out_specs=[spec, spec],
        out_shape=[shape, shape],
        compiler_params=params(),
        name="mlp_in",
    )(x, weight, bias)


def mlp_back(x, weight, slope, sequence, image_rows):
    blocks, rows, depth = x.shape
    width = weight.shape[2]
    tile = tile_of(width)

    def finish(stream, value, place, extra):
        factor = extra[0][place[0], place[1], :].astype(F32)
        return (value * factor.reshape(value.shape),)

    def body(x_ref, w_ref, s_ref, o_ref):
        up_kernel(image_rows, nn, finish, x_ref, w_ref, (s_ref,), (o_ref,))

    return pl.pallas_call(
        body,
        grid=(width // tile,),
        in_specs=[
            resident((blocks, rows, depth)),
            pl.BlockSpec((2, depth, tile), lambda n: (0, 0, n)),
            pl.BlockSpec((blocks, None, rows, tile), lambda n: (0, sequence, 0, n)),
        ],
        out_specs=pl.BlockSpec((blocks, rows, tile), lambda n: (0, 0, n)),
        out_shape=jax.ShapeDtypeStruct((blocks, rows, width), BF),
        compiler_params=params(),
        name="mlp_back",
    )(x, weight, slope)


def project_out(y, weight, image_rows, dtype=BF):
    groups, blocks, rows, width = y.shape
    depth = weight.shape[2]
    tile = tile_of(depth)
    together = width % 128 == 0

    def product(y_rows, w_rows):
        if together:
            return nt(*[jnp.concatenate(v, axis=1) if groups > 1 else v[0] for v in (y_rows, w_rows)])
        total = nt(y_rows[0], w_rows[0])
        for g in range(1, groups):
            total = total + nt(y_rows[g], w_rows[g])
        return total

    def body(y_ref, w_ref, o_ref):
        step = chunk_of(blocks, image_rows)

        def image(i, carry):
            part = pl.ds(i * step, step)
            y_rows = [
                y_ref[g, part, :image_rows, :].reshape(step * image_rows, width)
                for g in range(groups)
            ]
            total = product(y_rows, [w_ref[g, 0] for g in range(groups)])
            o_ref[part, :image_rows, :] = total.reshape(step, image_rows, tile).astype(dtype)
            return carry

        lax.fori_loop(0, blocks // step, image, 0, unroll=blocks // step)
        text_rows = rows - image_rows
        y_rows = [
            y_ref[g, :, image_rows:, :].reshape(blocks * text_rows, width) for g in range(groups)
        ]
        total = product(y_rows, [w_ref[g, 1] for g in range(groups)])
        o_ref[:, image_rows:, :] = total.reshape(blocks, text_rows, tile).astype(dtype)

    return pl.pallas_call(
        body,
        grid=(depth // tile,),
        in_specs=[
            resident((groups, blocks, rows, width)),
            pl.BlockSpec((groups, 2, tile, width), lambda n: (0, 0, n, 0)),
        ],
        out_specs=pl.BlockSpec((blocks, rows, tile), lambda n: (0, 0, n)),
        out_shape=jax.ShapeDtypeStruct((blocks, rows, depth), dtype),
        compiler_params=params(),
        name="project_out",
    )(y, weight)


def sequence_of(array, sequence):
    return (array, sequence)


def token_spec(entry, lead, tile, place):
    array, sequence = entry
    if sequence is None:
        return pl.BlockSpec(lead + array.shape[-3:-1] + (tile,), lambda *i: place(*i, ()))
    ranks, rows = array.shape[-4], array.shape[-2]
    return pl.BlockSpec(lead + (ranks, None, rows, tile), lambda *i: place(*i, (sequence,)))


def column_pieces(groups, width):
    if width % 128:
        return [[(g, slice(0, width))] for g in range(groups)]
    runs = []
    for low in range(0, groups * width, 512):
        high = min(low + 512, groups * width)
        run = []
        while low < high:
            g, start = divmod(low, width)
            stop = min(width, start + high - low)
            run.append((g, slice(start, stop)))
            low += stop - start
        runs.append(run)
    return runs


def weight_grad(parts, image_rows):
    rows, depth = parts[0][0][0].shape[-2:]
    groups, width = parts[0][1][0].shape[0], parts[0][1][0].shape[-1]
    tile = tile_of(depth, 256)
    count = len(parts)
    streams = ((0, image_rows), (image_rows, rows))
    wide = width % 128 == 0
    out_groups, out_width = (1, groups * width) if wide else (groups, width)

    def body(*refs):
        x_refs, y_refs, (o_ref, s_ref) = refs[:count], refs[count : 2 * count], refs[2 * count :]
        for stream, (low, high) in enumerate(streams):
            turned = []
            for x_ref in x_refs:
                tokens = x_ref.shape[0] * (high - low)
                turned.append(x_ref[:, low:high, :].reshape(tokens, tile).T)
            for run in column_pieces(groups, width):
                total = None
                for x, y_ref in zip(turned, y_refs):
                    pieces = []
                    for g, part in run:
                        y = y_ref[g, :, low:high, part]
                        pieces.append(y.reshape(x.shape[1], part.stop - part.start))
                    y = jnp.concatenate(pieces, axis=1) if len(pieces) > 1 else pieces[0]
                    term = nn(x, y)
                    total = term if total is None else total + term
                g, part = run[0]
                start = g * width + part.start if wide else 0
                place = slice(start, start + total.shape[1])
                o_ref[0 if wide else g, stream, :, place] = total.astype(BF)

        @pl.when(pl.program_id(0) == 0)
        def _():
            for stream, (low, high) in enumerate(streams):
                for g in range(groups):
                    total = jnp.zeros((high - low, width), F32)
                    for y_ref in y_refs:
                        total = lax.fori_loop(
                            0,
                            y_ref.shape[1],
                            lambda i, t, ref=y_ref, g=g: t + ref[g, i, low:high, :].astype(F32),
                            total,
                        )
                    s_ref[g, stream] = jnp.sum(total, axis=0, keepdims=True)

    grad, sums = pl.pallas_call(
        body,
        grid=(depth // tile,),
        in_specs=[token_spec(x, (), tile, lambda k, q: (0,) + q + (0, k)) for x, _ in parts]
        + [
            token_spec(y, (groups,), width, lambda k, q: (0, 0) + q + (0, 0)) for _, y in parts
        ],
        out_specs=[
            pl.BlockSpec((out_groups, 2, tile, out_width), lambda k: (0, 0, k, 0)),
            pl.BlockSpec((groups, 2, 1, width), lambda k: (0, 0, 0, 0)),
        ],
        out_shape=[
            jax.ShapeDtypeStruct((out_groups, 2, depth, out_width), BF),
            jax.ShapeDtypeStruct((groups, 2, 1, width), F32),
        ],
        compiler_params=params(),
        name="weight_grad",
    )(*[x[0] for x, _ in parts], *[y[0] for _, y in parts])
    return grad.reshape((2 * out_groups, depth, out_width)), sums


def by_group(total, groups):
    count, rows, width = total.shape
    if count == 2:
        return total.reshape(2, rows, groups, width // groups).transpose(2, 0, 1, 3)
    return total.reshape(groups, 2, rows, width)


def normalize(operand):
    center = operand - jnp.mean(operand, axis=-1, keepdims=True)
    inverse = lax.rsqrt(jnp.mean(center * center, axis=-1, keepdims=True) + EPSILON)
    return (center * inverse, inverse)


def normalize_back(grad_normed, normed, inverse):
    mean_grad = jnp.mean(grad_normed, axis=-1, keepdims=True)
    mean_cross = jnp.mean(grad_normed * normed, axis=-1, keepdims=True)
    return inverse * (grad_normed - mean_grad - normed * mean_cross)


def row_pass(name, work, inputs, mods, biases, image_rows, outs, sums):
    count, rows, depth = inputs[0].shape
    sequences = mods.shape[0]
    step = 16
    streams = ((0, image_rows), (image_rows, rows))
    apart_inputs = any(isinstance(entry, tuple) for entry in inputs)

    def body(*refs):
        refs = list(refs)
        in_refs = []
        for entry in inputs:
            many = len(entry) if isinstance(entry, tuple) else 1
            in_refs.append([refs.pop(0) for _ in range(many)])
        m_ref = refs.pop(0)
        bias_refs = [refs.pop(0) for _ in biases]
        out_refs = []
        for dtype, apart in outs:
            pair = [refs.pop(0), refs.pop(0)] if apart else [refs.pop(0)] * 2
            out_refs.append((dtype, apart, pair))
        if sums:
            s_ref, acc = refs
            acc[...] = jnp.zeros_like(acc)

        def run(row_refs):
            for stream, (low, high) in enumerate(streams):
                steps = (high - low) // step

                def some(i, carry, stream=stream, low=low):
                    start = pl.multiple_of(i * step, step)
                    part = pl.ds(low + start, step)
                    values = [ref[part, :].astype(F32) for ref in row_refs]
                    results, terms = work(
                        stream,
                        values,
                        lambda k: m_ref[stream, k : k + 1, :],
                        [ref[stream] for ref in bias_refs],
                    )
                    for (dtype, apart, pair), value in zip(out_refs, results):
                        place = pl.ds(start, step) if apart else part
                        pair[stream][place, :] = value.astype(dtype)
                    for k, term in enumerate(terms):
                        acc[stream, k] += term[:8] + term[8:]
                    return carry

                lax.fori_loop(0, steps, some, 0, unroll=min(8, steps))

        if apart_inputs:
            for n in range(count):
                pl.when(pl.program_id(0) == n)(
                    functools.partial(run, [r[n] if len(r) > 1 else r[0] for r in in_refs])
                )
        else:
            run([r[0] for r in in_refs])
        if sums:
            for stream in range(2):
                for k in range(sums):
                    s_ref[stream, k : k + 1, :] = jnp.sum(acc[stream, k], axis=0, keepdims=True)

    def rows_spec(size):
        return pl.BlockSpec((None, size, depth), lambda n: (n, 0, 0))

    in_specs, operands = [], []
    for entry in inputs:
        if isinstance(entry, tuple):
            in_specs += [pl.BlockSpec((rows, depth), lambda n: (0, 0)) for _ in entry]
            operands += list(entry)
        else:
            in_specs.append(rows_spec(rows))
            operands.append(entry)
    out_specs, out_shapes = [], []
    for dtype, apart in outs:
        for size in (image_rows, rows - image_rows) if apart else (rows,):
            out_specs.append(rows_spec(size))
            out_shapes.append(jax.ShapeDtypeStruct((count, size, depth), dtype))
    scratch = []
    if sums:
        out_specs.append(pl.BlockSpec((None, 2, sums, depth), lambda n: (n, 0, 0, 0)))
        out_shapes.append(jax.ShapeDtypeStruct((count, 2, sums, depth), F32))
        scratch.append(pltpu.VMEM((2, sums, 8, depth), F32))
    return pl.pallas_call(
        body,
        grid=(count,),
        in_specs=in_specs
        + [pl.BlockSpec((None,) + mods.shape[1:], lambda n: (lax.rem(n, sequences), 0, 0, 0))]
        + [pl.BlockSpec((2, 1, depth), lambda n: (0, 0, 0)) for _ in biases],
        out_specs=out_specs,
        out_shape=out_shapes,
        scratch_shapes=scratch,
        compiler_params=params(),
        name=name,
    )(*operands, mods, *biases)


def work_first(stream, values, mod, biases):
    normed, _ = normalize(values[0])
    return (normed * (1.0 + mod(1)) + mod(0), normed), ()


def work_grad_mlp(stream, values, mod, biases):
    lowered = (mod(5) * values[0]).astype(BF)
    return (lowered,), (lowered.astype(F32),)


def middle_of(values, mod, biases):
    attn_branch = values[0] + biases[0]
    return attn_branch, values[1] + mod(2) * attn_branch


def work_second(stream, values, mod, biases):
    _, middle = middle_of(values, mod, biases)
    normed, _ = normalize(middle)
    return (normed * (1.0 + mod(4)) + mod(3),), ()


def work_middle_back(stream, values, mod, biases):
    attn_branch, middle = middle_of(values, mod, biases)
    cotangent, incoming = values[2], values[3]
    normed, inverse = normalize(middle)
    scaled = incoming * (1.0 + mod(4))
    grad_middle = cotangent + normalize_back(scaled, normed, inverse)
    lowered = (mod(2) * grad_middle).astype(BF)
    terms = (incoming, incoming * normed, grad_middle * attn_branch, lowered.astype(F32))
    return (grad_middle, lowered), terms


def work_out(stream, values, mod, biases):
    attn_branch, middle = middle_of(values, mod, biases)
    residual, cotangent = values[1], values[2]
    mlp_branch = values[3] + biases[1]
    gated_attn = mod(2) * attn_branch
    gated_mlp = mod(5) * mlp_branch
    terms = (
        cotangent * mlp_branch,
        residual * residual,
        gated_attn * gated_attn,
        gated_mlp * gated_mlp,
    )
    return (middle + gated_mlp,), terms


def work_first_back(stream, values, mod, biases):
    residual, grad_middle, incoming = values
    normed, inverse = normalize(residual)
    scaled = incoming * (1.0 + mod(1))
    return (grad_middle + normalize_back(scaled, normed, inverse),), ()


def work_first_sums(stream, values, mod, biases):
    return (), (values[1], values[1] * values[0])


def head_block(width):
    return 128 if width % 128 == 0 else width


def query_parts(length):
    tile = next((t for t in (384, 256, 128) if length % t == 0), length)
    return [slice(low, low + tile) for low in range(0, length, tile)]


def attention(qkv, ranks):
    _, blocks, rows, width = qkv.shape
    sequences = blocks // ranks
    length = ranks * rows
    block = head_block(width)
    heads = block // HD
    parts = query_parts(length)
    view = qkv.reshape(3, ranks, sequences, rows, width)

    def body(q_ref, k_ref, v_ref, o_ref, m_ref):
        turned = []
        for h in range(heads):
            lanes = slice(h * HD, (h + 1) * HD)
            queries = q_ref[:, :, lanes].reshape(length, HD)
            keys = k_ref[:, :, lanes].reshape(length, HD)
            values = v_ref[:, :, lanes].reshape(length, HD).T
            pieces = []
            for part in parts:
                scores = nt(keys, queries[part])
                highest = jnp.max(scores, axis=0, keepdims=True)
                shifted = jnp.exp2((scores - highest) * (SCORE * LOG2E))
                total = jnp.sum(shifted, axis=0, keepdims=True)
                pieces.append(nn(values, shifted.astype(BF)) / total)
                m_ref[h : h + 1, part] = highest * (SCORE * LOG2E) + jnp.log2(total)
            turned.append(jnp.concatenate(pieces, axis=1))
        result = jnp.concatenate(turned, axis=0).T
        o_ref[...] = result.astype(BF).reshape(ranks, rows, block)

    def pick(j):
        return pl.BlockSpec((None, ranks, None, rows, block), lambda s, p: (j, 0, s, 0, p))

    attended, totals = pl.pallas_call(
        body,
        grid=(sequences, width // block),
        in_specs=[pick(0), pick(1), pick(2)],
        out_specs=[
            pl.BlockSpec((ranks, None, rows, block), lambda s, p: (0, s, 0, p)),
            pl.BlockSpec((None, None, heads, length), lambda s, p: (s, p, 0, 0)),
        ],
        out_shape=[
            jax.ShapeDtypeStruct((ranks, sequences, rows, width), BF),
            jax.ShapeDtypeStruct((sequences, width // block, heads, length), F32),
        ],
        compiler_params=params(),
        name="attention",
    )(view, view, view)
    return attended.reshape(blocks, rows, width), totals


def attention_back(qkv, totals, attended, grad, ranks):
    _, blocks, rows, width = qkv.shape
    sequences = blocks // ranks
    length = ranks * rows
    block = head_block(width)
    heads = block // HD
    parts = query_parts(length)
    view = qkv.reshape(3, ranks, sequences, rows, width)
    split = (ranks, sequences, rows, width)

    def body(q_ref, k_ref, v_ref, m_ref, a_ref, g_ref, o_ref):
        for h in range(heads):
            lanes = slice(h * HD, (h + 1) * HD)
            queries = q_ref[:, :, lanes].reshape(length, HD)
            keys = k_ref[:, :, lanes].reshape(length, HD)
            values = v_ref[:, :, lanes].reshape(length, HD)
            grads = g_ref[:, :, lanes].reshape(length, HD)
            attended_rows = a_ref[:, :, lanes].reshape(length, HD)
            cross = grads.astype(F32) * attended_rows.astype(F32)
            delta = jnp.sum(cross.T, axis=0, keepdims=True)
            keys_turned = keys.T
            grad_keys = jnp.zeros((length, HD), F32)
            grad_values = jnp.zeros((length, HD), F32)
            pieces = []
            for part in parts:
                scores = nt(keys, queries[part])
                probs = jnp.exp2(scores * (SCORE * LOG2E) - m_ref[h : h + 1, part])
                grad_probs = nt(values, grads[part])
                grad_scores = (probs * (grad_probs - delta[:, part])).astype(BF)
                grad_values = grad_values + nn(probs.astype(BF), grads[part])
                grad_keys = grad_keys + nn(grad_scores, queries[part])
                pieces.append(nn(keys_turned, grad_scores))
            grad_queries = jnp.concatenate(pieces, axis=1).T
            for j, value in enumerate((grad_queries * SCORE, grad_keys * SCORE, grad_values)):
                o_ref[j, :, :, lanes] = value.astype(BF).reshape(ranks, rows, HD)

    def pick(j):
        return pl.BlockSpec((None, ranks, None, rows, block), lambda s, p: (j, 0, s, 0, p))

    plain = pl.BlockSpec((ranks, None, rows, block), lambda s, p: (0, s, 0, p))
    out = pl.pallas_call(
        body,
        grid=(sequences, width // block),
        in_specs=[
            pick(0),
            pick(1),
            pick(2),
            pl.BlockSpec((None, None, heads, length), lambda s, p: (s, p, 0, 0)),
            plain,
            plain,
        ],
        out_specs=pl.BlockSpec((3, ranks, None, rows, block), lambda s, p: (0, 0, s, 0, p)),
        out_shape=jax.ShapeDtypeStruct((3, ranks, sequences, rows, width), BF),
        compiler_params=params(),
        name="attention_back",
    )(view, view, view, totals, attended.reshape(split), grad.reshape(split))
    return out.reshape(3, blocks, rows, width)


MESH = pl.DeviceIdType.MESH


def comm_params(collective_id):
    return pltpu.CompilerParams(
        vmem_limit_bytes=VMEM_LIMIT, collective_id=collective_id, has_side_effects=True
    )


def in_memory(shapes):
    return [pl.BlockSpec(memory_space=pltpu.VMEM) for _ in shapes]


def meet(peers):
    barrier = pltpu.get_barrier_semaphore()
    for peer in peers:
        pl.semaphore_signal(barrier, inc=1, device_id=peer, device_id_type=MESH)
    pl.semaphore_wait(barrier, len(peers))


def bit_steps(place, bits):
    core = lax.rem(place, 2)

    def flip(bit):
        return bit * (1 - 2 * lax.rem(lax.div(place, bit), 2))

    outer = bits - 1
    deltas = []
    for j in range(outer):
        low, high = flip(1 << (1 + j)), flip(1 << (outer - j))
        deltas.append(low + core * (high - low))
    return core, deltas, 1 - 2 * core


def gather_rows(arrays, size, collective_id):
    count = len(arrays)
    bits = size.bit_length() - 1
    outer = bits - 1

    def body(*refs):
        sources, targets = refs[:count], refs[count : 2 * count]
        send_sems, recv_sems, local_sems = refs[2 * count :]
        place = lax.axis_index("dp")
        core, deltas, core_delta = bit_steps(place, bits)
        steps = deltas + [core_delta]
        meet([{"dp": place + delta} for delta in steps])

        def piece(a, mask):
            index = place
            for j in range(outer):
                if mask >> j & 1:
                    index = index + deltas[j]
            rows = sources[a].shape[-2]
            lead = (slice(None),) * (len(sources[a].shape) - 2)
            start = pl.multiple_of(index * rows, rows)
            return targets[a].at[lead + (pl.ds(start, rows), slice(None))]

        def hop(a, mask, j):
            target = piece(a, mask)
            source = sources[a] if mask == 0 else target
            arrival = mask + (1 << j)
            return pltpu.make_async_remote_copy(
                src_ref=source,
                dst_ref=target,
                send_sem=send_sems.at[a, arrival],
                recv_sem=recv_sems.at[a, arrival],
                device_id={"dp": place + steps[j]},
                device_id_type=MESH,
            )

        hops = {}

        def start(a, mask, j):
            hops[a, mask + (1 << j)] = hop(a, mask, j)
            hops[a, mask + (1 << j)].start()

        locals_ = [
            pltpu.make_async_copy(sources[a], piece(a, 0), local_sems.at[a]) for a in range(count)
        ]
        for a in range(count):
            for j in range(bits):
                start(a, 0, j)
            locals_[a].start()
        for mask in range(1, 1 << outer):
            for a in range(count):
                hops[a, mask].wait_recv()
                for j in range(mask.bit_length(), bits):
                    start(a, mask, j)
        for a in range(count):
            locals_[a].wait()
            for mask in range(1, 1 << bits):
                if mask >> outer:
                    hops[a, mask].wait_recv()
                hops[a, mask].wait_send()

    shapes = [
        jax.ShapeDtypeStruct(a.shape[:-2] + (size * a.shape[-2], a.shape[-1]), a.dtype)
        for a in arrays
    ]
    return pl.pallas_call(
        body,
        in_specs=[pl.BlockSpec(memory_space=pl.ANY)] * count,
        out_specs=[pl.BlockSpec(memory_space=pl.ANY)] * count,
        out_shape=shapes,
        scratch_shapes=[
            pltpu.SemaphoreType.DMA((count, size)),
            pltpu.SemaphoreType.DMA((count, size)),
            pltpu.SemaphoreType.DMA((count,)),
        ],
        compiler_params=comm_params(collective_id),
        name="gather_rows",
    )(*arrays)


def scatter_rows(arrays, size, collective_id, dtypes):
    count = len(arrays)
    bits = size.bit_length() - 1
    outer = bits - 1
    half = size // 2
    dims = [(a.shape[0], a.shape[1] // size, a.shape[2]) for a in arrays]
    views = [a.reshape(g, half, 2, r, f) for a, (g, r, f) in zip(arrays, dims)]
    chunks = [(a, g) for a in range(count) for g in range(dims[a][0])]

    def body(*refs):
        sources, targets = refs[:count], refs[count : 2 * count]
        rest = list(refs[2 * count :])
        mine, met = rest[:count], rest[count : 2 * count]
        slots = [rest[(2 + j) * count : (3 + j) * count] for j in range(outer)]
        load_sems, send0, recv0, send_sems, recv_sems = rest[(2 + outer) * count :]
        place = lax.axis_index("dp")
        core, deltas, core_delta = bit_steps(place, bits)
        meet([{"dp": place + delta} for delta in deltas + [core_delta]])
        position = lax.div(place, 2)

        def shard(mask):
            index = position
            for j in range(outer):
                if mask >> j & 1:
                    index = index + lax.div(deltas[j], 2)
            return index

        def mirrored(mask):
            return sum(1 << (outer - 1 - j) for j in range(outer) if mask >> j & 1)

        loads, swaps, hops = {}, {}, {}
        first_needed = sorted(range(half), key=lambda m: (m & -m) or half)
        for mask in first_needed:
            for n, (a, g) in enumerate(chunks):
                theirs = shard(mirrored(mask))
                swaps[n, mask] = pltpu.make_async_remote_copy(
                    src_ref=sources[a].at[g, theirs, 1 - core],
                    dst_ref=met[a].at[g, theirs],
                    send_sem=send0.at[n, mask],
                    recv_sem=recv0.at[n, mask],
                    device_id={"dp": place + core_delta},
                    device_id_type=MESH,
                )
                loads[n, mask] = pltpu.make_async_copy(
                    sources[a].at[g, shard(mask), core],
                    mine[a].at[g, shard(mask)],
                    load_sems.at[n, mask],
                )
                swaps[n, mask].start()
                loads[n, mask].start()

        def total(n, mask, below, target):
            a, g = chunks[n]
            rows = dims[a][1]
            step = 32 if rows % 32 == 0 else 16
            k = shard(mask)

            def add(i, carry):
                part = pl.ds(pl.multiple_of(i * step, step), step)
                value = mine[a][g, k, part, :].astype(F32) + met[a][g, k, part, :].astype(F32)
                for j in range(below):
                    value = value + slots[j][a][g, mask >> (j + 1), part, :].astype(F32)
                target(a, g, k, part, value)
                return carry

            lax.fori_loop(0, rows // step, add, 0)

        def keep(a, g, k, part, value):
            met[a][g, k, part, :] = value.astype(BF)

        def finish(a, g, k, part, value):
            targets[a][g, part, :] = value.astype(dtypes[a])

        for j in range(outer):
            for n, (a, g) in enumerate(chunks):
                for mask in range(1, 1 << outer):
                    if mask & ((1 << (j + 1)) - 1) != 1 << j:
                        continue
                    swaps[n, mask].wait_recv()
                    loads[n, mask].wait()
                    for i in range(j):
                        hops[n, mask | 1 << i].wait_recv()
                    total(n, mask, j, keep)
                    hops[n, mask] = pltpu.make_async_remote_copy(
                        src_ref=met[a].at[g, shard(mask)],
                        dst_ref=slots[j][a].at[g, mask >> (j + 1)],
                        send_sem=send_sems.at[n, mask],
                        recv_sem=recv_sems.at[n, mask],
                        device_id={"dp": place + deltas[j]},
                        device_id_type=MESH,
                    )
                    hops[n, mask].start()
        for n in range(len(chunks)):
            swaps[n, 0].wait_recv()
            loads[n, 0].wait()
            for j in range(outer):
                hops[n, 1 << j].wait_recv()
            total(n, 0, outer, finish)
        for n in range(len(chunks)):
            for mask in range(half):
                swaps[n, mask].wait_send()
            for mask in range(1, 1 << outer):
                hops[n, mask].wait_send()

    scratch = []
    for repeat in range(2):
        scratch += [pltpu.VMEM((g, half, r, f), BF) for g, r, f in dims]
    for j in range(outer):
        scratch += [pltpu.VMEM((g, 1 << (outer - 1 - j), r, f), BF) for g, r, f in dims]
    total_chunks = len(chunks)
    return pl.pallas_call(
        body,
        in_specs=[pl.BlockSpec(memory_space=pl.ANY)] * count,
        out_specs=in_memory(arrays),
        out_shape=[jax.ShapeDtypeStruct(d, t) for d, t in zip(dims, dtypes)],
        scratch_shapes=scratch
        + [
            pltpu.SemaphoreType.DMA((total_chunks, half)),
            pltpu.SemaphoreType.DMA((total_chunks, half)),
            pltpu.SemaphoreType.DMA((total_chunks, half)),
            pltpu.SemaphoreType.DMA((total_chunks, half)),
            pltpu.SemaphoreType.DMA((total_chunks, half)),
        ],
        compiler_params=comm_params(collective_id),
        name="scatter_rows",
    )(*views)


def peers_of(axis, size):
    place = lax.axis_index(axis)
    return [lax.rem(place + i, size) for i in range(1, size)]


def exchange(axis, size, source, target, send_sems, recv_sems):
    place = lax.axis_index(axis)
    copies = []
    for i, peer in enumerate(peers_of(axis, size)):
        copy = pltpu.make_async_remote_copy(
            src_ref=source(peer),
            dst_ref=target(place),
            send_sem=send_sems.at[i],
            recv_sem=recv_sems.at[i],
            device_id={axis: peer},
            device_id_type=MESH,
        )
        copy.start()
        copies.append(copy)
    return copies


def wait_all(copies):
    for copy in copies:
        copy.wait_recv()
    for copy in copies:
        copy.wait_send()


def modulation_of(silu_parts, weight, bias, proj, ranks, collective_id):
    size, sequences, rows = silu_parts.shape
    width = weight.shape[2]

    def body(s_ref, w_ref, b_ref, p_ref, m_ref, all_ref, proj_ref, tall, terms, got, *sems):
        place, column = lax.axis_index("dp"), lax.axis_index("tensor")
        meet(
            [{"dp": p} for p in peers_of("dp", size)]
            + [{"tensor": p} for p in peers_of("tensor", ranks)]
        )
        copies = exchange(
            "dp", size, lambda p: s_ref.at[p], lambda p: all_ref.at[p], sems[0], sems[1]
        )
        spreads = exchange(
            "tensor", ranks, lambda p: p_ref, lambda p: proj_ref.at[p], sems[6], sems[7]
        )
        all_ref[place] = s_ref[place]
        proj_ref[column] = p_ref[...]
        tall[...] = jnp.zeros_like(tall)
        wait_all(copies)
        for j in range(size):
            tall[j, :sequences, :] = all_ref[j]
        left = tall[...].reshape(size * 8, rows).astype(BF)
        for stream in range(2):
            product = nn(left, w_ref[stream])
            for j in range(size):
                terms[j, :, stream * width : (stream + 1) * width] = product[
                    j * 8 : j * 8 + sequences
                ]
        copies = exchange(
            "dp", size, lambda p: terms.at[p], lambda p: got.at[p], sems[2], sems[3]
        )
        got[place] = terms[place]
        wait_all(copies)
        total = b_ref[...]
        for j in range(size):
            total = total + got[j]
        m_ref[column] = total.astype(BF).astype(F32)
        copies = exchange(
            "tensor",
            ranks,
            lambda p: m_ref.at[column],
            lambda p: m_ref.at[p],
            sems[4],
            sems[5],
        )
        wait_all(copies + spreads)

    dp_sems = pltpu.SemaphoreType.DMA((size,))
    tensor_sems = pltpu.SemaphoreType.DMA((ranks,))
    return pl.pallas_call(
        body,
        in_specs=in_memory(range(4)),
        out_specs=in_memory(range(3)),
        out_shape=[
            jax.ShapeDtypeStruct((ranks, sequences, 2 * width), F32),
            jax.ShapeDtypeStruct(silu_parts.shape, F32),
            jax.ShapeDtypeStruct((ranks,) + proj.shape, BF),
        ],
        scratch_shapes=[
            pltpu.VMEM((size, 8, rows), F32),
            pltpu.VMEM((size, sequences, 2 * width), F32),
            pltpu.VMEM((size, sequences, 2 * width), F32),
            dp_sems,
            dp_sems,
            dp_sems,
            dp_sems,
            tensor_sems,
            tensor_sems,
            tensor_sems,
            tensor_sems,
        ],
        compiler_params=comm_params(collective_id),
        name="modulation_of",
    )(silu_parts, weight, bias, proj)


def last_sums(grad_mod, line, stats, weight, silu_all, collective_id):
    ranks, sequences, both = grad_mod.shape
    size, _, rows = silu_all.shape
    width = both // 2
    length = line.shape[1]

    def body(
        g_ref,
        line_ref,
        stat_ref,
        w_ref,
        silu_ref,
        mod_ref,
        cond_ref,
        own_ref,
        got_g,
        all_g,
        all_line,
        tall_g,
        tall_s,
        terms,
        got_terms,
        summed,
        *sems,
    ):
        place, column = lax.axis_index("dp"), lax.axis_index("tensor")
        meet(
            [{"dp": p} for p in peers_of("dp", size)]
            + [{"tensor": p} for p in peers_of("tensor", ranks)]
        )
        copies = exchange(
            "tensor", ranks, lambda p: g_ref.at[p], lambda p: got_g.at[p], sems[0], sems[1]
        )
        lines = exchange(
            "dp", size, lambda p: line_ref, lambda p: all_line.at[p], sems[2], sems[3]
        )
        got_g[column] = g_ref[column]
        all_line[place] = line_ref[...]
        own_ref[column, :, length + both :] = stat_ref[...]
        tall_g[...] = jnp.zeros_like(tall_g)
        tall_s[...] = jnp.zeros_like(tall_s)
        for j in range(size):
            tall_s[j, :sequences, :] = silu_ref[j]
        turned = tall_s[...].reshape(size * 8, rows).T.astype(BF)
        wait_all(copies)
        total = got_g[0]
        for t in range(1, ranks):
            total = total + got_g[t]
        all_g[place] = total.astype(BF).astype(F32)
        copies = exchange(
            "dp", size, lambda p: all_g.at[place], lambda p: all_g.at[p], sems[4], sems[5]
        )
        wait_all(lines)
        line_total = all_line[0]
        for j in range(1, size):
            line_total = line_total + all_line[j]
        own_ref[column, :, :length] = line_total
        wait_all(copies)
        bias_rows = all_g[0]
        for j in range(1, size):
            bias_rows = bias_rows + all_g[j]
        own_ref[column, :, length : length + both] = jnp.sum(bias_rows, axis=0, keepdims=True)
        copies = exchange(
            "tensor",
            ranks,
            lambda p: own_ref.at[column],
            lambda p: own_ref.at[p],
            sems[6],
            sems[7],
        )
        for j in range(size):
            tall_g[j, :sequences, :] = all_g[j]
        grads = tall_g[...].reshape(size * 8, both).astype(BF)
        product = nt(grads[:, :width], w_ref[0]) + nt(grads[:, width:], w_ref[1])
        for j in range(size):
            terms[j] = product[j * 8 : j * 8 + sequences]
        copies += exchange(
            "tensor", ranks, lambda p: terms, lambda p: got_terms.at[p], sems[8], sems[9]
        )
        got_terms[column] = terms[...]
        for stream in range(2):
            mod_ref[stream] = nn(turned, grads[:, stream * width : (stream + 1) * width])
        wait_all(copies)
        total = got_terms[0]
        for t in range(1, ranks):
            total = total + got_terms[t]
        summed[...] = total
        cond_ref[place] = summed[place]
        copies = exchange(
            "dp", size, lambda p: summed.at[p], lambda p: cond_ref.at[p], sems[10], sems[11]
        )
        wait_all(copies)

    dp_sems = pltpu.SemaphoreType.DMA((size,))
    tensor_sems = pltpu.SemaphoreType.DMA((ranks,))
    return pl.pallas_call(
        body,
        in_specs=in_memory(range(5)),
        out_specs=in_memory(range(3)),
        out_shape=[
            jax.ShapeDtypeStruct((2, rows, width), F32),
            jax.ShapeDtypeStruct((size, sequences, rows), F32),
            jax.ShapeDtypeStruct((ranks, 1, length + both + 128), F32),
        ],
        scratch_shapes=[
            pltpu.VMEM((ranks, sequences, both), F32),
            pltpu.VMEM((size, sequences, both), F32),
            pltpu.VMEM((size, 1, length), F32),
            pltpu.VMEM((size, 8, both), F32),
            pltpu.VMEM((size, 8, rows), F32),
            pltpu.VMEM((size, sequences, rows), F32),
            pltpu.VMEM((ranks, size, sequences, rows), F32),
            pltpu.VMEM((size, sequences, rows), F32),
        ]
        + [tensor_sems] * 2
        + [dp_sems] * 4
        + [tensor_sems] * 4
        + [dp_sems] * 2,
        compiler_params=comm_params(collective_id),
        name="last_sums",
    )(grad_mod, line, stats, weight, silu_all)


def after(value, *others):
    return lax.optimization_barrier((value,) + others)[0]


def reduce_tokens(terms):
    return lax.psum_scatter(terms, "tensor", scatter_dimension=0)


def per_device(
    image_in,
    text_in,
    condition,
    mod_weight,
    qkv_weight,
    proj_weight,
    up_weight,
    down_weight,
    mod_bias,
    qkv_bias,
    proj_bias,
    up_bias,
    down_bias,
    image_cot,
    text_cot,
):
    ranks = lax.axis_size("tensor")
    column = lax.axis_index("tensor")
    sequences, image_rows, model_width = image_in.shape
    text_rows = text_in.shape[1]
    local_width = model_width // ranks
    local_inner = up_weight.shape[2]
    depth_rows = up_weight.shape[1]
    start_col = column * local_width
    start_inner = column * local_inner

    size = lax.axis_size("dp")

    rows = image_rows + text_rows
    tokens = (ranks, sequences, rows, model_width)

    raw = jnp.concatenate([image_in, text_in], axis=1)
    raw_full = lax.all_gather(raw, "tensor", axis=0)
    cotangent = jnp.concatenate([image_cot, text_cot], axis=1)

    cond_float = condition.astype(F32)
    silu_cond = jax.nn.silu(cond_float).astype(BF).astype(F32)
    silu_parts = silu_cond.reshape(sequences, size, depth_rows).transpose(1, 0, 2)
    mod_flat = mod_weight.reshape(2, depth_rows, 6 * local_width)
    mod_bias_cols = lax.dynamic_slice_in_dim(mod_bias, start_col, local_width, 2).astype(F32)
    mod_parts, silu_all, proj_ranks = modulation_of(
        silu_parts,
        mod_flat,
        mod_bias_cols.reshape(1, 12 * local_width),
        proj_weight.transpose(0, 2, 1),
        ranks,
        0,
    )
    modulation = (
        mod_parts.reshape(ranks, sequences, 2, 6, local_width)
        .transpose(1, 2, 3, 0, 4)
        .reshape(sequences, 2, 6, model_width)
    )

    qkv_bias_cols = (
        lax.dynamic_slice_in_dim(qkv_bias, start_col, local_width, 2)
        .astype(F32)
        .transpose(1, 0, 2)[:, :, None, :]
    )
    up_bias_cols = lax.dynamic_slice_in_dim(up_bias, start_inner, local_inner, 1).astype(F32)[
        :, None, :
    ]
    proj_bias_rows = proj_bias.astype(F32)[:, None, :]
    down_bias_rows = down_bias.astype(F32)[:, None, :]

    grad_mlp, down_bias_sums = row_pass(
        "grad_mlp", work_grad_mlp, (cotangent,), modulation, (), image_rows, ((BF, False),), 1
    )

    qkv_full, proj_full = gather_rows((qkv_weight.transpose(2, 0, 1, 3), proj_ranks), size, 1)
    raw_full, qkv_full, grad_mlp = lax.optimization_barrier((raw_full, qkv_full, grad_mlp))
    joined = (ranks * sequences, rows, model_width)
    first_full, first_normed = row_pass(
        "modulate_all",
        work_first,
        (raw_full.reshape(joined),),
        modulation,
        (),
        image_rows,
        ((BF, False), (BF, False)),
        0,
    )

    qkv = project_in(first_full, qkv_full, qkv_bias_cols, image_rows)

    grad_mlp_full = [lax.all_gather(after(grad_mlp[0], raw_full), "tensor", axis=0)]

    attended, log_totals = attention(qkv, ranks)
    split = (ranks, sequences, rows, local_width)
    attended_mine = lax.all_to_all(attended.reshape(split), "tensor", 0, 0)
    proj_out = project_out(attended_mine, proj_full, image_rows, F32)
    (second_low,) = row_pass(
        "modulate_second",
        work_second,
        (proj_out, raw),
        modulation,
        (proj_bias_rows,),
        image_rows,
        ((BF, False),),
        0,
    )
    second_full = lax.all_gather(after(second_low, grad_mlp_full[0]), "tensor", axis=0)
    up_shards = (up_weight, down_weight.transpose(0, 2, 1))
    up_shards = lax.optimization_barrier(up_shards + (second_low,))[:2]
    up_full, down_full = gather_rows(up_shards, size, 5)
    for sequence in range(1, sequences):
        late = after(grad_mlp[sequence], second_full, up_full)
        grad_mlp_full.append(lax.all_gather(late, "tensor", axis=0))

    activated, slope = mlp_in(second_full.reshape(joined), up_full, up_bias_cols, image_rows)
    wide_split = (ranks, sequences, rows, local_inner)
    slope = slope.reshape(wide_split)
    grad_pre, second_sums = [], []
    down_terms = None
    for sequence in range(sequences):
        incoming = grad_mlp_full[sequence]
        if down_terms is not None:
            incoming = after(incoming, down_terms)
        grad_pre.append(mlp_back(incoming, down_full, slope, sequence, image_rows))
        terms = project_out(grad_pre[-1][None], up_full[None], image_rows)
        second_sums.append(reduce_tokens(terms))
        if down_terms is None:
            down_terms = project_out(after(activated, terms)[None], down_full[None], image_rows)
    activated = activated.reshape((1,) + wide_split)
    down_grad, _ = weight_grad(
        [
            ((after(grad_mlp_full[q], terms), None), sequence_of(activated, q))
            for q in range(sequences)
        ],
        image_rows,
    )
    up_grad, up_bias_term = weight_grad(
        [
            (sequence_of(second_full, q), (after(grad_pre[q], terms)[None], None))
            for q in range(sequences)
        ],
        image_rows,
    )
    (down_total,) = scatter_rows((down_grad,), size, 2, (F32,))
    second_sums = lax.optimization_barrier(tuple(second_sums) + (down_total, up_grad))[:sequences]

    down_terms = after(down_terms, *second_sums).reshape(tokens)
    down_sums = reduce_tokens(down_terms)
    grad_middle, grad_attn, middle_terms = row_pass(
        "middle_back",
        work_middle_back,
        (proj_out, raw, cotangent, second_sums),
        modulation,
        (proj_bias_rows,),
        image_rows,
        ((F32, False), (BF, False)),
        4,
    )
    grad_attended = project_in(grad_attn, proj_full, None, image_rows)
    proj_grad, _ = weight_grad(
        [((after(grad_attn, grad_attended), None), (attended_mine, None))], image_rows
    )
    proj_total, up_total = scatter_rows(
        (proj_grad, after(up_grad, grad_attended)), size, 6, (BF, F32)
    )
    grad_attended = lax.all_to_all(grad_attended, "tensor", 0, 0).reshape(attended.shape)
    grad_attended = after(grad_attended, proj_total)
    proj_total = lax.all_to_all(by_group(proj_total, ranks), "tensor", 0, 0)
    grad_qkv = attention_back(qkv, log_totals, attended, grad_attended, ranks)
    grad_qkv, proj_total = lax.optimization_barrier((grad_qkv, proj_total))
    first_terms = project_out(grad_qkv, qkv_full, image_rows).reshape(tokens)
    down_sums = after(down_sums, grad_qkv)
    first_sums = reduce_tokens(after(first_terms, down_sums))
    proj_total = jnp.sum(after(proj_total, first_terms).astype(F32), axis=0)
    qkv_grad, qkv_bias_term = weight_grad(
        [((first_full, None), (after(grad_qkv, first_terms), None))], image_rows
    )
    image_out, text_out, out_terms = row_pass(
        "outputs",
        work_out,
        (proj_out, raw, cotangent, down_sums),
        modulation,
        (proj_bias_rows, down_bias_rows),
        image_rows,
        ((BF, True),),
        4,
    )
    (qkv_total,) = scatter_rows((qkv_grad,), size, 3, (F32,))
    qkv_total = by_group(qkv_total, 3)

    (first_shares,) = row_pass(
        "first_sums",
        work_first_sums,
        (first_normed, first_terms.reshape(joined)),
        modulation,
        (),
        image_rows,
        (),
        2,
    )
    first_shares = jnp.sum(first_shares.reshape((ranks, sequences, 2, 2, model_width)), axis=0)
    grad_mod = jnp.concatenate(
        [
            first_shares,
            middle_terms[:, :, 2:3],
            middle_terms[:, :, :2],
            out_terms[:, :, :1],
        ],
        axis=2,
    )
    stat_local = jnp.sum(out_terms[:, :, 1:], axis=3)
    grad_mod_parts = (
        grad_mod.reshape(sequences, 12, ranks, local_width)
        .transpose(2, 0, 1, 3)
        .reshape(ranks, sequences, 12 * local_width)
    )
    line = jnp.concatenate(
        [
            qkv_bias_term.ravel(),
            up_bias_term.ravel(),
            jnp.sum(middle_terms[:, :, 3], axis=0).ravel(),
            jnp.sum(down_bias_sums[:, :, 0], axis=0).ravel(),
        ]
    )[None]
    stat_line = jnp.pad(stat_local.reshape(1, -1), ((0, 0), (0, 128 - stat_local.size)))
    mod_total, cond_parts, columns = last_sums(
        grad_mod_parts, line, stat_line, mod_flat, silu_all, 4
    )
    cond_total = cond_parts.transpose(1, 0, 2).reshape(sequences, model_width)
    unused_silu, silu_pull = jax.vjp(jax.nn.silu, cond_float)
    condition_grad = silu_pull(cond_total)[0]
    columns = columns[:, 0]
    qkv_size, up_size = 6 * local_width, 2 * local_inner
    wide_start = qkv_size + up_size
    mod_start = wide_start + 4 * model_width
    stat_start = mod_start + 12 * local_width
    qkv_bias_grad = columns[:, :qkv_size].reshape(ranks, 3, 2, local_width)
    qkv_bias_grad = qkv_bias_grad.transpose(2, 1, 0, 3).reshape(2, 3, model_width)
    up_bias_grad = columns[:, qkv_size:wide_start].reshape(ranks, 2, local_inner)
    up_bias_grad = up_bias_grad.transpose(1, 0, 2).reshape(2, ranks * local_inner)
    wide_sum = jnp.sum(columns[:, wide_start:mod_start], axis=0).reshape(2, 2, model_width)
    mod_bias_grad = columns[:, mod_start:stat_start].reshape(ranks, 2, 6, local_width)
    mod_bias_grad = mod_bias_grad.transpose(1, 2, 0, 3).reshape(2, 6, model_width)
    stat_totals = jnp.sum(columns[:, stat_start : stat_start + stat_local.size], axis=0)
    stat_totals = stat_totals.reshape(stat_local.shape)

    first_sums = lax.optimization_barrier(
        (first_sums, qkv_total, image_out, mod_total, condition_grad, mod_bias_grad)
    )[0]
    image_grad, text_grad = row_pass(
        "first_back",
        work_first_back,
        (raw, grad_middle, first_sums),
        modulation,
        (),
        image_rows,
        ((F32, True),),
        0,
    )

    row_counts = jnp.array(
        [ranks * image_rows * model_width, ranks * text_rows * model_width], F32
    ).reshape(1, 2, 1)
    rms_stats = jnp.sqrt(stat_totals / row_counts)
    return (
        image_out,
        text_out,
        image_grad,
        text_grad,
        condition_grad,
        mod_total.reshape(mod_weight.shape),
        qkv_total.transpose(1, 2, 0, 3),
        proj_total.transpose(0, 2, 1),
        up_total,
        down_total.transpose(0, 2, 1),
        mod_bias_grad,
        qkv_bias_grad,
        wide_sum[0],
        up_bias_grad,
        wide_sum[1],
        rms_stats,
    )


def solution(mesh):
    tokens = P("dp", "tensor", None)
    return jax.shard_map(
        per_device,
        mesh=mesh,
        in_specs=(
            tokens,
            tokens,
            P("dp", None),
            P(None, "dp", None, "tensor"),
            P(None, "dp", None, "tensor"),
            P(None, "tensor", "dp"),
            P(None, "dp", "tensor"),
            P(None, "tensor", "dp"),
            P(),
            P(),
            P(),
            P(),
            P(),
            tokens,
            tokens,
        ),
        out_specs=(
            tokens,
            tokens,
            tokens,
            tokens,
            P("dp", None),
            P(None, "dp", None, "tensor"),
            P(None, "dp", None, "tensor"),
            P(None, "tensor", "dp"),
            P(None, "dp", "tensor"),
            P(None, "tensor", "dp"),
            P(),
            P(),
            P(),
            P(),
            P(),
            P("dp", None, None),
        ),
        check_vma=False,
    )
```

```python
import functools

import jax
import jax.numpy as jnp
from jax import lax
from jax.experimental import pallas as pl
from jax.experimental.pallas import tpu as pltpu
from jax.sharding import PartitionSpec as P

HD = 64
EPSILON = 1e-06
LOG2E = 1.4426950408889634
SCORE = HD ** (-0.5)
VMEM_LIMIT = 56 * 1024 * 1024
BF = jnp.bfloat16
F32 = jnp.float32


def nn(a, b):
    return lax.dot_general(a, b, (((1,), (0,)), ((), ())), preferred_element_type=F32)


def nt(a, b):
    return lax.dot_general(a, b, (((1,), (1,)), ((), ())), preferred_element_type=F32)


def params():
    return pltpu.CompilerParams(vmem_limit_bytes=VMEM_LIMIT)


def resident(shape):
    zeros = (0,) * len(shape)
    return pl.BlockSpec(shape, lambda *_: zeros, pipeline_mode=pl.Buffered(1))


def tile_of(width, most=512):
    for tile in (512, 384, 256, 128):
        if tile <= most and width % tile == 0:
            return tile
    return width


def chunk_of(blocks, rows):
    count = 1
    while count * rows < 512 and blocks % (2 * count) == 0:
        count *= 2
    return count


def up_kernel(image_rows, product, finish, x_ref, w_ref, extra_refs, out_refs):
    blocks, rows, depth = x_ref.shape
    width = out_refs[0].shape[-1]
    step = chunk_of(blocks, image_rows)

    def image(i, carry):
        part = pl.ds(i * step, step)
        x = x_ref[part, :image_rows, :].reshape(step * image_rows, depth)
        results = finish(0, product(x, w_ref[0]), (part, slice(0, image_rows)), extra_refs)
        for ref, value in zip(out_refs, results):
            ref[part, :image_rows, :] = value.reshape(step, image_rows, width).astype(ref.dtype)
        return carry

    lax.fori_loop(0, blocks // step, image, 0, unroll=blocks // step)
    text_rows = rows - image_rows
    x = x_ref[:, image_rows:, :].reshape(blocks * text_rows, depth)
    results = finish(1, product(x, w_ref[1]), (slice(None), slice(image_rows, rows)), extra_refs)
    for ref, value in zip(out_refs, results):
        ref[:, image_rows:, :] = value.reshape(blocks, text_rows, width).astype(ref.dtype)


def project_in(x, weight, bias, image_rows):
    blocks, rows, depth = x.shape
    groups, width = weight.shape[0], weight.shape[3]
    tile = tile_of(width)

    extras = () if bias is None else (bias,)

    def finish(stream, value, place, extra):
        return (value + extra[0][stream] if extra else value,)

    def body(x_ref, w_ref, *refs):
        up_kernel(image_rows, nn, finish, x_ref, w_ref, refs[:-1], refs[-1:])

    return pl.pallas_call(
        body,
        grid=(groups, width // tile),
        in_specs=[
            resident((blocks, rows, depth)),
            pl.BlockSpec((None, 2, depth, tile), lambda g, n: (g, 0, 0, n)),
        ]
        + [pl.BlockSpec((None, 2, 1, tile), lambda g, n: (g, 0, 0, n)) for _ in extras],
        out_specs=pl.BlockSpec((None, blocks, rows, tile), lambda g, n: (g, 0, 0, n)),
        out_shape=jax.ShapeDtypeStruct((groups, blocks, rows, width), BF),
        compiler_params=params(),
        name="project_in",
    )(x, weight, *extras)


def mlp_in(x, weight, bias, image_rows):
    blocks, rows, depth = x.shape
    width = weight.shape[2]
    tile = tile_of(width)
    root = 0.7978845608028654

    def finish(stream, value, place, extra):
        v = value + extra[0][stream]
        square = v * v
        t = jnp.tanh(v * (root + (root * 0.044715) * square))
        half = 0.5 + 0.5 * t
        slope = half + v * (0.5 - 0.5 * t * t) * (root + (root * 3.0 * 0.044715) * square)
        return (v * half, slope)

    def body(x_ref, w_ref, b_ref, a_ref, s_ref):
        up_kernel(image_rows, nn, finish, x_ref, w_ref, (b_ref,), (a_ref, s_ref))

    spec = pl.BlockSpec((blocks, rows, tile), lambda n: (0, 0, n))
    shape = jax.ShapeDtypeStruct((blocks, rows, width), BF)
    return pl.pallas_call(
        body,
        grid=(width // tile,),
        in_specs=[
            resident((blocks, rows, depth)),
            pl.BlockSpec((2, depth, tile), lambda n: (0, 0, n)),
            pl.BlockSpec((2, 1, tile), lambda n: (0, 0, n)),
        ],
        out_specs=[spec, spec],
        out_shape=[shape, shape],
        compiler_params=params(),
        name="mlp_in",
    )(x, weight, bias)


def mlp_back(x, weight, slope, sequence, image_rows):
    blocks, rows, depth = x.shape
    width = weight.shape[2]
    tile = tile_of(width)

    def finish(stream, value, place, extra):
        factor = extra[0][place[0], place[1], :].astype(F32)
        return (value * factor.reshape(value.shape),)

    def body(x_ref, w_ref, s_ref, o_ref):
        up_kernel(image_rows, nn, finish, x_ref, w_ref, (s_ref,), (o_ref,))

    return pl.pallas_call(
        body,
        grid=(width // tile,),
        in_specs=[
            resident((blocks, rows, depth)),
            pl.BlockSpec((2, depth, tile), lambda n: (0, 0, n)),
            pl.BlockSpec((blocks, None, rows, tile), lambda n: (0, sequence, 0, n)),
        ],
        out_specs=pl.BlockSpec((blocks, rows, tile), lambda n: (0, 0, n)),
        out_shape=jax.ShapeDtypeStruct((blocks, rows, width), BF),
        compiler_params=params(),
        name="mlp_back",
    )(x, weight, slope)


def project_out(y, weight, image_rows, dtype=BF):
    groups, blocks, rows, width = y.shape
    depth = weight.shape[2]
    tile = tile_of(depth)
    together = width % 128 == 0

    def product(y_rows, w_rows):
        if together:
            return nt(*[jnp.concatenate(v, axis=1) if groups > 1 else v[0] for v in (y_rows, w_rows)])
        total = nt(y_rows[0], w_rows[0])
        for g in range(1, groups):
            total = total + nt(y_rows[g], w_rows[g])
        return total

    def body(y_ref, w_ref, o_ref):
        step = chunk_of(blocks, image_rows)

        def image(i, carry):
            part = pl.ds(i * step, step)
            y_rows = [
                y_ref[g, part, :image_rows, :].reshape(step * image_rows, width)
                for g in range(groups)
            ]
            total = product(y_rows, [w_ref[g, 0] for g in range(groups)])
            o_ref[part, :image_rows, :] = total.reshape(step, image_rows, tile).astype(dtype)
            return carry

        lax.fori_loop(0, blocks // step, image, 0, unroll=blocks // step)
        text_rows = rows - image_rows
        y_rows = [
            y_ref[g, :, image_rows:, :].reshape(blocks * text_rows, width) for g in range(groups)
        ]
        total = product(y_rows, [w_ref[g, 1] for g in range(groups)])
        o_ref[:, image_rows:, :] = total.reshape(blocks, text_rows, tile).astype(dtype)

    return pl.pallas_call(
        body,
        grid=(depth // tile,),
        in_specs=[
            resident((groups, blocks, rows, width)),
            pl.BlockSpec((groups, 2, tile, width), lambda n: (0, 0, n, 0)),
        ],
        out_specs=pl.BlockSpec((blocks, rows, tile), lambda n: (0, 0, n)),
        out_shape=jax.ShapeDtypeStruct((blocks, rows, depth), dtype),
        compiler_params=params(),
        name="project_out",
    )(y, weight)


def sequence_of(array, sequence):
    return (array, sequence)


def token_spec(entry, lead, tile, place):
    array, sequence = entry
    if sequence is None:
        return pl.BlockSpec(lead + array.shape[-3:-1] + (tile,), lambda *i: place(*i, ()))
    ranks, rows = array.shape[-4], array.shape[-2]
    return pl.BlockSpec(lead + (ranks, None, rows, tile), lambda *i: place(*i, (sequence,)))


def column_pieces(groups, width):
    if width % 128:
        return [[(g, slice(0, width))] for g in range(groups)]
    runs = []
    for low in range(0, groups * width, 512):
        high = min(low + 512, groups * width)
        run = []
        while low < high:
            g, start = divmod(low, width)
            stop = min(width, start + high - low)
            run.append((g, slice(start, stop)))
            low += stop - start
        runs.append(run)
    return runs


def weight_grad(parts, image_rows):
    rows, depth = parts[0][0][0].shape[-2:]
    groups, width = parts[0][1][0].shape[0], parts[0][1][0].shape[-1]
    tile = tile_of(depth, 256)
    count = len(parts)
    streams = ((0, image_rows), (image_rows, rows))
    wide = width % 128 == 0
    out_groups, out_width = (1, groups * width) if wide else (groups, width)

    def body(*refs):
        x_refs, y_refs, (o_ref, s_ref) = refs[:count], refs[count : 2 * count], refs[2 * count :]
        for stream, (low, high) in enumerate(streams):
            turned = []
            for x_ref in x_refs:
                tokens = x_ref.shape[0] * (high - low)
                turned.append(x_ref[:, low:high, :].reshape(tokens, tile).T)
            for run in column_pieces(groups, width):
                total = None
                for x, y_ref in zip(turned, y_refs):
                    pieces = []
                    for g, part in run:
                        y = y_ref[g, :, low:high, part]
                        pieces.append(y.reshape(x.shape[1], part.stop - part.start))
                    y = jnp.concatenate(pieces, axis=1) if len(pieces) > 1 else pieces[0]
                    term = nn(x, y)
                    total = term if total is None else total + term
                g, part = run[0]
                start = g * width + part.start if wide else 0
                place = slice(start, start + total.shape[1])
                o_ref[0 if wide else g, stream, :, place] = total.astype(BF)

        @pl.when(pl.program_id(0) == 0)
        def _():
            for stream, (low, high) in enumerate(streams):
                for g in range(groups):
                    total = jnp.zeros((high - low, width), F32)
                    for y_ref in y_refs:
                        total = lax.fori_loop(
                            0,
                            y_ref.shape[1],
                            lambda i, t, ref=y_ref, g=g: t + ref[g, i, low:high, :].astype(F32),
                            total,
                        )
                    s_ref[g, stream] = jnp.sum(total, axis=0, keepdims=True)

    grad, sums = pl.pallas_call(
        body,
        grid=(depth // tile,),
        in_specs=[token_spec(x, (), tile, lambda k, q: (0,) + q + (0, k)) for x, _ in parts]
        + [
            token_spec(y, (groups,), width, lambda k, q: (0, 0) + q + (0, 0)) for _, y in parts
        ],
        out_specs=[
            pl.BlockSpec((out_groups, 2, tile, out_width), lambda k: (0, 0, k, 0)),
            pl.BlockSpec((groups, 2, 1, width), lambda k: (0, 0, 0, 0)),
        ],
        out_shape=[
            jax.ShapeDtypeStruct((out_groups, 2, depth, out_width), BF),
            jax.ShapeDtypeStruct((groups, 2, 1, width), F32),
        ],
        compiler_params=params(),
        name="weight_grad",
    )(*[x[0] for x, _ in parts], *[y[0] for _, y in parts])
    return grad.reshape((2 * out_groups, depth, out_width)), sums


def parts_of(grad, groups):
    return groups if grad.shape[0] == 2 else 1


def normalize(operand):
    center = operand - jnp.mean(operand, axis=-1, keepdims=True)
    inverse = lax.rsqrt(jnp.mean(center * center, axis=-1, keepdims=True) + EPSILON)
    return (center * inverse, inverse)


def normalize_back(grad_normed, normed, inverse):
    mean_grad = jnp.mean(grad_normed, axis=-1, keepdims=True)
    mean_cross = jnp.mean(grad_normed * normed, axis=-1, keepdims=True)
    return inverse * (grad_normed - mean_grad - normed * mean_cross)


def row_pass(name, work, inputs, mods, biases, image_rows, outs, sums):
    count, rows, depth = inputs[0].shape
    sequences = mods.shape[0]
    step = 16
    streams = ((0, image_rows), (image_rows, rows))
    apart_inputs = any(isinstance(entry, tuple) for entry in inputs)

    def body(*refs):
        refs = list(refs)
        in_refs = []
        for entry in inputs:
            many = len(entry) if isinstance(entry, tuple) else 1
            in_refs.append([refs.pop(0) for _ in range(many)])
        m_ref = refs.pop(0)
        bias_refs = [refs.pop(0) for _ in biases]
        out_refs = []
        for dtype, apart in outs:
            pair = [refs.pop(0), refs.pop(0)] if apart else [refs.pop(0)] * 2
            out_refs.append((dtype, apart, pair))
        if sums:
            s_ref, acc = refs
            acc[...] = jnp.zeros_like(acc)

        def run(row_refs):
            for stream, (low, high) in enumerate(streams):
                steps = (high - low) // step

                def some(i, carry, stream=stream, low=low):
                    start = pl.multiple_of(i * step, step)
                    part = pl.ds(low + start, step)
                    values = [ref[part, :].astype(F32) for ref in row_refs]
                    results, terms = work(
                        stream,
                        values,
                        lambda k: m_ref[stream, k : k + 1, :],
                        [ref[stream] for ref in bias_refs],
                    )
                    for (dtype, apart, pair), value in zip(out_refs, results):
                        place = pl.ds(start, step) if apart else part
                        pair[stream][place, :] = value.astype(dtype)
                    for k, term in enumerate(terms):
                        acc[stream, k] += term[:8] + term[8:]
                    return carry

                lax.fori_loop(0, steps, some, 0, unroll=min(8, steps))

        if apart_inputs:
            for n in range(count):
                pl.when(pl.program_id(0) == n)(
                    functools.partial(run, [r[n] if len(r) > 1 else r[0] for r in in_refs])
                )
        else:
            run([r[0] for r in in_refs])
        if sums:
            for stream in range(2):
                for k in range(sums):
                    s_ref[stream, k : k + 1, :] = jnp.sum(acc[stream, k], axis=0, keepdims=True)

    def rows_spec(size):
        return pl.BlockSpec((None, size, depth), lambda n: (n, 0, 0))

    in_specs, operands = [], []
    for entry in inputs:
        if isinstance(entry, tuple):
            in_specs += [pl.BlockSpec((rows, depth), lambda n: (0, 0)) for _ in entry]
            operands += list(entry)
        else:
            in_specs.append(rows_spec(rows))
            operands.append(entry)
    out_specs, out_shapes = [], []
    for dtype, apart in outs:
        for size in (image_rows, rows - image_rows) if apart else (rows,):
            out_specs.append(rows_spec(size))
            out_shapes.append(jax.ShapeDtypeStruct((count, size, depth), dtype))
    scratch = []
    if sums:
        out_specs.append(pl.BlockSpec((None, 2, sums, depth), lambda n: (n, 0, 0, 0)))
        out_shapes.append(jax.ShapeDtypeStruct((count, 2, sums, depth), F32))
        scratch.append(pltpu.VMEM((2, sums, 8, depth), F32))
    return pl.pallas_call(
        body,
        grid=(count,),
        in_specs=in_specs
        + [pl.BlockSpec((None,) + mods.shape[1:], lambda n: (lax.rem(n, sequences), 0, 0, 0))]
        + [pl.BlockSpec((2, 1, depth), lambda n: (0, 0, 0)) for _ in biases],
        out_specs=out_specs,
        out_shape=out_shapes,
        scratch_shapes=scratch,
        compiler_params=params(),
        name=name,
    )(*operands, mods, *biases)


def work_first(stream, values, mod, biases):
    normed, _ = normalize(values[0])
    return (normed * (1.0 + mod(1)) + mod(0), normed), ()


def work_grad_mlp(stream, values, mod, biases):
    lowered = (mod(5) * values[0]).astype(BF)
    return (lowered,), (lowered.astype(F32),)


def middle_of(values, mod, biases):
    attn_branch = values[0] + biases[0]
    return attn_branch, values[1] + mod(2) * attn_branch


def work_second(stream, values, mod, biases):
    _, middle = middle_of(values, mod, biases)
    normed, _ = normalize(middle)
    return (normed * (1.0 + mod(4)) + mod(3),), ()


def work_middle_back(stream, values, mod, biases):
    attn_branch, middle = middle_of(values, mod, biases)
    cotangent, incoming = values[2], values[3]
    normed, inverse = normalize(middle)
    scaled = incoming * (1.0 + mod(4))
    grad_middle = cotangent + normalize_back(scaled, normed, inverse)
    lowered = (mod(2) * grad_middle).astype(BF)
    terms = (incoming, incoming * normed, grad_middle * attn_branch, lowered.astype(F32))
    return (grad_middle, lowered), terms


def work_out(stream, values, mod, biases):
    attn_branch, middle = middle_of(values, mod, biases)
    residual, cotangent = values[1], values[2]
    mlp_branch = values[3] + biases[1]
    gated_attn = mod(2) * attn_branch
    gated_mlp = mod(5) * mlp_branch
    terms = (
        cotangent * mlp_branch,
        residual * residual,
        gated_attn * gated_attn,
        gated_mlp * gated_mlp,
    )
    return (middle + gated_mlp,), terms


def work_first_back(stream, values, mod, biases):
    residual, grad_middle, incoming = values
    normed, inverse = normalize(residual)
    scaled = incoming * (1.0 + mod(1))
    return (grad_middle + normalize_back(scaled, normed, inverse),), ()


def work_first_sums(stream, values, mod, biases):
    return (), (values[1], values[1] * values[0])


def head_block(width):
    return 128 if width % 128 == 0 else width


def query_parts(length):
    tile = next((t for t in (384, 256, 128) if length % t == 0), length)
    return [slice(low, low + tile) for low in range(0, length, tile)]


def attention(qkv, ranks):
    _, blocks, rows, width = qkv.shape
    sequences = blocks // ranks
    length = ranks * rows
    block = head_block(width)
    heads = block // HD
    parts = query_parts(length)
    view = qkv.reshape(3, ranks, sequences, rows, width)

    def body(q_ref, k_ref, v_ref, o_ref, m_ref):
        turned = []
        for h in range(heads):
            lanes = slice(h * HD, (h + 1) * HD)
            queries = q_ref[:, :, lanes].reshape(length, HD)
            keys = k_ref[:, :, lanes].reshape(length, HD)
            values = v_ref[:, :, lanes].reshape(length, HD).T
            pieces = []
            for part in parts:
                scores = nt(keys, queries[part])
                highest = jnp.max(scores, axis=0, keepdims=True)
                shifted = jnp.exp2((scores - highest) * (SCORE * LOG2E))
                total = jnp.sum(shifted, axis=0, keepdims=True)
                pieces.append(nn(values, shifted.astype(BF)) / total)
                m_ref[h : h + 1, part] = highest * (SCORE * LOG2E) + jnp.log2(total)
            turned.append(jnp.concatenate(pieces, axis=1))
        result = jnp.concatenate(turned, axis=0).T
        o_ref[...] = result.astype(BF).reshape(ranks, rows, block)

    def pick(j):
        return pl.BlockSpec((None, ranks, None, rows, block), lambda s, p: (j, 0, s, 0, p))

    attended, totals = pl.pallas_call(
        body,
        grid=(sequences, width // block),
        in_specs=[pick(0), pick(1), pick(2)],
        out_specs=[
            pl.BlockSpec((ranks, None, rows, block), lambda s, p: (0, s, 0, p)),
            pl.BlockSpec((None, None, heads, length), lambda s, p: (s, p, 0, 0)),
        ],
        out_shape=[
            jax.ShapeDtypeStruct((ranks, sequences, rows, width), BF),
            jax.ShapeDtypeStruct((sequences, width // block, heads, length), F32),
        ],
        compiler_params=params(),
        name="attention",
    )(view, view, view)
    return attended.reshape(blocks, rows, width), totals


def attention_back(qkv, totals, attended, grad, ranks):
    _, blocks, rows, width = qkv.shape
    sequences = blocks // ranks
    length = ranks * rows
    block = head_block(width)
    heads = block // HD
    parts = query_parts(length)
    view = qkv.reshape(3, ranks, sequences, rows, width)
    split = (ranks, sequences, rows, width)

    def body(q_ref, k_ref, v_ref, m_ref, a_ref, g_ref, o_ref):
        for h in range(heads):
            lanes = slice(h * HD, (h + 1) * HD)
            queries = q_ref[:, :, lanes].reshape(length, HD)
            keys = k_ref[:, :, lanes].reshape(length, HD)
            values = v_ref[:, :, lanes].reshape(length, HD)
            grads = g_ref[:, :, lanes].reshape(length, HD)
            attended_rows = a_ref[:, :, lanes].reshape(length, HD)
            cross = grads.astype(F32) * attended_rows.astype(F32)
            delta = jnp.sum(cross.T, axis=0, keepdims=True)
            keys_turned = keys.T
            grad_keys = jnp.zeros((length, HD), F32)
            grad_values = jnp.zeros((length, HD), F32)
            pieces = []
            for part in parts:
                scores = nt(keys, queries[part])
                probs = jnp.exp2(scores * (SCORE * LOG2E) - m_ref[h : h + 1, part])
                grad_probs = nt(values, grads[part])
                grad_scores = (probs * (grad_probs - delta[:, part])).astype(BF)
                grad_values = grad_values + nn(probs.astype(BF), grads[part])
                grad_keys = grad_keys + nn(grad_scores, queries[part])
                pieces.append(nn(keys_turned, grad_scores))
            grad_queries = jnp.concatenate(pieces, axis=1).T
            for j, value in enumerate((grad_queries * SCORE, grad_keys * SCORE, grad_values)):
                o_ref[j, :, :, lanes] = value.astype(BF).reshape(ranks, rows, HD)

    def pick(j):
        return pl.BlockSpec((None, ranks, None, rows, block), lambda s, p: (j, 0, s, 0, p))

    plain = pl.BlockSpec((ranks, None, rows, block), lambda s, p: (0, s, 0, p))
    out = pl.pallas_call(
        body,
        grid=(sequences, width // block),
        in_specs=[
            pick(0),
            pick(1),
            pick(2),
            pl.BlockSpec((None, None, heads, length), lambda s, p: (s, p, 0, 0)),
            plain,
            plain,
        ],
        out_specs=pl.BlockSpec((3, ranks, None, rows, block), lambda s, p: (0, 0, s, 0, p)),
        out_shape=jax.ShapeDtypeStruct((3, ranks, sequences, rows, width), BF),
        compiler_params=params(),
        name="attention_back",
    )(view, view, view, totals, attended.reshape(split), grad.reshape(split))
    return out.reshape(3, blocks, rows, width)


MESH = pl.DeviceIdType.MESH


def comm_params(collective_id):
    return pltpu.CompilerParams(
        vmem_limit_bytes=VMEM_LIMIT, collective_id=collective_id, has_side_effects=True
    )


def in_memory(shapes):
    return [pl.BlockSpec(memory_space=pltpu.VMEM) for _ in shapes]


def meet(peers):
    barrier = pltpu.get_barrier_semaphore()
    for peer in peers:
        pl.semaphore_signal(barrier, inc=1, device_id=peer, device_id_type=MESH)
    pl.semaphore_wait(barrier, len(peers))


def bit_steps(place, bits):
    core = lax.rem(place, 2)

    def flip(bit):
        return bit * (1 - 2 * lax.rem(lax.div(place, bit), 2))

    outer = bits - 1
    deltas = []
    for j in range(outer):
        low, high = flip(1 << (1 + j)), flip(1 << (outer - j))
        deltas.append(low + core * (high - low))
    return core, deltas, 1 - 2 * core


def gather_rows(arrays, size, collective_id):
    count = len(arrays)
    bits = size.bit_length() - 1
    outer = bits - 1

    def body(*refs):
        sources, targets = refs[:count], refs[count : 2 * count]
        send_sems, recv_sems, local_sems = refs[2 * count :]
        place = lax.axis_index("dp")
        core, deltas, core_delta = bit_steps(place, bits)
        steps = deltas + [core_delta]
        meet([{"dp": place + delta} for delta in steps])

        def piece(a, mask):
            index = place
            for j in range(outer):
                if mask >> j & 1:
                    index = index + deltas[j]
            rows = sources[a].shape[-2]
            lead = (slice(None),) * (len(sources[a].shape) - 2)
            start = pl.multiple_of(index * rows, rows)
            return targets[a].at[lead + (pl.ds(start, rows), slice(None))]

        def hop(a, mask, j):
            target = piece(a, mask)
            source = sources[a] if mask == 0 else target
            arrival = mask + (1 << j)
            return pltpu.make_async_remote_copy(
                src_ref=source,
                dst_ref=target,
                send_sem=send_sems.at[a, arrival],
                recv_sem=recv_sems.at[a, arrival],
                device_id={"dp": place + steps[j]},
                device_id_type=MESH,
            )

        hops = {}

        def start(a, mask, j):
            hops[a, mask + (1 << j)] = hop(a, mask, j)
            hops[a, mask + (1 << j)].start()

        locals_ = [
            pltpu.make_async_copy(sources[a], piece(a, 0), local_sems.at[a]) for a in range(count)
        ]
        for a in range(count):
            for j in range(bits):
                start(a, 0, j)
            locals_[a].start()
        for mask in range(1, 1 << outer):
            for a in range(count):
                hops[a, mask].wait_recv()
                for j in range(mask.bit_length(), bits):
                    start(a, mask, j)
        for a in range(count):
            locals_[a].wait()
            for mask in range(1, 1 << bits):
                if mask >> outer:
                    hops[a, mask].wait_recv()
                hops[a, mask].wait_send()

    shapes = [
        jax.ShapeDtypeStruct(a.shape[:-2] + (size * a.shape[-2], a.shape[-1]), a.dtype)
        for a in arrays
    ]
    return pl.pallas_call(
        body,
        in_specs=[pl.BlockSpec(memory_space=pl.ANY)] * count,
        out_specs=[pl.BlockSpec(memory_space=pl.ANY)] * count,
        out_shape=shapes,
        scratch_shapes=[
            pltpu.SemaphoreType.DMA((count, size)),
            pltpu.SemaphoreType.DMA((count, size)),
            pltpu.SemaphoreType.DMA((count,)),
        ],
        compiler_params=comm_params(collective_id),
        name="gather_rows",
    )(*arrays)


def scatter_plan(arrays, size, dtypes, splits):
    count = len(arrays)
    bits = size.bit_length() - 1
    outer = bits - 1
    half = size // 2
    ranged = [a if isinstance(a, tuple) else (a, range(a.shape[0])) for a in arrays]
    origins = [span[0] for _, span in ranged]
    dims = [(len(span), a.shape[1] // size, a.shape[2]) for a, span in ranged]
    views = [a.reshape(a.shape[0], half, 2, r, f) for (a, _), (_, r, f) in zip(ranged, dims)]
    chunks = [(a, g) for a in range(count) for g in range(dims[a][0])]

    def stages(sources, targets, rest):
        mine, met = rest[:count], rest[count : 2 * count]
        slots = [rest[(2 + j) * count : (3 + j) * count] for j in range(outer)]
        load_sems, send0, recv0, send_sems, recv_sems = rest[(2 + outer) * count :]
        place = lax.axis_index("dp")
        core, deltas, core_delta = bit_steps(place, bits)
        position = lax.div(place, 2)

        def shard(mask):
            index = position
            for j in range(outer):
                if mask >> j & 1:
                    index = index + lax.div(deltas[j], 2)
            return index

        def mirrored(mask):
            return sum(1 << (outer - 1 - j) for j in range(outer) if mask >> j & 1)

        loads, swaps, hops = {}, {}, {}
        first_needed = sorted(range(half), key=lambda m: (m & -m) or half)

        def start():
            for mask in first_needed:
                for n, (a, g) in enumerate(chunks):
                    theirs = shard(mirrored(mask))
                    swaps[n, mask] = pltpu.make_async_remote_copy(
                        src_ref=sources[a].at[origins[a] + g, theirs, 1 - core],
                        dst_ref=met[a].at[g, theirs],
                        send_sem=send0.at[n, mask],
                        recv_sem=recv0.at[n, mask],
                        device_id={"dp": place + core_delta},
                        device_id_type=MESH,
                    )
                    loads[n, mask] = pltpu.make_async_copy(
                        sources[a].at[origins[a] + g, shard(mask), core],
                        mine[a].at[g, shard(mask)],
                        load_sems.at[n, mask],
                    )
                    swaps[n, mask].start()
                    loads[n, mask].start()

        def total(n, mask, below, target):
            a, g = chunks[n]
            rows = dims[a][1]
            step = 32 if rows % 32 == 0 else 16
            k = shard(mask)

            def add(i, carry):
                part = pl.ds(pl.multiple_of(i * step, step), step)
                value = mine[a][g, k, part, :].astype(F32) + met[a][g, k, part, :].astype(F32)
                for j in range(below):
                    value = value + slots[j][a][g, mask >> (j + 1), part, :].astype(F32)
                target(a, g, k, part, value)
                return carry

            lax.fori_loop(0, rows // step, add, 0)

        def keep(a, g, k, part, value):
            met[a][g, k, part, :] = value.astype(BF)

        def finish(a, g, k, part, value):
            value = value.astype(dtypes[a])
            if splits[a] == 1:
                targets[a][g, part, :] = value
            else:
                width = dims[a][2] // splits[a]
                for p in range(splits[a]):
                    targets[a][p, g, part, :] = value[:, p * width : (p + 1) * width]

        def step(j):
            for n, (a, g) in enumerate(chunks):
                for mask in range(1, 1 << outer):
                    if mask & ((1 << (j + 1)) - 1) != 1 << j:
                        continue
                    swaps[n, mask].wait_recv()
                    loads[n, mask].wait()
                    for i in range(j):
                        hops[n, mask | 1 << i].wait_recv()
                    total(n, mask, j, keep)
                    hops[n, mask] = pltpu.make_async_remote_copy(
                        src_ref=met[a].at[g, shard(mask)],
                        dst_ref=slots[j][a].at[g, mask >> (j + 1)],
                        send_sem=send_sems.at[n, mask],
                        recv_sem=recv_sems.at[n, mask],
                        device_id={"dp": place + deltas[j]},
                        device_id_type=MESH,
                    )
                    hops[n, mask].start()
        def end():
            for n in range(len(chunks)):
                swaps[n, 0].wait_recv()
                loads[n, 0].wait()
                for j in range(outer):
                    hops[n, 1 << j].wait_recv()
                total(n, 0, outer, finish)
            for n in range(len(chunks)):
                for mask in range(half):
                    swaps[n, mask].wait_send()
                for mask in range(1, 1 << outer):
                    hops[n, mask].wait_send()

        return start, [functools.partial(step, j) for j in range(outer)], end

    scratch = []
    for repeat in range(2):
        scratch += [pltpu.VMEM((g, half, r, f), BF) for g, r, f in dims]
    for j in range(outer):
        scratch += [pltpu.VMEM((g, 1 << (outer - 1 - j), r, f), BF) for g, r, f in dims]
    total_chunks = len(chunks)
    shapes = []
    for (g, r, f), dtype, split in zip(dims, dtypes, splits):
        shape = (g, r, f) if split == 1 else (split, g, r, f // split)
        shapes.append(jax.ShapeDtypeStruct(shape, dtype))
    sems = [pltpu.SemaphoreType.DMA((total_chunks, half)) for _ in range(5)]
    return views, stages, shapes, scratch + sems


def scatter_rows(arrays, size, collective_id, dtypes, splits):
    count = len(arrays)
    views, stages, shapes, scratch = scatter_plan(arrays, size, dtypes, splits)

    def body(*refs):
        place = lax.axis_index("dp")
        _, deltas, core_delta = bit_steps(place, size.bit_length() - 1)
        meet([{"dp": place + delta} for delta in deltas + [core_delta]])
        start, steps, end = stages(refs[:count], refs[count : 2 * count], list(refs[2 * count :]))
        start()
        for step in steps:
            step()
        end()

    return pl.pallas_call(
        body,
        in_specs=[pl.BlockSpec(memory_space=pl.ANY)] * count,
        out_specs=in_memory(arrays),
        out_shape=shapes,
        scratch_shapes=scratch,
        compiler_params=comm_params(collective_id),
        name="scatter_rows",
    )(*views)


def peers_of(axis, size):
    place = lax.axis_index(axis)
    return [lax.rem(place + i, size) for i in range(1, size)]


def exchange(axis, size, source, target, send_sems, recv_sems):
    place = lax.axis_index(axis)
    copies = []
    for i, peer in enumerate(peers_of(axis, size)):
        copy = pltpu.make_async_remote_copy(
            src_ref=source(peer),
            dst_ref=target(place),
            send_sem=send_sems.at[i],
            recv_sem=recv_sems.at[i],
            device_id={axis: peer},
            device_id_type=MESH,
        )
        copy.start()
        copies.append(copy)
    return copies


def wait_all(copies):
    for copy in copies:
        copy.wait_recv()
    for copy in copies:
        copy.wait_send()


def modulation_of(silu_parts, weight, bias, proj, ranks, collective_id):
    size, sequences, rows = silu_parts.shape
    width = weight.shape[2]

    def body(s_ref, w_ref, b_ref, p_ref, m_ref, all_ref, proj_ref, tall, terms, got, *sems):
        place, column = lax.axis_index("dp"), lax.axis_index("tensor")
        meet(
            [{"dp": p} for p in peers_of("dp", size)]
            + [{"tensor": p} for p in peers_of("tensor", ranks)]
        )
        copies = exchange(
            "dp", size, lambda p: s_ref.at[p], lambda p: all_ref.at[p], sems[0], sems[1]
        )
        spreads = exchange(
            "tensor", ranks, lambda p: p_ref, lambda p: proj_ref.at[p], sems[6], sems[7]
        )
        all_ref[place] = s_ref[place]
        proj_ref[column] = p_ref[...]
        tall[...] = jnp.zeros_like(tall)
        wait_all(copies)
        for j in range(size):
            tall[j, :sequences, :] = all_ref[j]
        left = tall[...].reshape(size * 8, rows).astype(BF)
        for stream in range(2):
            product = nn(left, w_ref[stream])
            for j in range(size):
                terms[j, :, stream * width : (stream + 1) * width] = product[
                    j * 8 : j * 8 + sequences
                ]
        copies = exchange(
            "dp", size, lambda p: terms.at[p], lambda p: got.at[p], sems[2], sems[3]
        )
        got[place] = terms[place]
        wait_all(copies)
        total = b_ref[...]
        for j in range(size):
            total = total + got[j]
        m_ref[column] = total.astype(BF).astype(F32)
        copies = exchange(
            "tensor",
            ranks,
            lambda p: m_ref.at[column],
            lambda p: m_ref.at[p],
            sems[4],
            sems[5],
        )
        wait_all(copies + spreads)

    dp_sems = pltpu.SemaphoreType.DMA((size,))
    tensor_sems = pltpu.SemaphoreType.DMA((ranks,))
    return pl.pallas_call(
        body,
        in_specs=in_memory(range(4)),
        out_specs=in_memory(range(3)),
        out_shape=[
            jax.ShapeDtypeStruct((ranks, sequences, 2 * width), F32),
            jax.ShapeDtypeStruct(silu_parts.shape, F32),
            jax.ShapeDtypeStruct((ranks,) + proj.shape, BF),
        ],
        scratch_shapes=[
            pltpu.VMEM((size, 8, rows), F32),
            pltpu.VMEM((size, sequences, 2 * width), F32),
            pltpu.VMEM((size, sequences, 2 * width), F32),
            dp_sems,
            dp_sems,
            dp_sems,
            dp_sems,
            tensor_sems,
            tensor_sems,
            tensor_sems,
            tensor_sems,
        ],
        compiler_params=comm_params(collective_id),
        name="modulation_of",
    )(silu_parts, weight, bias, proj)


def last_sums(arrays, dtypes, splits, grad_mod, line, stats, weight, silu_all, collective_id):
    ranks, sequences, both = grad_mod.shape
    size, _, rows = silu_all.shape
    width = both // 2
    length = line.shape[1]
    count = len(arrays)
    views, stages, shapes, scratch = scatter_plan(arrays, size, dtypes, splits)

    def body(*refs):
        refs = list(refs)

        def take(number):
            taken = refs[:number]
            del refs[:number]
            return taken

        sources = take(count)
        g_ref, line_ref, stat_ref, w_ref, silu_ref = take(5)
        targets = take(count)
        mod_ref, cond_ref, own_ref = take(3)
        scatter_scratch = take(len(scratch))
        got_g, all_g, all_line, tall_g, tall_s, terms, got_terms, summed = take(8)
        sems = refs
        place, column = lax.axis_index("dp"), lax.axis_index("tensor")
        meet(
            [{"dp": p} for p in peers_of("dp", size)]
            + [{"tensor": p} for p in peers_of("tensor", ranks)]
        )
        first = exchange(
            "tensor", ranks, lambda p: g_ref.at[p], lambda p: got_g.at[p], sems[0], sems[1]
        )
        lines = exchange(
            "dp", size, lambda p: line_ref, lambda p: all_line.at[p], sems[2], sems[3]
        )
        start, steps, end = stages(sources, targets, scatter_scratch)
        start()
        got_g[column] = g_ref[column]
        all_line[place] = line_ref[...]
        own_ref[column, :, length + both :] = stat_ref[...]
        tall_g[...] = jnp.zeros_like(tall_g)
        tall_s[...] = jnp.zeros_like(tall_s)
        for j in range(size):
            tall_s[j, :sequences, :] = silu_ref[j]
        turned = tall_s[...].reshape(size * 8, rows).T.astype(BF)
        steps[0]()
        wait_all(first)
        total = got_g[0]
        for t in range(1, ranks):
            total = total + got_g[t]
        all_g[place] = total.astype(BF).astype(F32)
        second = exchange(
            "dp", size, lambda p: all_g.at[place], lambda p: all_g.at[p], sems[4], sems[5]
        )
        wait_all(lines)
        line_total = all_line[0]
        for j in range(1, size):
            line_total = line_total + all_line[j]
        own_ref[column, :, :length] = line_total
        for step in steps[1:]:
            step()
        wait_all(second)
        bias_rows = all_g[0]
        for j in range(1, size):
            bias_rows = bias_rows + all_g[j]
        own_ref[column, :, length : length + both] = jnp.sum(bias_rows, axis=0, keepdims=True)
        third = exchange(
            "tensor",
            ranks,
            lambda p: own_ref.at[column],
            lambda p: own_ref.at[p],
            sems[6],
            sems[7],
        )
        for j in range(size):
            tall_g[j, :sequences, :] = all_g[j]
        grads = tall_g[...].reshape(size * 8, both).astype(BF)
        product = nt(grads[:, :width], w_ref[0]) + nt(grads[:, width:], w_ref[1])
        for j in range(size):
            terms[j] = product[j * 8 : j * 8 + sequences]
        third += exchange(
            "tensor", ranks, lambda p: terms, lambda p: got_terms.at[p], sems[8], sems[9]
        )
        got_terms[column] = terms[...]
        for stream in range(2):
            mod_ref[stream] = nn(turned, grads[:, stream * width : (stream + 1) * width])
        end()
        wait_all(third)
        total = got_terms[0]
        for t in range(1, ranks):
            total = total + got_terms[t]
        summed[...] = total
        cond_ref[place] = summed[place]
        fourth = exchange(
            "dp", size, lambda p: summed.at[p], lambda p: cond_ref.at[p], sems[10], sems[11]
        )
        wait_all(fourth)

    dp_sems = pltpu.SemaphoreType.DMA((size,))
    tensor_sems = pltpu.SemaphoreType.DMA((ranks,))
    return pl.pallas_call(
        body,
        in_specs=[pl.BlockSpec(memory_space=pl.ANY)] * count + in_memory(range(5)),
        out_specs=in_memory(range(count + 3)),
        out_shape=shapes
        + [
            jax.ShapeDtypeStruct((2, rows, width), F32),
            jax.ShapeDtypeStruct((size, sequences, rows), F32),
            jax.ShapeDtypeStruct((ranks, 1, length + both + 128), F32),
        ],
        scratch_shapes=scratch
        + [
            pltpu.VMEM((ranks, sequences, both), F32),
            pltpu.VMEM((size, sequences, both), F32),
            pltpu.VMEM((size, 1, length), F32),
            pltpu.VMEM((size, 8, both), F32),
            pltpu.VMEM((size, 8, rows), F32),
            pltpu.VMEM((size, sequences, rows), F32),
            pltpu.VMEM((ranks, size, sequences, rows), F32),
            pltpu.VMEM((size, sequences, rows), F32),
        ]
        + [tensor_sems] * 2
        + [dp_sems] * 4
        + [tensor_sems] * 4
        + [dp_sems] * 2,
        compiler_params=comm_params(collective_id),
        name="last_sums",
    )(*views, grad_mod, line, stats, weight, silu_all)


def after(value, *others):
    return lax.optimization_barrier((value,) + others)[0]


def reduce_tokens(terms):
    return lax.psum_scatter(terms, "tensor", scatter_dimension=0)


def per_device(
    image_in,
    text_in,
    condition,
    mod_weight,
    qkv_weight,
    proj_weight,
    up_weight,
    down_weight,
    mod_bias,
    qkv_bias,
    proj_bias,
    up_bias,
    down_bias,
    image_cot,
    text_cot,
):
    ranks = lax.axis_size("tensor")
    column = lax.axis_index("tensor")
    sequences, image_rows, model_width = image_in.shape
    text_rows = text_in.shape[1]
    local_width = model_width // ranks
    local_inner = up_weight.shape[2]
    depth_rows = up_weight.shape[1]
    start_col = column * local_width
    start_inner = column * local_inner

    size = lax.axis_size("dp")

    rows = image_rows + text_rows
    tokens = (ranks, sequences, rows, model_width)

    raw = jnp.concatenate([image_in, text_in], axis=1)
    raw_full = lax.all_gather(raw, "tensor", axis=0)
    cotangent = jnp.concatenate([image_cot, text_cot], axis=1)

    cond_float = condition.astype(F32)
    silu_cond = jax.nn.silu(cond_float).astype(BF).astype(F32)
    silu_parts = silu_cond.reshape(sequences, size, depth_rows).transpose(1, 0, 2)
    mod_flat = mod_weight.reshape(2, depth_rows, 6 * local_width)
    mod_bias_cols = lax.dynamic_slice_in_dim(mod_bias, start_col, local_width, 2).astype(F32)
    mod_parts, silu_all, proj_ranks = modulation_of(
        silu_parts,
        mod_flat,
        mod_bias_cols.reshape(1, 12 * local_width),
        proj_weight.transpose(0, 2, 1),
        ranks,
        0,
    )
    modulation = (
        mod_parts.reshape(ranks, sequences, 2, 6, local_width)
        .transpose(1, 2, 3, 0, 4)
        .reshape(sequences, 2, 6, model_width)
    )

    qkv_bias_cols = (
        lax.dynamic_slice_in_dim(qkv_bias, start_col, local_width, 2)
        .astype(F32)
        .transpose(1, 0, 2)[:, :, None, :]
    )
    up_bias_cols = lax.dynamic_slice_in_dim(up_bias, start_inner, local_inner, 1).astype(F32)[
        :, None, :
    ]
    proj_bias_rows = proj_bias.astype(F32)[:, None, :]
    down_bias_rows = down_bias.astype(F32)[:, None, :]

    grad_mlp, down_bias_sums = row_pass(
        "grad_mlp", work_grad_mlp, (cotangent,), modulation, (), image_rows, ((BF, False),), 1
    )

    qkv_full, proj_full = gather_rows((qkv_weight.transpose(2, 0, 1, 3), proj_ranks), size, 1)
    raw_full, qkv_full, grad_mlp = lax.optimization_barrier((raw_full, qkv_full, grad_mlp))
    joined = (ranks * sequences, rows, model_width)
    first_full, first_normed = row_pass(
        "modulate_all",
        work_first,
        (raw_full.reshape(joined),),
        modulation,
        (),
        image_rows,
        ((BF, False), (BF, False)),
        0,
    )

    qkv = project_in(first_full, qkv_full, qkv_bias_cols, image_rows)

    grad_mlp_full = [lax.all_gather(after(grad_mlp[0], raw_full), "tensor", axis=0)]

    attended, log_totals = attention(qkv, ranks)
    split = (ranks, sequences, rows, local_width)
    attended_mine = lax.all_to_all(attended.reshape(split), "tensor", 0, 0)
    proj_out = project_out(attended_mine, proj_full, image_rows, F32)
    (second_low,) = row_pass(
        "modulate_second",
        work_second,
        (proj_out, raw),
        modulation,
        (proj_bias_rows,),
        image_rows,
        ((BF, False),),
        0,
    )
    second_full = lax.all_gather(after(second_low, grad_mlp_full[0]), "tensor", axis=0)
    up_shards = (up_weight, down_weight.transpose(0, 2, 1))
    up_shards = lax.optimization_barrier(up_shards + (second_low,))[:2]
    up_full, down_full = gather_rows(up_shards, size, 5)
    for sequence in range(1, sequences):
        late = after(grad_mlp[sequence], second_full, up_full)
        grad_mlp_full.append(lax.all_gather(late, "tensor", axis=0))

    activated, slope = mlp_in(second_full.reshape(joined), up_full, up_bias_cols, image_rows)
    wide_split = (ranks, sequences, rows, local_inner)
    slope = slope.reshape(wide_split)
    grad_pre, second_sums = [], []
    down_terms = None
    for sequence in range(sequences):
        incoming = grad_mlp_full[sequence]
        if down_terms is not None:
            incoming = after(incoming, down_terms)
        grad_pre.append(mlp_back(incoming, down_full, slope, sequence, image_rows))
        terms = project_out(grad_pre[-1][None], up_full[None], image_rows)
        second_sums.append(reduce_tokens(terms))
        if down_terms is None:
            down_terms = project_out(after(activated, terms)[None], down_full[None], image_rows)
    activated = activated.reshape((1,) + wide_split)
    down_grad, _ = weight_grad(
        [
            ((after(grad_mlp_full[q], terms), None), sequence_of(activated, q))
            for q in range(sequences)
        ],
        image_rows,
    )
    up_grad, up_bias_term = weight_grad(
        [
            (sequence_of(second_full, q), (after(grad_pre[q], terms)[None], None))
            for q in range(sequences)
        ],
        image_rows,
    )
    down_total = scatter_rows(
        ((down_grad, range(1)), (down_grad, range(1, 2))), size, 2, (F32, F32), (1, 1)
    )
    second_sums = lax.optimization_barrier(tuple(second_sums) + (*down_total, up_grad))[:sequences]

    down_terms = after(down_terms, *second_sums).reshape(tokens)
    down_sums = reduce_tokens(down_terms)
    grad_middle, grad_attn, middle_terms = row_pass(
        "middle_back",
        work_middle_back,
        (proj_out, raw, cotangent, second_sums),
        modulation,
        (proj_bias_rows,),
        image_rows,
        ((F32, False), (BF, False)),
        4,
    )
    grad_attended = project_in(grad_attn, proj_full, None, image_rows)
    proj_grad, _ = weight_grad(
        [((after(grad_attn, grad_attended), None), (attended_mine, None))], image_rows
    )
    up_late = after(up_grad, grad_attended)
    proj_total, up_image, up_text = scatter_rows(
        (proj_grad, (up_late, range(1)), (up_late, range(1, 2))),
        size,
        6,
        (BF, F32, F32),
        (parts_of(proj_grad, ranks), 1, 1),
    )
    grad_attended = lax.all_to_all(grad_attended, "tensor", 0, 0).reshape(attended.shape)
    grad_attended = after(grad_attended, proj_total)
    proj_total = proj_total.reshape(ranks, 2, depth_rows, local_width)
    proj_total = lax.all_to_all(proj_total, "tensor", 0, 0)
    grad_qkv = attention_back(qkv, log_totals, attended, grad_attended, ranks)
    first_terms = project_out(grad_qkv, qkv_full, image_rows).reshape(tokens)
    first_terms, proj_total = lax.optimization_barrier((first_terms, proj_total))
    down_sums = after(down_sums, grad_qkv)
    first_sums = reduce_tokens(after(first_terms, down_sums))
    proj_total = jnp.sum(after(proj_total, first_terms).astype(F32), axis=0)
    qkv_grad, qkv_bias_term = weight_grad(
        [((first_full, None), (after(grad_qkv, first_terms), None))], image_rows
    )
    image_out, text_out, out_terms = row_pass(
        "outputs",
        work_out,
        (proj_out, raw, cotangent, down_sums),
        modulation,
        (proj_bias_rows, down_bias_rows),
        image_rows,
        ((BF, True),),
        4,
    )

    (first_shares,) = row_pass(
        "first_sums",
        work_first_sums,
        (first_normed, first_terms.reshape(joined)),
        modulation,
        (),
        image_rows,
        (),
        2,
    )
    first_shares = jnp.sum(first_shares.reshape((ranks, sequences, 2, 2, model_width)), axis=0)
    grad_mod = jnp.concatenate(
        [
            first_shares,
            middle_terms[:, :, 2:3],
            middle_terms[:, :, :2],
            out_terms[:, :, :1],
        ],
        axis=2,
    )
    stat_local = jnp.sum(out_terms[:, :, 1:], axis=3)
    grad_mod_parts = (
        grad_mod.reshape(sequences, 12, ranks, local_width)
        .transpose(2, 0, 1, 3)
        .reshape(ranks, sequences, 12 * local_width)
    )
    line = jnp.concatenate(
        [
            qkv_bias_term.ravel(),
            up_bias_term.ravel(),
            jnp.sum(middle_terms[:, :, 3], axis=0).ravel(),
            jnp.sum(down_bias_sums[:, :, 0], axis=0).ravel(),
        ]
    )[None]
    stat_line = jnp.pad(stat_local.reshape(1, -1), ((0, 0), (0, 128 - stat_local.size)))
    qkv_total, mod_total, cond_parts, columns = last_sums(
        (qkv_grad,),
        (F32,),
        (parts_of(qkv_grad, 3),),
        grad_mod_parts,
        line,
        stat_line,
        mod_flat,
        silu_all,
        4,
    )
    qkv_total = qkv_total.reshape(3, 2, depth_rows, local_width)
    cond_total = cond_parts.transpose(1, 0, 2).reshape(sequences, model_width)
    unused_silu, silu_pull = jax.vjp(jax.nn.silu, cond_float)
    condition_grad = silu_pull(cond_total)[0]
    columns = columns[:, 0]
    qkv_size, up_size = 6 * local_width, 2 * local_inner
    wide_start = qkv_size + up_size
    mod_start = wide_start + 4 * model_width
    stat_start = mod_start + 12 * local_width
    qkv_bias_grad = columns[:, :qkv_size].reshape(ranks, 3, 2, local_width)
    qkv_bias_grad = qkv_bias_grad.transpose(2, 1, 0, 3).reshape(2, 3, model_width)
    up_bias_grad = columns[:, qkv_size:wide_start].reshape(ranks, 2, local_inner)
    up_bias_grad = up_bias_grad.transpose(1, 0, 2).reshape(2, ranks * local_inner)
    wide_sum = jnp.sum(columns[:, wide_start:mod_start], axis=0).reshape(2, 2, model_width)
    mod_bias_grad = columns[:, mod_start:stat_start].reshape(ranks, 2, 6, local_width)
    mod_bias_grad = mod_bias_grad.transpose(1, 2, 0, 3).reshape(2, 6, model_width)
    stat_totals = jnp.sum(columns[:, stat_start : stat_start + stat_local.size], axis=0)
    stat_totals = stat_totals.reshape(stat_local.shape)

    up_total = jnp.concatenate([up_image, up_text], axis=0)
    down_total = jnp.concatenate(down_total, axis=0)
    mod_total = mod_total.reshape(mod_weight.shape)
    qkv_total = qkv_total.transpose(1, 2, 0, 3)
    first_sums = lax.optimization_barrier(
        (
            first_sums,
            up_total,
            down_total,
            qkv_total,
            image_out,
            mod_total,
            condition_grad,
            mod_bias_grad,
        )
    )[0]
    image_grad, text_grad = row_pass(
        "first_back",
        work_first_back,
        (raw, grad_middle, first_sums),
        modulation,
        (),
        image_rows,
        ((F32, True),),
        0,
    )

    row_counts = jnp.array(
        [ranks * image_rows * model_width, ranks * text_rows * model_width], F32
    ).reshape(1, 2, 1)
    rms_stats = jnp.sqrt(stat_totals / row_counts)
    return (
        image_out,
        text_out,
        image_grad,
        text_grad,
        condition_grad,
        mod_total,
        qkv_total,
        proj_total.transpose(0, 2, 1),
        up_total,
        down_total.transpose(0, 2, 1),
        mod_bias_grad,
        qkv_bias_grad,
        wide_sum[0],
        up_bias_grad,
        wide_sum[1],
        rms_stats,
    )


def solution(mesh):
    tokens = P("dp", "tensor", None)
    return jax.shard_map(
        per_device,
        mesh=mesh,
        in_specs=(
            tokens,
            tokens,
            P("dp", None),
            P(None, "dp", None, "tensor"),
            P(None, "dp", None, "tensor"),
            P(None, "tensor", "dp"),
            P(None, "dp", "tensor"),
            P(None, "tensor", "dp"),
            P(),
            P(),
            P(),
            P(),
            P(),
            tokens,
            tokens,
        ),
        out_specs=(
            tokens,
            tokens,
            tokens,
            tokens,
            P("dp", None),
            P(None, "dp", None, "tensor"),
            P(None, "dp", None, "tensor"),
            P(None, "tensor", "dp"),
            P(None, "dp", "tensor"),
            P(None, "tensor", "dp"),
            P(),
            P(),
            P(),
            P(),
            P(),
            P("dp", None, None),
        ),
        check_vma=False,
    )
```
